32 devices in a mesh: owner: 4 (over x, core), fsdp: 8 (over z, y).
Axes of the slice: x: 2, y: 2, z: 4, core: 2. Of those that a mesh axis runs over, the one named last changes fastest.
Arguments:
- gradients: bfloat16 [8, 16384, 512], P(None, ('fsdp', 'owner')), may hold values from -120 to 120
- momentum: float32 [8, 16384, 512], P('owner', 'fsdp'), may hold values from -120 to 120
- slot_table: int32 [8], replicated, may hold values from 0 to 7, each once
Outputs:
- updates: bfloat16 [8, 16384, 512], P(None, ('fsdp', 'owner'))
- new_momentum: float32 [8, 16384, 512], P('owner', 'fsdp')
The draws below stay inside these ranges and needn't reach their ends.
Inputs may be any that keep to these rules, and one draw needn't show every extreme that they name: `slot_table`: each matrix has its own slot.
All inputs are finite; a program needn't handle non-finite values.
Results may differ from the reference program's by a relative error of at most 0.04.
Values may be sent and summed in bfloat16 or wider, within the bound.
No kernel may reach another device: no remote copies, remote signals or barrier semaphores. Data moves between devices by JAX's collectives and lax.ppermute only.
A program may use at most 128 MiB of HBM per device.

```python
import math
import jax
import jax.numpy as jnp
from jax import lax

LONG = 16384
RANK = 512
ITERS = 5
MATS = 8


def scale_field(key, spread):
    key_rows, key_cols = jax.random.split(key)
    row_scale = jnp.exp(jax.random.uniform(key_rows, (MATS, LONG, 1), jnp.float32, -spread, spread))
    col_scale = jnp.exp(jax.random.uniform(key_cols, (MATS, 1, RANK), jnp.float32, -spread, spread))
    position = jnp.arange(LONG, dtype=jnp.float32).reshape(1, LONG, 1) / LONG
    rising = jnp.exp(math.log(3.0) * (position - 0.5))
    return row_scale * col_scale * rising


def draw_gradients(key, part):
    key = jax.random.fold_in(key, 11)
    key_scale, key_noise = jax.random.split(key, 2)
    noise_part = jnp.clip(jax.random.normal(key_noise, (MATS, LONG, RANK), jnp.float32), -4.0, 4.0)
    values_field = scale_field(key_scale, 1.15) * noise_part
    return values_field.astype(jnp.bfloat16)


def draw_momentum(key, part):
    key = jax.random.fold_in(key, 12)
    key_scale, key_noise = jax.random.split(key, 2)
    noise_part = jnp.clip(jax.random.normal(key_noise, (MATS, LONG, RANK), jnp.float32), -4.0, 4.0)
    values_field = scale_field(key_scale, 1.15) * noise_part
    return values_field.astype(jnp.float32)


def setup_inputs(seed: int = 0) -> dict:
    streams_of = jax.random.split(jax.random.key(seed), 4)
    return {
        "gradients": draw_gradients(jax.random.fold_in(streams_of[3], 71), 0),
        "momentum": draw_momentum(jax.random.fold_in(streams_of[3], 71), 0),
        "slot_table": jax.random.permutation(streams_of[2], MATS).astype(jnp.int32),
    }


quintic = (3.4445, -4.775, 2.0315)
momentum_decay = 0.95
epsilon = 1e-07

def orthogonalize(blended):
    norm_value = jnp.sqrt(jnp.sum(blended * blended))
    panels = (blended / (norm_value + epsilon)).astype(jnp.bfloat16)
    for iteration in range(ITERS):
        gram_matrix = jnp.dot(panels.T, panels, preferred_element_type=jnp.float32).astype(jnp.bfloat16)
        squared = jnp.dot(gram_matrix, gram_matrix, preferred_element_type=jnp.float32)
        polynomial = (quintic[1] * gram_matrix.astype(jnp.float32) + quintic[2] * squared).astype(jnp.bfloat16)
        product = jnp.dot(panels, polynomial, preferred_element_type=jnp.float32)
        panels = (quintic[0] * panels.astype(jnp.float32) + product).astype(jnp.bfloat16)
    return panels

def slot_inverse(slot_table, matrix_count):
    slots = jnp.arange(matrix_count, dtype=jnp.int32)
    matches = slot_table[None, :] == slots[:, None]
    return lax.optimization_barrier(jnp.sum(jnp.where(matches, slots[None, :], 0), axis=1)).astype(jnp.int32)

def reference(gradients, momentum, slot_table):
    inverse = slot_inverse(slot_table, MATS)

    def per_slot(slot):
        matrix_index = inverse[slot]
        gradient = lax.dynamic_index_in_dim(gradients, matrix_index, 0, keepdims=False).astype(jnp.float32)
        previous = lax.dynamic_index_in_dim(momentum, slot, 0, keepdims=False)
        renewed = momentum_decay * previous + gradient
        blended = gradient + momentum_decay * renewed
        scaled = (math.sqrt(max(LONG, RANK)) * orthogonalize(blended).astype(jnp.float32)).astype(jnp.bfloat16)
        return (scaled, renewed)
    by_slot, new_momentum = lax.map(per_slot, jnp.arange(MATS, dtype=jnp.int32))
    updates = jnp.take(by_slot, slot_table, axis=0)
    return (updates, new_momentum)
```

```python
import functools
import math

import jax
import jax.numpy as jnp
from jax import lax
from jax.experimental import pallas as pl
from jax.experimental.pallas import tpu as pltpu
from jax.sharding import PartitionSpec as P

LONG = 16384
RANK = 512
ITERS = 5
TILE = 128

quintic = (3.4445, -4.775, 2.0315)
momentum_decay = 0.95
epsilon = 1e-07

BLOCKS = [(i, j) for i in range(RANK // TILE) for j in range(i, RANK // TILE)]
PACKED = len(BLOCKS) * TILE

f32, bf16 = jnp.float32, jnp.bfloat16


def slot_inverse(slot_table, matrix_count):
    slots = jnp.arange(matrix_count, dtype=jnp.int32)
    matches = slot_table[None, :] == slots[:, None]
    return jnp.sum(jnp.where(matches, slots[None, :], 0), axis=1)


def partners(size, step):
    return [(i, i ^ step) for i in range(size)]


def blend_kernel(shares, has_buffer, has_sum, *refs):
    refs = list(refs)
    place = refs.pop(0)
    gradient, momentum = refs.pop(0), refs.pop(0)
    if has_buffer:
        refs.pop(0)
    before = refs.pop(0) if has_sum else None
    renewed, rows, total, held = refs
    step = pl.program_id(0)

    @pl.when(step == 0)
    def _():
        held[...] = before[...] if has_sum else jnp.zeros_like(held)

    g = gradient[...].astype(f32)
    m = momentum_decay * momentum[...] + g
    renewed[...] = m
    x = (g + momentum_decay * m).astype(bf16)
    rows[...] = x
    half = RANK // 2
    dims = (((0,), (0,)), ((), ()))
    upper = lax.dot_general(x[:, :half], x, dims, preferred_element_type=f32)
    lower = lax.dot_general(x[:, half:], x[:, half:], dims, preferred_element_type=f32)
    for n, (i, j) in enumerate(BLOCKS):
        part, i0, j0 = (upper, i, j) if i < half // TILE else (lower, i - half // TILE, j - half // TILE)
        held[n * TILE : (n + 1) * TILE, :] += part[
            i0 * TILE : (i0 + 1) * TILE, j0 * TILE : (j0 + 1) * TILE
        ]

    @pl.when(step == pl.num_programs(0) - 1)
    def _():
        if shares is None:
            total[...] = held[...]
        else:
            near, far = shares
            count = PACKED // (near * far)
            for e1 in range(near):
                for e2 in range(far):
                    who = jnp.bitwise_xor(place[2], e2 * near + e1)
                    start = pl.multiple_of(who * count, 8)
                    total[e1, e2] = held[pl.ds(start, count), :]


def blend(place, gradient, local, momentum, slot, piece_rows, buffer, before, shares):
    tile = min(256, piece_rows)
    steps = piece_rows // tile
    if local:
        gradient_spec = pl.BlockSpec((None, tile, RANK), lambda i, p: (p[1], i, 0))
    else:
        gradient_spec = pl.BlockSpec((tile, RANK), lambda i, p: (i, 0))
    momentum_spec = pl.BlockSpec((None, tile, RANK), lambda i, p: (slot, p[0] * steps + i, 0))
    in_specs, operands = [gradient_spec, momentum_spec], [gradient, momentum]
    aliases = {}
    if buffer is not None:
        aliases = {1 + len(operands): 0}
        in_specs.append(pl.BlockSpec(memory_space=pl.ANY))
        operands.append(buffer)
    if before is not None:
        in_specs.append(pl.BlockSpec((PACKED, TILE), lambda i, p: (0, 0)))
        operands.append(before)
    if shares is None:
        total = (PACKED, TILE)
    else:
        total = (*shares, PACKED // (shares[0] * shares[1]), TILE)
    return pl.pallas_call(
        functools.partial(blend_kernel, shares, buffer is not None, before is not None),
        grid_spec=pltpu.PrefetchScalarGridSpec(
            num_scalar_prefetch=1,
            grid=(steps,),
            in_specs=in_specs,
            out_specs=[
                momentum_spec,
                pl.BlockSpec((tile, RANK), lambda i, p: (i, 0)),
                pl.BlockSpec(total, lambda i, p: (0,) * len(total)),
            ],
            scratch_shapes=[pltpu.VMEM((PACKED, TILE), f32)],
        ),
        out_shape=[
            jax.ShapeDtypeStruct(momentum.shape, f32),
            jax.ShapeDtypeStruct((piece_rows, RANK), bf16),
            jax.ShapeDtypeStruct(total, f32),
        ],
        input_output_aliases=aliases,
        compiler_params=pltpu.CompilerParams(vmem_limit_bytes=24 * 2**20),
        cost_estimate=pl.CostEstimate(
            flops=2 * piece_rows * RANK * RANK, bytes_accessed=piece_rows * RANK * 12, transcendentals=0
        ),
        name="blend",
    )(place, *operands)


def two(x):
    high = x.astype(bf16)
    return high, (x - high.astype(f32)).astype(bf16)


def dot(a, b):
    return jnp.dot(a, b, preferred_element_type=f32)


def product(a, b):
    (ah, al), (bh, bl) = a, b
    return dot(ah, bh) + (dot(ah, bl) + dot(al, bh))


def polynomial_kernel(near, far, count, place, *refs):
    refs = list(refs)
    packed = refs.pop()
    result = refs.pop()
    for e2 in range(far):
        who = jnp.bitwise_xor(place[2], e2 * near)
        packed[pl.ds(pl.multiple_of(who * count, 8), count), :] = refs.pop(0)[...]
    for e1 in range(1, near):
        other = refs.pop(0)
        for e2 in range(far):
            who = jnp.bitwise_xor(place[2], e2 * near + e1)
            packed[pl.ds(pl.multiple_of(who * count, 8), count), :] = other[e2]
    sides = RANK // TILE
    parts = {}
    trace = jnp.zeros((), f32)
    rows_id = lax.broadcasted_iota(jnp.int32, (TILE, TILE), 0)
    cols_id = lax.broadcasted_iota(jnp.int32, (TILE, TILE), 1)
    for n, (i, j) in enumerate(BLOCKS):
        block = packed[n * TILE : (n + 1) * TILE, :]
        parts[i, j] = block
        if i == j:
            trace = trace + jnp.sum(jnp.where(rows_id == cols_id, block, 0.0))
        else:
            parts[j, i] = block.T
    gram = jnp.concatenate(
        [jnp.concatenate([parts[i, j] for j in range(sides)], axis=1) for i in range(sides)], axis=0
    )
    scale = 1.0 / (jnp.sqrt(jnp.full((1, 1), trace, f32)) + epsilon)
    gram = (gram * scale) * scale
    a, b, c = quintic
    r_id = lax.broadcasted_iota(jnp.int32, (RANK, RANK), 0)
    c_id = lax.broadcasted_iota(jnp.int32, (RANK, RANK), 1)
    poly = None
    for iteration in range(ITERS):
        g = two(gram)
        rest = b * gram + c * product(g, g)
        r = two(rest)
        if poly is None:
            poly = rest + jnp.where(r_id == c_id, a, 0.0)
        else:
            poly = a * poly + product(two(poly), r)
        if iteration < ITERS - 1:
            middle = a * gram + product(g, r)
            gram = a * middle + product(two(middle), r)
    high, low = two(poly * (scale * math.sqrt(max(LONG, RANK))))
    result[:RANK, :] = high
    result[RANK:, :] = low


def polynomial(place, shares, own, others):
    near, far = shares
    count = PACKED // (near * far)
    operands = [*own, *others]
    return pl.pallas_call(
        functools.partial(polynomial_kernel, near, far, count),
        grid_spec=pltpu.PrefetchScalarGridSpec(
            num_scalar_prefetch=1,
            grid=(1,),
            in_specs=[pl.BlockSpec(x.shape, lambda i, p, r=x.ndim: (0,) * r) for x in operands],
            out_specs=pl.BlockSpec((2 * RANK, RANK), lambda i, p: (0, 0)),
            scratch_shapes=[pltpu.VMEM((PACKED, TILE), f32)],
        ),
        out_shape=jax.ShapeDtypeStruct((2 * RANK, RANK), bf16),
        compiler_params=pltpu.CompilerParams(vmem_limit_bytes=40 * 2**20),
        cost_estimate=pl.CostEstimate(flops=51 * 2 * RANK**3, bytes_accessed=2 * 2**20, transcendentals=0),
        name="polynomial",
    )(place, *operands)


def apply_kernel(rows, poly, out):
    x = rows[...]
    out[...] = (dot(x, poly[:RANK, :]) + dot(x, poly[RANK:, :])).astype(bf16)


def apply_polynomial(rows, poly):
    return pl.pallas_call(
        apply_kernel,
        out_shape=jax.ShapeDtypeStruct(rows.shape, bf16),
        compiler_params=pltpu.CompilerParams(vmem_limit_bytes=16 * 2**20),
        cost_estimate=pl.CostEstimate(
            flops=4 * rows.shape[0] * RANK * RANK, bytes_accessed=2 * 2**20, transcendentals=0
        ),
        name="apply",
    )(rows, poly)


def on_device(gradients, momentum, slot_table, *, owners, group):
    matrix_count, piece_rows, _ = gradients.shape
    held_slots = momentum.shape[0]
    inverse = slot_inverse(slot_table, matrix_count)
    me_owner, me_group = lax.axis_index("owner"), lax.axis_index("fsdp")
    near = 1 << ((group.bit_length() - 1) // 2)
    shares = (near, group // near)

    def matrix_of(slot, d):
        return inverse[held_slots * jnp.bitwise_xor(me_owner, d) + slot]

    far_steps, near_steps = list(range(2, owners)), list(range(1, min(2, owners)))
    arrived = {}
    for slot in range(held_slots):
        for d in far_steps + near_steps:
            piece = lax.dynamic_index_in_dim(gradients, matrix_of(slot, d), 0, keepdims=False)
            arrived[slot, d] = lax.ppermute(piece, "owner", partners(owners, d))

    order = [(slot, d) for slot in range(held_slots) for d in [0] + near_steps]
    order += [(slot, d) for slot in range(held_slots) for d in far_steps]
    renewed, rows, sums = None, {}, {}
    for slot, d in order:
        place = jnp.stack([jnp.bitwise_xor(me_owner, d), matrix_of(slot, d), me_group]).astype(jnp.int32)
        last = d == owners - 1
        renewed, rows[slot, d], sums[slot] = blend(
            place,
            gradients if d == 0 else arrived[slot, d],
            d == 0,
            momentum,
            slot,
            piece_rows,
            renewed,
            sums.get(slot),
            shares if last else None,
        )

    place = jnp.stack([me_owner, me_owner, me_group]).astype(jnp.int32)
    updates = jnp.zeros(gradients.shape, bf16)
    for slot in range(held_slots):
        share = sums[slot]
        line = share[0]
        for e1 in range(1, shares[0]):
            line = line + lax.ppermute(share[e1], "fsdp", partners(group, e1))
        mine = line[0]
        for e2 in range(1, shares[1]):
            mine = mine + lax.ppermute(line[e2], "fsdp", partners(group, e2 * near))
        own = [mine]
        for e2 in range(1, shares[1]):
            own.append(lax.ppermute(mine, "fsdp", partners(group, e2 * near)))
        stacked = jnp.stack(own)
        others = [lax.ppermute(stacked, "fsdp", partners(group, e1)) for e1 in range(1, shares[0])]
        poly = polynomial(place, shares, own, others)
        for d in far_steps + near_steps + [0]:
            out = apply_polynomial(rows[slot, d], poly)
            if d:
                out = lax.ppermute(out, "owner", partners(owners, d))
            updates = lax.dynamic_update_index_in_dim(updates, out, matrix_of(slot, d), 0)
    return (updates, renewed)


def solution(mesh):
    return jax.shard_map(
        functools.partial(on_device, owners=mesh.shape["owner"], group=mesh.shape["fsdp"]),
        mesh=mesh,
        in_specs=(P(None, ("fsdp", "owner"), None), P("owner", "fsdp", None), P()),
        out_specs=(P(None, ("fsdp", "owner"), None), P("owner", "fsdp", None)),
        check_vma=False,
    )
```

```python
import functools
import math

import jax
import jax.numpy as jnp
from jax import lax
from jax.experimental import pallas as pl
from jax.experimental.pallas import tpu as pltpu
from jax.sharding import PartitionSpec as P

LONG = 16384
RANK = 512
ITERS = 5
TILE = 128

quintic = (3.4445, -4.775, 2.0315)
momentum_decay = 0.95
epsilon = 1e-07

BLOCKS = [(i, j) for i in range(RANK // TILE) for j in range(i, RANK // TILE)]
PACKED = len(BLOCKS) * TILE

f32, bf16 = jnp.float32, jnp.bfloat16


def in_hbm(x):
    return pltpu.with_memory_space_constraint(x, pltpu.HBM)


def matrix_of(place, count, slots, slot, d):
    wanted = slots * jnp.bitwise_xor(place[count], d) + slot
    found = jnp.int32(0)
    for m in range(1, count):
        found = found + jnp.where(place[m] == wanted, m, 0)
    return found


def group_index(place):
    return place[place.shape[0] - 1]


def partners(size, step):
    return [(i, i ^ step) for i in range(size)]


def blend_kernel(shares, has_buffer, has_sum, *refs):
    refs = list(refs)
    place = refs.pop(0)
    gradient, momentum = refs.pop(0), refs.pop(0)
    if has_buffer:
        refs.pop(0)
    before = refs.pop(0) if has_sum else None
    renewed, rows, total, held = refs
    step = pl.program_id(0)

    @pl.when(step == 0)
    def _():
        held[...] = before[...] if has_sum else jnp.zeros_like(held)

    g = gradient[...].astype(f32)
    m = momentum_decay * momentum[...] + g
    renewed[...] = m
    x = (g + momentum_decay * m).astype(bf16)
    rows[...] = x
    half = RANK // 2
    dims = (((0,), (0,)), ((), ()))
    upper = lax.dot_general(x[:, :half], x, dims, preferred_element_type=f32)
    lower = lax.dot_general(x[:, half:], x[:, half:], dims, preferred_element_type=f32)
    for n, (i, j) in enumerate(BLOCKS):
        part, i0, j0 = (upper, i, j) if i < half // TILE else (lower, i - half // TILE, j - half // TILE)
        held[n * TILE : (n + 1) * TILE, :] += part[
            i0 * TILE : (i0 + 1) * TILE, j0 * TILE : (j0 + 1) * TILE
        ]

    @pl.when(step == pl.num_programs(0) - 1)
    def _():
        if shares is None:
            total[...] = held[...]
        else:
            near, far = shares
            count = PACKED // (near * far)
            for e1 in range(near):
                for e2 in range(far):
                    who = jnp.bitwise_xor(group_index(place), e2 * near + e1)
                    start = pl.multiple_of(who * count, 8)
                    total[e1, e2] = held[pl.ds(start, count), :]


def pick_kernel(place, *refs):
    half = len(refs) // 2
    for source, target in zip(refs[:half], refs[half:]):
        target[...] = source[...]


def pick(place, gradients, slots, wanted):
    count, rows, _ = gradients.shape

    def spec(slot, d):
        return pl.BlockSpec(
            (None, rows, RANK), lambda i, p: (matrix_of(p, count, slots, slot, d), 0, 0)
        )

    return pl.pallas_call(
        pick_kernel,
        grid_spec=pltpu.PrefetchScalarGridSpec(
            num_scalar_prefetch=1,
            grid=(1,),
            in_specs=[spec(slot, d) for slot, d in wanted],
            out_specs=[pl.BlockSpec((rows, RANK), lambda i, p: (0, 0)) for _ in wanted],
        ),
        out_shape=[jax.ShapeDtypeStruct((rows, RANK), bf16) for _ in wanted],
        compiler_params=pltpu.CompilerParams(vmem_limit_bytes=16 * 2**20),
        cost_estimate=pl.CostEstimate(
            flops=0, bytes_accessed=4 * len(wanted) * rows * RANK, transcendentals=0
        ),
        name="pick",
    )(place, *[in_hbm(gradients)] * len(wanted))


def drop_kernel(place, piece, *refs):
    refs[-1][...] = piece[...]


def drop(place, piece, shape, slots, slot, d, buffer):
    count, rows, _ = shape
    operands = [piece] + ([] if buffer is None else [in_hbm(buffer)])
    return pl.pallas_call(
        drop_kernel,
        grid_spec=pltpu.PrefetchScalarGridSpec(
            num_scalar_prefetch=1,
            grid=(1,),
            in_specs=[pl.BlockSpec((rows, RANK), lambda i, p: (0, 0))]
            + [pl.BlockSpec(memory_space=pltpu.HBM)] * (len(operands) - 1),
            out_specs=pl.BlockSpec(
                (None, rows, RANK), lambda i, p: (matrix_of(p, count, slots, slot, d), 0, 0)
            ),
        ),
        out_shape=pltpu.HBM(shape, bf16),
        input_output_aliases={} if buffer is None else {2: 0},
        compiler_params=pltpu.CompilerParams(vmem_limit_bytes=16 * 2**20),
        cost_estimate=pl.CostEstimate(flops=0, bytes_accessed=4 * rows * RANK, transcendentals=0),
        name="drop",
    )(place, *operands)


def blend(place, gradient, momentum, slot, d, count, buffer, before, shares):
    slots = momentum.shape[0]
    piece_rows = gradient.shape[-2]
    tile = min(256, piece_rows)
    steps = piece_rows // tile
    if d == 0:
        gradient_spec = pl.BlockSpec(
            (None, tile, RANK), lambda i, p: (matrix_of(p, count, slots, slot, 0), i, 0)
        )
        gradient = in_hbm(gradient)
    else:
        gradient_spec = pl.BlockSpec((tile, RANK), lambda i, p: (i, 0))
    momentum_spec = pl.BlockSpec(
        (None, tile, RANK), lambda i, p: (slot, jnp.bitwise_xor(p[count], d) * steps + i, 0)
    )
    in_specs, operands = [gradient_spec, momentum_spec], [gradient, in_hbm(momentum)]
    aliases = {}
    if buffer is not None:
        aliases = {1 + len(operands): 0}
        in_specs.append(pl.BlockSpec(memory_space=pltpu.HBM))
        operands.append(in_hbm(buffer))
    if before is not None:
        in_specs.append(pl.BlockSpec((PACKED, TILE), lambda i, p: (0, 0)))
        operands.append(before)
    if shares is None:
        total = (PACKED, TILE)
    else:
        total = (*shares, PACKED // (shares[0] * shares[1]), TILE)
    return pl.pallas_call(
        functools.partial(blend_kernel, shares, buffer is not None, before is not None),
        grid_spec=pltpu.PrefetchScalarGridSpec(
            num_scalar_prefetch=1,
            grid=(steps,),
            in_specs=in_specs,
            out_specs=[
                momentum_spec,
                pl.BlockSpec((tile, RANK), lambda i, p: (i, 0)),
                pl.BlockSpec(total, lambda i, p: (0,) * len(total)),
            ],
            scratch_shapes=[pltpu.VMEM((PACKED, TILE), f32)],
        ),
        out_shape=[
            pltpu.HBM(momentum.shape, f32),
            jax.ShapeDtypeStruct((piece_rows, RANK), bf16),
            jax.ShapeDtypeStruct(total, f32),
        ],
        input_output_aliases=aliases,
        compiler_params=pltpu.CompilerParams(vmem_limit_bytes=24 * 2**20),
        cost_estimate=pl.CostEstimate(
            flops=2 * piece_rows * RANK * RANK, bytes_accessed=piece_rows * RANK * 12, transcendentals=0
        ),
        name="blend",
    )(place, *operands)


def two(x):
    high = x.astype(bf16)
    return high, (x - high.astype(f32)).astype(bf16)


def dot(a, b):
    return jnp.dot(a, b, preferred_element_type=f32)


def product(a, b):
    (ah, al), (bh, bl) = a, b
    return dot(ah, bh) + (dot(ah, bl) + dot(al, bh))


def polynomial_kernel(near, far, count, place, *refs):
    refs = list(refs)
    packed = refs.pop()
    result = refs.pop()
    for e2 in range(far):
        who = jnp.bitwise_xor(group_index(place), e2 * near)
        packed[pl.ds(pl.multiple_of(who * count, 8), count), :] = refs.pop(0)[...]
    for e1 in range(1, near):
        other = refs.pop(0)
        for e2 in range(far):
            who = jnp.bitwise_xor(group_index(place), e2 * near + e1)
            packed[pl.ds(pl.multiple_of(who * count, 8), count), :] = other[e2]
    sides = RANK // TILE
    parts = {}
    trace = jnp.zeros((), f32)
    rows_id = lax.broadcasted_iota(jnp.int32, (TILE, TILE), 0)
    cols_id = lax.broadcasted_iota(jnp.int32, (TILE, TILE), 1)
    for n, (i, j) in enumerate(BLOCKS):
        block = packed[n * TILE : (n + 1) * TILE, :]
        parts[i, j] = block
        if i == j:
            trace = trace + jnp.sum(jnp.where(rows_id == cols_id, block, 0.0))
        else:
            parts[j, i] = block.T
    gram = jnp.concatenate(
        [jnp.concatenate([parts[i, j] for j in range(sides)], axis=1) for i in range(sides)], axis=0
    )
    scale = 1.0 / (jnp.sqrt(jnp.full((1, 1), trace, f32)) + epsilon)
    gram = (gram * scale) * scale
    a, b, c = quintic
    r_id = lax.broadcasted_iota(jnp.int32, (RANK, RANK), 0)
    c_id = lax.broadcasted_iota(jnp.int32, (RANK, RANK), 1)
    poly = None
    for iteration in range(ITERS):
        g = two(gram)
        rest = b * gram + c * product(g, g)
        r = two(rest)
        if poly is None:
            poly = rest + jnp.where(r_id == c_id, a, 0.0)
        else:
            poly = a * poly + product(two(poly), r)
        if iteration < ITERS - 1:
            middle = a * gram + product(g, r)
            gram = a * middle + product(two(middle), r)
    high, low = two(poly * (scale * math.sqrt(max(LONG, RANK))))
    result[:RANK, :] = high
    result[RANK:, :] = low


def polynomial(place, shares, own, others):
    near, far = shares
    count = PACKED // (near * far)
    operands = [*own, *others]
    return pl.pallas_call(
        functools.partial(polynomial_kernel, near, far, count),
        grid_spec=pltpu.PrefetchScalarGridSpec(
            num_scalar_prefetch=1,
            grid=(1,),
            in_specs=[pl.BlockSpec(x.shape, lambda i, p, r=x.ndim: (0,) * r) for x in operands],
            out_specs=pl.BlockSpec((2 * RANK, RANK), lambda i, p: (0, 0)),
            scratch_shapes=[pltpu.VMEM((PACKED, TILE), f32)],
        ),
        out_shape=jax.ShapeDtypeStruct((2 * RANK, RANK), bf16),
        compiler_params=pltpu.CompilerParams(vmem_limit_bytes=40 * 2**20),
        cost_estimate=pl.CostEstimate(flops=51 * 2 * RANK**3, bytes_accessed=2 * 2**20, transcendentals=0),
        name="polynomial",
    )(place, *operands)


def apply_kernel(rows, poly, out):
    x = rows[...]
    out[...] = (dot(x, poly[:RANK, :]) + dot(x, poly[RANK:, :])).astype(bf16)


def apply_polynomial(rows, poly):
    return pl.pallas_call(
        apply_kernel,
        out_shape=jax.ShapeDtypeStruct(rows.shape, bf16),
        compiler_params=pltpu.CompilerParams(vmem_limit_bytes=16 * 2**20),
        cost_estimate=pl.CostEstimate(
            flops=4 * rows.shape[0] * RANK * RANK, bytes_accessed=2 * 2**20, transcendentals=0
        ),
        name="apply",
    )(rows, poly)


def on_device(gradients, momentum, slot_table, *, owners, group):
    matrix_count = gradients.shape[0]
    held_slots = momentum.shape[0]
    near = 1 << ((group.bit_length() - 1) // 2)
    shares = (near, group // near)
    place = jnp.concatenate(
        [
            slot_table.astype(jnp.int32),
            jnp.stack([lax.axis_index("owner"), lax.axis_index("fsdp")]).astype(jnp.int32),
        ]
    )

    far_steps, near_steps = list(range(2, owners)), list(range(1, min(2, owners)))
    arrived = {}
    first = [(0, d) for d in far_steps]
    later = [(slot, d) for slot in range(1, held_slots) for d in far_steps]
    beside = [(slot, d) for slot in range(held_slots) for d in near_steps]
    for wanted in (first, beside, later):
        pieces = pick(place, gradients, held_slots, wanted)
        for (slot, d), piece in zip(wanted, pieces):
            arrived[slot, d] = lax.ppermute(piece, "owner", partners(owners, d))

    order = [(slot, d) for slot in range(held_slots) for d in [0] + near_steps]
    order += [(slot, d) for slot in range(held_slots) for d in far_steps]
    renewed, rows, sums = None, {}, {}
    for slot, d in order:
        renewed, rows[slot, d], sums[slot] = blend(
            place,
            arrived[slot, d] if d else gradients,
            momentum,
            slot,
            d,
            matrix_count,
            renewed,
            sums.get(slot),
            shares if d == owners - 1 else None,
        )

    updates = None
    for slot in range(held_slots):
        share = sums[slot]
        line = share[0]
        for e1 in range(1, shares[0]):
            line = line + lax.ppermute(share[e1], "fsdp", partners(group, e1))
        mine = line[0]
        for e2 in range(1, shares[1]):
            mine = mine + lax.ppermute(line[e2], "fsdp", partners(group, e2 * near))
        own = [mine]
        for e2 in range(1, shares[1]):
            own.append(lax.ppermute(mine, "fsdp", partners(group, e2 * near)))
        stacked = jnp.stack(own)
        others = [lax.ppermute(stacked, "fsdp", partners(group, e1)) for e1 in range(1, shares[0])]
        poly = polynomial(place, shares, own, others)
        for d in far_steps + near_steps + [0]:
            out = apply_polynomial(rows[slot, d], poly)
            if d:
                out = lax.ppermute(out, "owner", partners(owners, d))
            updates = drop(place, out, gradients.shape, held_slots, slot, d, updates)
    return (updates, renewed)


def solution(mesh):
    return jax.shard_map(
        functools.partial(on_device, owners=mesh.shape["owner"], group=mesh.shape["fsdp"]),
        mesh=mesh,
        in_specs=(P(None, ("fsdp", "owner"), None), P("owner", "fsdp", None), P()),
        out_specs=(P(None, ("fsdp", "owner"), None), P("owner", "fsdp", None)),
        check_vma=False,
    )
```

```python
import functools
import math

import jax
import jax.numpy as jnp
from jax import lax
from jax.experimental import pallas as pl
from jax.experimental.pallas import tpu as pltpu
from jax.sharding import PartitionSpec as P

LONG = 16384
RANK = 512
ITERS = 5
TILE = 128

quintic = (3.4445, -4.775, 2.0315)
momentum_decay = 0.95
epsilon = 1e-07

BLOCKS = [(i, j) for i in range(RANK // TILE) for j in range(i, RANK // TILE)]
PACKED = len(BLOCKS) * TILE
TAIL = 16

f32, bf16 = jnp.float32, jnp.bfloat16


def in_hbm(x):
    return pltpu.with_memory_space_constraint(x, pltpu.HBM)


def matrix_of(place, count, slots, slot, d):
    wanted = slots * jnp.bitwise_xor(place[count], d) + slot
    found = jnp.int32(0)
    for m in range(1, count):
        found = found + jnp.where(place[m] == wanted, m, 0)
    return found


def group_index(place):
    return place[place.shape[0] - 1]


def partners(size, step):
    return [(i, i ^ step) for i in range(size)]


def blend_kernel(shares, buffers, has_sum, *refs):
    refs = list(refs)
    place = refs.pop(0)
    gradient, momentum = refs.pop(0), refs.pop(0)
    del refs[:buffers]
    before = refs.pop(0) if has_sum else None
    renewed, rows, total, held = refs
    step = pl.program_id(0)

    @pl.when(step == 0)
    def _():
        held[...] = before[...] if has_sum else jnp.zeros_like(held)

    g = gradient[...].astype(f32)
    m = momentum_decay * momentum[...] + g
    renewed[...] = m
    x = (g + momentum_decay * m).astype(bf16)
    rows[...] = x
    half = RANK // 2
    dims = (((0,), (0,)), ((), ()))
    upper = lax.dot_general(x[:, :half], x, dims, preferred_element_type=f32)
    lower = lax.dot_general(x[:, half:], x[:, half:], dims, preferred_element_type=f32)
    for n, (i, j) in enumerate(BLOCKS):
        part, i0, j0 = (upper, i, j) if i < half // TILE else (lower, i - half // TILE, j - half // TILE)
        held[n * TILE : (n + 1) * TILE, :] += part[
            i0 * TILE : (i0 + 1) * TILE, j0 * TILE : (j0 + 1) * TILE
        ]

    @pl.when(step == pl.num_programs(0) - 1)
    def _():
        if shares is None:
            total[...] = held[...]
        else:
            near, far = shares
            count = PACKED // (near * far)
            for e1 in range(near):
                for e2 in range(far):
                    who = jnp.bitwise_xor(group_index(place), e2 * near + e1)
                    start = pl.multiple_of(who * count, 8)
                    total[e1, e2] = held[pl.ds(start, count), :]


class Line:
    def __init__(self, place):
        self.place, self.last, self.due, self.waiting, self.passed = place, None, [], {}, {}

    def run(
        self,
        kernel,
        operands,
        specs,
        out_shape,
        out_specs,
        *,
        name,
        work,
        token=0,
        grid=(1,),
        scratch=(),
        aliases=None,
        vmem=8,
    ):
        before = [] if self.last is None or (token is None and out_shape) else [self.last]
        before += self.due
        keys = list(self.waiting)
        before += [self.waiting[key] for key in keys]
        skip, given, results = len(before), len(before) + len(operands), len(out_shape)
        aliases = {1 + skip + i: o for i, o in (aliases or {}).items()}
        for k in range(len(keys)):
            aliases[1 + skip - len(keys) + k] = results + k

        def body(place, *refs):
            kernel(place, *refs[skip : given + results], *refs[given + results + len(keys) :])

        any_spec = pl.BlockSpec(memory_space=pl.ANY)
        flops, moved = work
        outs = pl.pallas_call(
            body,
            grid_spec=pltpu.PrefetchScalarGridSpec(
                num_scalar_prefetch=1,
                grid=grid,
                in_specs=[any_spec] * skip + specs,
                out_specs=out_specs + [any_spec] * len(keys),
                scratch_shapes=list(scratch),
            ),
            out_shape=out_shape
            + [jax.ShapeDtypeStruct(self.waiting[key].shape, self.waiting[key].dtype) for key in keys],
            input_output_aliases=aliases,
            compiler_params=pltpu.CompilerParams(vmem_limit_bytes=vmem * 2**20),
            cost_estimate=pl.CostEstimate(flops=20 * flops, bytes_accessed=20 * moved, transcendentals=0),
            name=name,
        )(self.place, *before, *operands)
        if token is not None:
            self.last = outs[token]
        elif not out_shape:
            self.last = outs[0]
        self.due, self.waiting = [], {}
        self.passed.update(zip(keys, outs[results:]))
        return outs[:results]


IN_VMEM = pl.BlockSpec(memory_space=pltpu.VMEM)
IN_HBM = pl.BlockSpec(memory_space=pltpu.HBM)


def pick_kernel(slots, count, wanted, place, gradients, *refs):
    targets, sems = refs[:-1], refs[-1]
    copies = []
    for n, (slot, d) in enumerate(wanted):
        source = gradients.at[matrix_of(place, count, slots, slot, d)]
        copies.append(pltpu.make_async_copy(source, targets[n], sems.at[n]))
        copies[-1].start()
    for copy in copies:
        copy.wait()


def pick(line, gradients, slots, wanted):
    count, rows, _ = gradients.shape
    return line.run(
        functools.partial(pick_kernel, slots, count, wanted),
        [in_hbm(gradients)],
        [IN_HBM],
        [jax.ShapeDtypeStruct((rows, RANK), bf16) for _ in wanted],
        [IN_VMEM for _ in wanted],
        name="pick",
        scratch=[pltpu.SemaphoreType.DMA((len(wanted),))],
        work=(0, 4 * len(wanted) * rows * RANK),
    )


def blend(line, gradient, momentum, slot, d, count, buffer, pair, before, shares):
    slots = momentum.shape[0]
    piece_rows = gradient.shape[-2]
    tile = min(256, piece_rows)
    steps = piece_rows // tile
    if d == 0:
        gradient_spec = pl.BlockSpec(
            (None, tile, RANK), lambda i, p: (matrix_of(p, count, slots, slot, 0), i, 0)
        )
        gradient = in_hbm(gradient)
    else:
        gradient_spec = pl.BlockSpec((tile, RANK), lambda i, p: (i, 0))
    momentum_spec = pl.BlockSpec(
        (None, tile, RANK), lambda i, p: (slot, jnp.bitwise_xor(p[count], d) * steps + i, 0)
    )
    in_specs, operands = [gradient_spec, momentum_spec], [gradient, in_hbm(momentum)]
    aliases = {}
    for result, array in enumerate((buffer, pair)):
        if array is not None:
            aliases[len(operands)] = result
            in_specs.append(IN_HBM if result == 0 else pl.BlockSpec(memory_space=pl.ANY))
            operands.append(in_hbm(array) if result == 0 else array)
    if d < 2:
        rows_shape, rows_spec = (piece_rows, RANK), pl.BlockSpec((tile, RANK), lambda i, p: (i, 0))
    else:
        rows_shape = (2, piece_rows, RANK)
        rows_spec = pl.BlockSpec((None, tile, RANK), lambda i, p: (d % 2, i, 0))
    if before is not None:
        in_specs.append(pl.BlockSpec((PACKED, TILE), lambda i, p: (0, 0)))
        operands.append(before)
    if shares is None:
        total = (PACKED, TILE)
    else:
        total = (*shares, PACKED // (shares[0] * shares[1]), TILE)
    return line.run(
        functools.partial(blend_kernel, shares, len(aliases), before is not None),
        operands,
        in_specs,
        [
            pltpu.HBM(momentum.shape, f32),
            jax.ShapeDtypeStruct(rows_shape, bf16),
            jax.ShapeDtypeStruct(total, f32),
        ],
        [
            momentum_spec,
            rows_spec,
            pl.BlockSpec(total, lambda i, p: (0,) * len(total)),
        ],
        name="blend",
        token=2,
        grid=(steps,),
        scratch=[pltpu.VMEM((PACKED, TILE), f32)],
        aliases=aliases,
        vmem=12,
        work=(2 * piece_rows * RANK * RANK, piece_rows * RANK * 12),
    )


def add_near_kernel(place, share, *refs):
    far = share.shape[1]
    received, targets = refs[: len(refs) - far], refs[len(refs) - far :]
    for e2, target in enumerate(targets):
        total = share[0, e2]
        for other in received:
            total = total + other[e2]
        target[...] = total


def add_near(line, share, received):
    _, far, count, _ = share.shape
    return line.run(
        add_near_kernel,
        [share, *received],
        [IN_VMEM] * (1 + len(received)),
        [jax.ShapeDtypeStruct((count, TILE), f32)] * far,
        [IN_VMEM] * far,
        name="add_near",
        work=(0, 12 * far * count * TILE),
    )


def add_far_kernel(place, *refs):
    total = refs[0][...]
    for other in refs[1:-1]:
        total = total + other[...]
    refs[-1][...] = total


def add_far(line, parts):
    return line.run(
        add_far_kernel,
        list(parts),
        [IN_VMEM] * len(parts),
        [jax.ShapeDtypeStruct(parts[0].shape, f32)],
        [IN_VMEM],
        name="add_far",
        work=(0, 4 * (len(parts) + 1) * parts[0].size),
    )[0]


def step(line, array):
    line.waiting["step"] = array
    line.run(lambda place: None, [], [], [], [], name="step", token=None, work=(0, 0))
    return line.passed["step"]


def stack_kernel(place, *refs):
    for e, part in enumerate(refs[:-1]):
        refs[-1][e] = part[...]


def stack(line, parts):
    return line.run(
        stack_kernel,
        list(parts),
        [IN_VMEM] * len(parts),
        [jax.ShapeDtypeStruct((len(parts), *parts[0].shape), f32)],
        [IN_VMEM],
        name="stack",
        work=(0, 8 * len(parts) * parts[0].size),
    )[0]


SHIFTS = (0.0, 0.0, 0.1, 0.6, 0.85)
PASSES = (1, 1, 3, 1, 1)
HALF = RANK // 2


def dot(a, b):
    return jnp.dot(a, b, preferred_element_type=f32)


def whole(x):
    top, corner = x
    return jnp.concatenate([top, jnp.concatenate([top[:, HALF:].T, corner], axis=1)], axis=0)


def operand(x, passes):
    high = tuple(part.astype(bf16) for part in x)
    if passes == 1:
        return (whole(high),)
    low = tuple((part - rounded.astype(f32)).astype(bf16) for part, rounded in zip(x, high))
    return (whole(high), whole(low))


def product(a, b):
    top, corner = dot(a[0][:HALF], b[0]), dot(a[0][HALF:], b[0][:, HALF:])
    if len(a) > 1:
        top += dot(a[0][:HALF], b[1]) + dot(a[1][:HALF], b[0])
        corner += dot(a[0][HALF:], b[1][:, HALF:]) + dot(a[1][HALF:], b[0][:, HALF:])
    return (top, corner)


def combine(*terms):
    return tuple(
        functools.reduce(lambda x, y: x + y, [w * x[part] for w, x in terms]) for part in range(2)
    )


def add_identity(x, value):
    top, corner = x
    row = lax.broadcasted_iota(jnp.int32, (HALF, HALF), 0)
    column = lax.broadcasted_iota(jnp.int32, (HALF, HALF), 1)
    eye = jnp.where(row == column, value, 0.0)
    return (jnp.concatenate([top[:, :HALF] + eye, top[:, HALF:]], axis=1), corner + eye)


def polynomial_kernel(near, far, count, place, *refs):
    *shared, result, packed = refs
    for e1, other in enumerate(shared):
        for e2 in range(far):
            who = jnp.bitwise_xor(group_index(place), e2 * near + e1)
            packed[pl.ds(pl.multiple_of(who * count, 8), count), :] = other[e2]
    parts = {}
    trace = jnp.zeros((), f32)
    row = lax.broadcasted_iota(jnp.int32, (TILE, TILE), 0)
    column = lax.broadcasted_iota(jnp.int32, (TILE, TILE), 1)
    for n, (i, j) in enumerate(BLOCKS):
        block = packed[n * TILE : (n + 1) * TILE, :]
        parts[i, j] = block
        if i == j:
            trace = trace + jnp.sum(jnp.where(row == column, block, 0.0))
    for i, j in ((0, 1), (2, 3)):
        parts[j, i] = parts[i, j].T

    def rows_of(count, first):
        return jnp.concatenate(
            [
                jnp.concatenate([parts[i, j] for j in range(first, RANK // TILE)], axis=1)
                for i in range(first, first + count)
            ],
            axis=0,
        )

    half = HALF // TILE
    scale = 1.0 / (jnp.sqrt(jnp.full((1, 1), trace, f32)) + epsilon)
    rest = tuple((x * scale) * scale for x in (rows_of(half, 0), rows_of(half, half)))
    a, b, c = quintic
    poly = None
    for k in range(ITERS):
        shift = SHIFTS[k]
        gain = a + b * shift + c * shift * shift
        d = operand(rest, PASSES[k])
        step = combine((b + 2 * c * shift, rest), (c, product(d, d)))
        s = operand(step, PASSES[k])
        if poly is None:
            poly = add_identity(step, gain)
        else:
            poly = combine((gain, poly), (1.0, product(operand(poly, PASSES[k]), s)))
        if k < ITERS - 1:
            middle = combine((gain, rest), (shift, step), (1.0, product(d, s)))
            turned = product(operand(middle, PASSES[k]), s)
            rest = combine((gain, middle), (gain * shift, step), (1.0, turned))
            rest = add_identity(rest, gain * gain * shift - SHIFTS[k + 1])
    top, corner = tuple(x * (scale * math.sqrt(max(LONG, RANK))) for x in poly)
    for n, (i, j) in enumerate(BLOCKS):
        part, i0, j0 = (top, i, j) if i < half else (corner, i - half, j - half)
        block = part[i0 * TILE : (i0 + 1) * TILE, j0 * TILE : (j0 + 1) * TILE]
        high = block.astype(bf16)
        result[n * TILE : (n + 1) * TILE, :] = high
        if i == j:
            low = jnp.where(row == column, block - high.astype(f32), 0.0)
            result[PACKED + i * TAIL : PACKED + (i + 1) * TAIL, :] = jnp.broadcast_to(
                jnp.sum(low, axis=0, keepdims=True), (TAIL, TILE)
            ).astype(bf16)


def polynomial(line, shared):
    near, (far, count, _) = len(shared), shared[0].shape
    return line.run(
        functools.partial(polynomial_kernel, near, far, count),
        list(shared),
        [IN_VMEM] * near,
        [jax.ShapeDtypeStruct((PACKED + RANK // TILE * TAIL, TILE), bf16)],
        [IN_VMEM],
        name="polynomial",
        scratch=[pltpu.VMEM((PACKED, TILE), f32)],
        vmem=20,
        work=(20 * 2 * RANK**3, 2 * 2**20),
    )[0]


def finish_kernel(slots, slot, steps, matrices, picks, place, *refs):
    refs = list(refs)
    count = len(steps)
    pieces, polys = refs[:count], refs[count : 2 * count]
    updates, _, held, sems = refs[-4:]
    copies = []
    for n, d in enumerate(steps):
        parts = {}
        for k, (i, j) in enumerate(BLOCKS):
            parts[i, j] = polys[n][k * TILE : (k + 1) * TILE, :]
            if i != j:
                parts[j, i] = parts[i, j].T
        sides = range(RANK // TILE)
        poly = jnp.concatenate(
            [jnp.concatenate([parts[i, j] for j in sides], axis=1) for i in sides], axis=0
        )
        low = jnp.concatenate(
            [polys[n][PACKED + i * TAIL : PACKED + (i + 1) * TAIL, :][:1] for i in sides], axis=1
        )
        x = pieces[n][...] if picks[n] is None else pieces[n][picks[n]]
        held[n] = (dot(x, poly) + x.astype(f32) * low.astype(f32)).astype(bf16)
        target = updates.at[matrix_of(place, matrices, slots, slot, d)]
        copies.append(pltpu.make_async_copy(held.at[n], target, sems.at[n]))
        copies[-1].start()
    for copy in copies:
        copy.wait()


def finish(line, slots, slot, steps, pieces, polys, shape, buffer):
    operands = [piece for piece, _ in pieces] + list(polys)
    specs = [IN_VMEM] * len(operands)
    aliases = {}
    if buffer is not None:
        aliases = {len(operands): 0}
        operands.append(in_hbm(buffer))
        specs.append(IN_HBM)
    return line.run(
        functools.partial(finish_kernel, slots, slot, steps, shape[0], [index for _, index in pieces]),
        operands,
        specs,
        [pltpu.HBM(shape, bf16), jax.ShapeDtypeStruct((8, TILE), f32)],
        [IN_HBM, IN_VMEM],
        name="finish",
        token=1,
        scratch=[pltpu.VMEM((len(steps), shape[1], RANK), bf16), pltpu.SemaphoreType.DMA((len(steps),))],
        aliases=aliases,
        vmem=12,
        work=(2 * len(steps) * shape[1] * RANK * RANK, 4 * len(steps) * shape[1] * RANK),
    )[0]


def on_device(gradients, momentum, slot_table, *, owners, group):
    matrix_count = gradients.shape[0]
    held_slots = momentum.shape[0]
    near = 1 << ((group.bit_length() - 1) // 2)
    shares = (near, group // near)
    place = jnp.concatenate(
        [
            slot_table.astype(jnp.int32),
            jnp.stack([lax.axis_index("owner"), lax.axis_index("fsdp")]).astype(jnp.int32),
        ]
    )

    line = Line(place)
    all_slots = range(held_slots)
    far_steps, near_steps = list(range(2, owners)), list(range(1, min(2, owners)))
    arrived = {}
    wanted = [(0, d) for d in far_steps] + [(slot, d) for slot in all_slots for d in near_steps]
    wanted += [(slot, d) for slot in range(1, held_slots) for d in far_steps]
    picked = {}
    for few in (wanted[:1], wanted[1:]):
        picked.update(zip(few, pick(line, gradients, held_slots, few)))

    def send(pieces):
        for slot, d in pieces:
            arrived[slot, d] = lax.ppermute(picked[slot, d], "owner", partners(owners, d))

    renewed, rows, returned, sums, lines, mine, gathered, polys = None, {}, {}, {}, {}, {}, {}, {}

    def blend_piece(slot, d, then=()):
        nonlocal renewed
        line.waiting.update({piece: picked[piece] for piece in then})
        renewed, rows[slot, d], sums[slot] = blend(
            line,
            arrived[slot, d] if d else gradients,
            momentum,
            slot,
            d,
            matrix_count,
            renewed,
            rows[slot, d - 1] if d > 1 and d % 2 else None,
            sums.get(slot),
            shares if d == owners - 1 else None,
        )
        picked.update({piece: line.passed[piece] for piece in then})
        send(then)

    def send_back(slot, d):
        if d == 0:
            returned[slot, 0] = rows[slot, 0], None
        elif d == 1:
            returned[slot, 1] = lax.ppermute(rows[slot, 1], "owner", partners(owners, 1)), None
        else:
            pair = lax.ppermute(rows[slot, d + 1], "owner", partners(owners, d))
            returned[slot, d] = pair, 0
            returned[slot, d + 1] = lax.ppermute(pair, "owner", partners(owners, 1)), 1

    def across_near(x, e1):
        return lax.ppermute(x, "fsdp", partners(group, e1))

    def across_far(x, e2):
        return lax.ppermute(x, "fsdp", partners(group, e2 * near))

    def first_sum(slot):
        received = [across_near(sums[slot][e1], e1) for e1 in range(1, near)]
        lines[slot] = add_near(line, sums[slot], received)

    def second_sum(slot):
        parts = lines[slot]
        received = [across_far(parts[e2], e2) for e2 in range(1, shares[1])]
        mine[slot] = add_far(line, [parts[0], *received])

    def collect(slot):
        part = mine[slot]
        whole_line = stack(line, [part] + [across_far(part, e2) for e2 in range(1, shares[1])])
        gathered[slot] = [whole_line] + [across_near(whole_line, e1) for e1 in range(1, near)]

    def make_polynomial(slot):
        polys[slot, 0] = polynomial(line, gathered[slot])
        for d in far_steps[::2]:
            polys[slot, d] = lax.ppermute(polys[slot, 0], "owner", partners(owners, d))
        for d in near_steps:
            polys[slot, d] = lax.ppermute(polys[slot, 0], "owner", partners(owners, d))

    def pass_polynomials(slot):
        for d in far_steps[::2]:
            polys[slot, d] = step(line, polys[slot, d])
            polys[slot, d + 1] = lax.ppermute(polys[slot, d], "owner", partners(owners, 1))

    updates = None

    def finish_steps(slot, steps):
        nonlocal updates
        updates = finish(
            line,
            held_slots,
            slot,
            steps,
            [returned[slot, d] for d in steps],
            [polys[slot, d] for d in steps],
            gradients.shape,
            updates,
        )

    def expect(*wanted):
        line.due += [returned[slot, d][0] for slot, d in wanted if d < owners]

    far_pieces = [(slot, d) for slot in all_slots for d in far_steps]
    near_pieces = [(slot, d) for slot in all_slots for d in near_steps]
    send(far_pieces[:2] + near_pieces[:1])
    blend_piece(0, 0, far_pieces[2:] + near_pieces[1:])
    blend_piece(1, 0)
    for slot in all_slots:
        send_back(slot, 0)
    for d in near_steps:
        for slot in all_slots:
            blend_piece(slot, d)
            send_back(slot, d)
    for d in far_steps[:-1]:
        blend_piece(0, d)
    expect((0, 1))
    for d in far_steps[-1:]:
        blend_piece(0, d)
    expect((1, 1))
    for d in far_steps[:-1]:
        blend_piece(1, d)
    for d in far_steps[1::2]:
        line.waiting[d] = rows[0, d]
    first_sum(0)
    for d in far_steps[1::2]:
        rows[0, d] = line.passed[d]
        send_back(0, d - 1)
    for d in far_steps[-1:]:
        blend_piece(1, d)
    line.waiting["sum"] = sums[1]
    second_sum(0)
    sums[1] = line.passed["sum"]
    first_sum(1)
    collect(0)
    expect(*[(0, d) for d in far_steps[::2]])
    for d in far_steps[1::2]:
        rows[1, d] = step(line, rows[1, d])
        send_back(1, d - 1)
    second_sum(1)
    collect(1)
    make_polynomial(0)
    make_polynomial(1)
    finish_steps(0, [0] + near_steps)
    pass_polynomials(0)
    finish_steps(1, [0] + near_steps)
    finish_steps(0, far_steps)
    pass_polynomials(1)
    for d in far_steps:
        finish_steps(1, [d])
    return (updates, renewed)


def solution(mesh):
    return jax.shard_map(
        functools.partial(on_device, owners=mesh.shape["owner"], group=mesh.shape["fsdp"]),
        mesh=mesh,
        in_specs=(P(None, ("fsdp", "owner"), None), P("owner", "fsdp", None), P()),
        out_specs=(P(None, ("fsdp", "owner"), None), P("owner", "fsdp", None)),
        check_vma=False,
    )
```

```python
import functools
import math

import jax
import jax.numpy as jnp
from jax import lax
from jax.experimental import pallas as pl
from jax.experimental.pallas import tpu as pltpu
from jax.sharding import PartitionSpec as P

LONG = 16384
RANK = 512
ITERS = 5
TILE = 128

quintic = (3.4445, -4.775, 2.0315)
momentum_decay = 0.95
epsilon = 1e-07

BLOCKS = [(i, j) for i in range(RANK // TILE) for j in range(i, RANK // TILE)]
PACKED = len(BLOCKS) * TILE
TAIL = 16

f32, bf16 = jnp.float32, jnp.bfloat16


def in_hbm(x):
    return pltpu.with_memory_space_constraint(x, pltpu.HBM)


def matrix_of(place, count, slots, slot, d):
    wanted = slots * jnp.bitwise_xor(place[count], d) + slot
    found = jnp.int32(0)
    for m in range(1, count):
        found = found + jnp.where(place[m] == wanted, m, 0)
    return found


def group_index(place):
    return place[place.shape[0] - 1]


def partners(size, step):
    return [(i, i ^ step) for i in range(size)]


def blend_kernel(shares, buffers, has_sum, *refs):
    refs = list(refs)
    place = refs.pop(0)
    gradient, momentum = refs.pop(0), refs.pop(0)
    del refs[:buffers]
    before = refs.pop(0) if has_sum else None
    renewed, rows, total, held = refs
    step = pl.program_id(0)

    @pl.when(step == 0)
    def _():
        held[...] = before[...] if has_sum else jnp.zeros_like(held)

    g = gradient[...].astype(f32)
    m = momentum_decay * momentum[...] + g
    renewed[...] = m
    x = (g + momentum_decay * m).astype(bf16)
    rows[...] = x
    half = RANK // 2
    dims = (((0,), (0,)), ((), ()))
    upper = lax.dot_general(x[:, :half], x, dims, preferred_element_type=f32)
    lower = lax.dot_general(x[:, half:], x[:, half:], dims, preferred_element_type=f32)
    for n, (i, j) in enumerate(BLOCKS):
        part, i0, j0 = (upper, i, j) if i < half // TILE else (lower, i - half // TILE, j - half // TILE)
        held[n * TILE : (n + 1) * TILE, :] += part[
            i0 * TILE : (i0 + 1) * TILE, j0 * TILE : (j0 + 1) * TILE
        ]

    @pl.when(step == pl.num_programs(0) - 1)
    def _():
        if shares is None:
            total[...] = held[...]
        else:
            near, far = shares
            count = PACKED // (near * far)
            for e1 in range(near):
                for e2 in range(far):
                    who = jnp.bitwise_xor(group_index(place), e2 * near + e1)
                    start = pl.multiple_of(who * count, 8)
                    total[e1, e2] = held[pl.ds(start, count), :]


class Line:
    def __init__(self, place):
        self.place, self.last, self.due, self.waiting, self.passed = place, None, [], {}, {}

    def run(
        self,
        kernel,
        operands,
        specs,
        out_shape,
        out_specs,
        *,
        name,
        work,
        token=0,
        grid=(1,),
        scratch=(),
        aliases=None,
        vmem=8,
    ):
        before = [] if self.last is None or (token is None and out_shape) else [self.last]
        before += self.due
        keys = list(self.waiting)
        before += [self.waiting[key] for key in keys]
        skip, given, results = len(before), len(before) + len(operands), len(out_shape)
        aliases = {1 + skip + i: o for i, o in (aliases or {}).items()}
        for k in range(len(keys)):
            aliases[1 + skip - len(keys) + k] = results + k

        def body(place, *refs):
            kernel(place, *refs[skip : given + results], *refs[given + results + len(keys) :])

        any_spec = pl.BlockSpec(memory_space=pl.ANY)
        flops, moved = work
        outs = pl.pallas_call(
            body,
            grid_spec=pltpu.PrefetchScalarGridSpec(
                num_scalar_prefetch=1,
                grid=grid,
                in_specs=[any_spec] * skip + specs,
                out_specs=out_specs + [any_spec] * len(keys),
                scratch_shapes=list(scratch),
            ),
            out_shape=out_shape
            + [jax.ShapeDtypeStruct(self.waiting[key].shape, self.waiting[key].dtype) for key in keys],
            input_output_aliases=aliases,
            compiler_params=pltpu.CompilerParams(vmem_limit_bytes=vmem * 2**20),
            cost_estimate=pl.CostEstimate(flops=20 * flops, bytes_accessed=20 * moved, transcendentals=0),
            name=name,
        )(self.place, *before, *operands)
        if token is not None:
            self.last = outs[token]
        elif not out_shape:
            self.last = outs[0]
        self.due, self.waiting = [], {}
        self.passed.update(zip(keys, outs[results:]))
        return outs[:results]


IN_VMEM = pl.BlockSpec(memory_space=pltpu.VMEM)
IN_HBM = pl.BlockSpec(memory_space=pltpu.HBM)


def pick_kernel(slots, count, wanted, place, gradients, *refs):
    targets, sems = refs[:-1], refs[-1]
    copies = []
    for n, (slot, d) in enumerate(wanted):
        source = gradients.at[matrix_of(place, count, slots, slot, d)]
        copies.append(pltpu.make_async_copy(source, targets[n], sems.at[n]))
        copies[-1].start()
    for copy in copies:
        copy.wait()


def pick(line, gradients, slots, wanted):
    count, rows, _ = gradients.shape
    return line.run(
        functools.partial(pick_kernel, slots, count, wanted),
        [in_hbm(gradients)],
        [IN_HBM],
        [jax.ShapeDtypeStruct((rows, RANK), bf16) for _ in wanted],
        [IN_VMEM for _ in wanted],
        name="pick",
        scratch=[pltpu.SemaphoreType.DMA((len(wanted),))],
        work=(0, 4 * len(wanted) * rows * RANK),
    )


def blend(line, gradient, momentum, slot, d, count, buffer, pair, before, shares):
    slots = momentum.shape[0]
    piece_rows = gradient.shape[-2]
    tile = min(256, piece_rows)
    steps = piece_rows // tile
    if d == 0:
        gradient_spec = pl.BlockSpec(
            (None, tile, RANK), lambda i, p: (matrix_of(p, count, slots, slot, 0), i, 0)
        )
        gradient = in_hbm(gradient)
    else:
        gradient_spec = pl.BlockSpec((tile, RANK), lambda i, p: (i, 0))
    momentum_spec = pl.BlockSpec(
        (None, tile, RANK), lambda i, p: (slot, jnp.bitwise_xor(p[count], d) * steps + i, 0)
    )
    in_specs, operands = [gradient_spec, momentum_spec], [gradient, in_hbm(momentum)]
    aliases = {}
    for result, array in enumerate((buffer, pair)):
        if array is not None:
            aliases[len(operands)] = result
            in_specs.append(IN_HBM if result == 0 else pl.BlockSpec(memory_space=pl.ANY))
            operands.append(in_hbm(array) if result == 0 else array)
    if d < 2:
        rows_shape, rows_spec = (piece_rows, RANK), pl.BlockSpec((tile, RANK), lambda i, p: (i, 0))
    else:
        rows_shape = (2, piece_rows, RANK)
        rows_spec = pl.BlockSpec((None, tile, RANK), lambda i, p: (d % 2, i, 0))
    if before is not None:
        in_specs.append(pl.BlockSpec((PACKED, TILE), lambda i, p: (0, 0)))
        operands.append(before)
    if shares is None:
        total = (PACKED, TILE)
    else:
        total = (*shares, PACKED // (shares[0] * shares[1]), TILE)
    return line.run(
        functools.partial(blend_kernel, shares, len(aliases), before is not None),
        operands,
        in_specs,
        [
            pltpu.HBM(momentum.shape, f32),
            jax.ShapeDtypeStruct(rows_shape, bf16),
            jax.ShapeDtypeStruct(total, f32),
        ],
        [
            momentum_spec,
            rows_spec,
            pl.BlockSpec(total, lambda i, p: (0,) * len(total)),
        ],
        name="blend",
        token=2,
        grid=(steps,),
        scratch=[pltpu.VMEM((PACKED, TILE), f32)],
        aliases=aliases,
        vmem=12,
        work=(2 * piece_rows * RANK * RANK, piece_rows * RANK * 12),
    )


def add_near_kernel(place, share, *refs):
    far = share.shape[1]
    received, targets = refs[: len(refs) - far], refs[len(refs) - far :]
    for e2, target in enumerate(targets):
        total = share[0, e2]
        for other in received:
            total = total + other[e2]
        target[...] = total


def add_near(line, share, received):
    _, far, count, _ = share.shape
    return line.run(
        add_near_kernel,
        [share, *received],
        [IN_VMEM] * (1 + len(received)),
        [jax.ShapeDtypeStruct((count, TILE), f32)] * far,
        [IN_VMEM] * far,
        name="add_near",
        work=(0, 12 * far * count * TILE),
    )


def add_far_kernel(place, *refs):
    total = refs[0][...]
    for other in refs[1:-1]:
        total = total + other[...]
    refs[-1][...] = total


def add_far(line, parts):
    return line.run(
        add_far_kernel,
        list(parts),
        [IN_VMEM] * len(parts),
        [jax.ShapeDtypeStruct(parts[0].shape, f32)],
        [IN_VMEM],
        name="add_far",
        work=(0, 4 * (len(parts) + 1) * parts[0].size),
    )[0]


def step(line, array):
    line.waiting["step"] = array
    line.run(lambda place: None, [], [], [], [], name="step", token=None, work=(0, 0))
    return line.passed["step"]


def stack_kernel(place, *refs):
    for e, part in enumerate(refs[:-1]):
        refs[-1][e] = part[...]


def stack(line, parts):
    return line.run(
        stack_kernel,
        list(parts),
        [IN_VMEM] * len(parts),
        [jax.ShapeDtypeStruct((len(parts), *parts[0].shape), f32)],
        [IN_VMEM],
        name="stack",
        work=(0, 8 * len(parts) * parts[0].size),
    )[0]


SHIFTS = (0.0, 0.0, 0.1, 0.6, 0.85)
PASSES = (1, 1, 3, 1, 1)
HALF = RANK // 2


def dot(a, b):
    return jnp.dot(a, b, preferred_element_type=f32)


def whole(x):
    top, corner = x
    return jnp.concatenate([top, jnp.concatenate([top[:, HALF:].T, corner], axis=1)], axis=0)


def operand(x, passes):
    high = tuple(part.astype(bf16) for part in x)
    if passes == 1:
        return (whole(high),)
    low = tuple((part - rounded.astype(f32)).astype(bf16) for part, rounded in zip(x, high))
    return (whole(high), whole(low))


def product(a, b):
    top, corner = dot(a[0][:HALF], b[0]), dot(a[0][HALF:], b[0][:, HALF:])
    if len(a) > 1:
        top += dot(a[0][:HALF], b[1]) + dot(a[1][:HALF], b[0])
        corner += dot(a[0][HALF:], b[1][:, HALF:]) + dot(a[1][HALF:], b[0][:, HALF:])
    return (top, corner)


def combine(*terms):
    return tuple(
        functools.reduce(lambda x, y: x + y, [w * x[part] for w, x in terms]) for part in range(2)
    )


def add_identity(x, value):
    top, corner = x
    row = lax.broadcasted_iota(jnp.int32, (HALF, HALF), 0)
    column = lax.broadcasted_iota(jnp.int32, (HALF, HALF), 1)
    eye = jnp.where(row == column, value, 0.0)
    return (jnp.concatenate([top[:, :HALF] + eye, top[:, HALF:]], axis=1), corner + eye)


def polynomial_kernel(near, far, count, place, *refs):
    *shared, result, packed = refs
    for e1, other in enumerate(shared):
        for e2 in range(far):
            who = jnp.bitwise_xor(group_index(place), e2 * near + e1)
            packed[pl.ds(pl.multiple_of(who * count, 8), count), :] = other[e2]
    parts = {}
    trace = jnp.zeros((), f32)
    row = lax.broadcasted_iota(jnp.int32, (TILE, TILE), 0)
    column = lax.broadcasted_iota(jnp.int32, (TILE, TILE), 1)
    for n, (i, j) in enumerate(BLOCKS):
        block = packed[n * TILE : (n + 1) * TILE, :]
        parts[i, j] = block
        if i == j:
            trace = trace + jnp.sum(jnp.where(row == column, block, 0.0))
    for i, j in ((0, 1), (2, 3)):
        parts[j, i] = parts[i, j].T

    def rows_of(count, first):
        return jnp.concatenate(
            [
                jnp.concatenate([parts[i, j] for j in range(first, RANK // TILE)], axis=1)
                for i in range(first, first + count)
            ],
            axis=0,
        )

    half = HALF // TILE
    scale = 1.0 / (jnp.sqrt(jnp.full((1, 1), trace, f32)) + epsilon)
    rest = tuple((x * scale) * scale for x in (rows_of(half, 0), rows_of(half, half)))
    a, b, c = quintic
    poly = None
    for k in range(ITERS):
        shift = SHIFTS[k]
        gain = a + b * shift + c * shift * shift
        d = operand(rest, PASSES[k])
        step = combine((b + 2 * c * shift, rest), (c, product(d, d)))
        s = operand(step, PASSES[k])
        if poly is None:
            poly = add_identity(step, gain)
        else:
            poly = combine((gain, poly), (1.0, product(operand(poly, PASSES[k]), s)))
        if k < ITERS - 1:
            middle = combine((gain, rest), (shift, step), (1.0, product(d, s)))
            turned = product(operand(middle, PASSES[k]), s)
            rest = combine((gain, middle), (gain * shift, step), (1.0, turned))
            rest = add_identity(rest, gain * gain * shift - SHIFTS[k + 1])
    top, corner = tuple(x * (scale * math.sqrt(max(LONG, RANK))) for x in poly)
    for n, (i, j) in enumerate(BLOCKS):
        part, i0, j0 = (top, i, j) if i < half else (corner, i - half, j - half)
        block = part[i0 * TILE : (i0 + 1) * TILE, j0 * TILE : (j0 + 1) * TILE]
        high = block.astype(bf16)
        result[n * TILE : (n + 1) * TILE, :] = high
        if i == j:
            low = jnp.where(row == column, block - high.astype(f32), 0.0)
            result[PACKED + i * TAIL : PACKED + (i + 1) * TAIL, :] = jnp.broadcast_to(
                jnp.sum(low, axis=0, keepdims=True), (TAIL, TILE)
            ).astype(bf16)


def polynomial(line, shared):
    near, (far, count, _) = len(shared), shared[0].shape
    return line.run(
        functools.partial(polynomial_kernel, near, far, count),
        list(shared),
        [IN_VMEM] * near,
        [jax.ShapeDtypeStruct((PACKED + RANK // TILE * TAIL, TILE), bf16)],
        [IN_VMEM],
        name="polynomial",
        scratch=[pltpu.VMEM((PACKED, TILE), f32)],
        vmem=20,
        work=(RANK**3, 2**16),
    )[0]


def finish_kernel(slots, slot, steps, matrices, picks, place, *refs):
    refs = list(refs)
    count = len(steps)
    pieces, polys = refs[:count], refs[count : 2 * count]
    updates, _, held, sems = refs[-4:]
    copies = []
    for n, d in enumerate(steps):
        parts = {}
        for k, (i, j) in enumerate(BLOCKS):
            parts[i, j] = polys[n][k * TILE : (k + 1) * TILE, :]
            if i != j:
                parts[j, i] = parts[i, j].T
        sides = range(RANK // TILE)
        poly = jnp.concatenate(
            [jnp.concatenate([parts[i, j] for j in sides], axis=1) for i in sides], axis=0
        )
        low = jnp.concatenate(
            [polys[n][PACKED + i * TAIL : PACKED + (i + 1) * TAIL, :][:1] for i in sides], axis=1
        )
        x = pieces[n][...] if picks[n] is None else pieces[n][picks[n]]
        held[n] = (dot(x, poly) + x.astype(f32) * low.astype(f32)).astype(bf16)
        target = updates.at[matrix_of(place, matrices, slots, slot, d)]
        copies.append(pltpu.make_async_copy(held.at[n], target, sems.at[n]))
        copies[-1].start()
    for copy in copies:
        copy.wait()


def finish(line, slots, slot, steps, pieces, polys, shape, buffer):
    operands = [piece for piece, _ in pieces] + list(polys)
    specs = [IN_VMEM] * len(operands)
    aliases = {}
    if buffer is not None:
        aliases = {len(operands): 0}
        operands.append(in_hbm(buffer))
        specs.append(IN_HBM)
    return line.run(
        functools.partial(finish_kernel, slots, slot, steps, shape[0], [index for _, index in pieces]),
        operands,
        specs,
        [pltpu.HBM(shape, bf16), jax.ShapeDtypeStruct((8, TILE), f32)],
        [IN_HBM, IN_VMEM],
        name="finish",
        token=1,
        scratch=[pltpu.VMEM((len(steps), shape[1], RANK), bf16), pltpu.SemaphoreType.DMA((len(steps),))],
        aliases=aliases,
        vmem=12,
        work=(2 * len(steps) * shape[1] * RANK * RANK, 4 * len(steps) * shape[1] * RANK),
    )[0]


def on_device(gradients, momentum, slot_table, *, owners, group):
    matrix_count = gradients.shape[0]
    held_slots = momentum.shape[0]
    near = 1 << ((group.bit_length() - 1) // 2)
    shares = (near, group // near)
    place = jnp.concatenate(
        [
            slot_table.astype(jnp.int32),
            jnp.stack([lax.axis_index("owner"), lax.axis_index("fsdp")]).astype(jnp.int32),
        ]
    )

    line = Line(place)
    all_slots = range(held_slots)
    far_steps, near_steps = list(range(2, owners)), list(range(1, min(2, owners)))
    arrived = {}
    wanted = [(0, d) for d in far_steps] + [(slot, d) for slot in all_slots for d in near_steps]
    wanted += [(slot, d) for slot in range(1, held_slots) for d in far_steps]
    picked = {}
    for few in (wanted[:1], wanted[1:]):
        picked.update(zip(few, pick(line, gradients, held_slots, few)))

    def send(pieces):
        for slot, d in pieces:
            arrived[slot, d] = lax.ppermute(picked[slot, d], "owner", partners(owners, d))

    renewed, rows, returned, sums, lines, mine, gathered, polys = None, {}, {}, {}, {}, {}, {}, {}

    def blend_piece(slot, d, then=()):
        nonlocal renewed
        line.waiting.update({piece: picked[piece] for piece in then})
        renewed, rows[slot, d], sums[slot] = blend(
            line,
            arrived[slot, d] if d else gradients,
            momentum,
            slot,
            d,
            matrix_count,
            renewed,
            rows[slot, d - 1] if d > 1 and d % 2 else None,
            sums.get(slot),
            shares if d == owners - 1 else None,
        )
        picked.update({piece: line.passed[piece] for piece in then})
        send(then)

    def send_back(slot, d):
        if d == 0:
            returned[slot, 0] = rows[slot, 0], None
        elif d == 1:
            returned[slot, 1] = lax.ppermute(rows[slot, 1], "owner", partners(owners, 1)), None
        else:
            pair = lax.ppermute(rows[slot, d + 1], "owner", partners(owners, d))
            returned[slot, d] = pair, 0
            returned[slot, d + 1] = lax.ppermute(pair, "owner", partners(owners, 1)), 1

    def across_near(x, e1):
        return lax.ppermute(x, "fsdp", partners(group, e1))

    def across_far(x, e2):
        return lax.ppermute(x, "fsdp", partners(group, e2 * near))

    def first_sum(slot):
        received = [across_near(sums[slot][e1], e1) for e1 in range(1, near)]
        lines[slot] = add_near(line, sums[slot], received)

    def second_sum(slot):
        parts = lines[slot]
        received = [across_far(parts[e2], e2) for e2 in range(1, shares[1])]
        mine[slot] = add_far(line, [parts[0], *received])

    def collect(slot):
        part = mine[slot]
        whole_line = stack(line, [part] + [across_far(part, e2) for e2 in range(1, shares[1])])
        gathered[slot] = [whole_line] + [across_near(whole_line, e1) for e1 in range(1, near)]

    def make_polynomial(slot):
        polys[slot, 0] = polynomial(line, gathered[slot])
        for d in far_steps[::2]:
            polys[slot, d] = lax.ppermute(polys[slot, 0], "owner", partners(owners, d))
        for d in near_steps:
            polys[slot, d] = lax.ppermute(polys[slot, 0], "owner", partners(owners, d))

    def pass_polynomials(slot):
        for d in far_steps[::2]:
            polys[slot, d] = step(line, polys[slot, d])
            polys[slot, d + 1] = lax.ppermute(polys[slot, d], "owner", partners(owners, 1))

    updates = None

    def finish_steps(slot, steps):
        nonlocal updates
        updates = finish(
            line,
            held_slots,
            slot,
            steps,
            [returned[slot, d] for d in steps],
            [polys[slot, d] for d in steps],
            gradients.shape,
            updates,
        )

    def expect(*wanted):
        line.due += [returned[slot, d][0] for slot, d in wanted if d < owners]

    far_pieces = [(slot, d) for slot in all_slots for d in far_steps]
    near_pieces = [(slot, d) for slot in all_slots for d in near_steps]
    send(far_pieces[:2] + near_pieces[:1])
    blend_piece(0, 0, far_pieces[2:] + near_pieces[1:])
    blend_piece(1, 0)
    for slot in all_slots:
        send_back(slot, 0)
    for d in near_steps:
        for slot in all_slots:
            blend_piece(slot, d)
            send_back(slot, d)
    for d in far_steps[:-1]:
        blend_piece(0, d)
    expect((0, 1))
    for d in far_steps[-1:]:
        blend_piece(0, d)
    expect((1, 1))
    for d in far_steps[:-1]:
        blend_piece(1, d)
    for d in far_steps[1::2]:
        line.waiting[d] = rows[0, d]
    first_sum(0)
    for d in far_steps[1::2]:
        rows[0, d] = line.passed[d]
        send_back(0, d - 1)
    for d in far_steps[-1:]:
        blend_piece(1, d)
    line.waiting["sum"] = sums[1]
    second_sum(0)
    sums[1] = line.passed["sum"]
    first_sum(1)
    collect(0)
    expect(*[(0, d) for d in far_steps[::2]])
    for d in far_steps[1::2]:
        line.waiting[d] = rows[1, d]
    second_sum(1)
    for d in far_steps[1::2]:
        rows[1, d] = line.passed[d]
        send_back(1, d - 1)
    collect(1)
    make_polynomial(0)
    expect(*[(1, d) for d in far_steps[::2]])
    make_polynomial(1)
    finish_steps(0, [0] + near_steps)
    pass_polynomials(0)
    finish_steps(1, [0] + near_steps)
    finish_steps(0, far_steps)
    pass_polynomials(1)
    for d in far_steps:
        finish_steps(1, [d])
    return (updates, renewed)


def solution(mesh):
    return jax.shard_map(
        functools.partial(on_device, owners=mesh.shape["owner"], group=mesh.shape["fsdp"]),
        mesh=mesh,
        in_specs=(P(None, ("fsdp", "owner"), None), P("owner", "fsdp", None), P()),
        out_specs=(P(None, ("fsdp", "owner"), None), P("owner", "fsdp", None)),
        check_vma=False,
    )
```

```python
import functools
import math

import jax
import jax.numpy as jnp
from jax import lax
from jax.experimental import pallas as pl
from jax.experimental.pallas import tpu as pltpu
from jax.sharding import PartitionSpec as P

LONG = 16384
RANK = 512
ITERS = 5
TILE = 128

quintic = (3.4445, -4.775, 2.0315)
momentum_decay = 0.95
epsilon = 1e-07

SIDES = RANK // TILE
ABOVE = [(i, j) for i in range(SIDES) for j in range(i + 1, SIDES)]
TWOS = [(i, i + 1) for i in range(0, SIDES, 2)]
DIAGONALS = (len(ABOVE) + len(TWOS)) * TILE
POLY_ROWS = DIAGONALS + 16

f32, bf16 = jnp.float32, jnp.bfloat16


def in_hbm(x):
    return pltpu.with_memory_space_constraint(x, pltpu.HBM)


def matrix_of(place, count, slots, slot, d):
    wanted = slots * jnp.bitwise_xor(place[count], d) + slot
    found = jnp.int32(0)
    for m in range(1, count):
        found = found + jnp.where(place[m] == wanted, m, 0)
    return found


def group_index(place):
    return place[place.shape[0] - 1]


def packed_rows(group):
    return -(-(DIAGONALS + 8) // (8 * group)) * (8 * group)


def block_ids():
    return (
        lax.broadcasted_iota(jnp.int32, (TILE, TILE), 0),
        lax.broadcasted_iota(jnp.int32, (TILE, TILE), 1),
    )


def diagonal_of(block):
    row, column = block_ids()
    return jnp.sum(jnp.where(row == column, block, 0.0), axis=0, keepdims=True)


def pack(block):
    row, column = block_ids()
    blocks = [block(i, j) for i, j in ABOVE]
    blocks += [jnp.where(row <= column, block(i, i), block(j, j)) for i, j in TWOS]
    return blocks, [diagonal_of(block(j, j)) for _, j in TWOS]


def unpack(blocks, diagonals):
    row, column = block_ids()
    parts = dict(zip(ABOVE, blocks))
    for (i, j), both, diagonal in zip(TWOS, blocks[len(ABOVE) :], diagonals):
        turned = both.T
        parts[i, i] = jnp.where(row <= column, both, turned)
        parts[j, j] = jnp.where(row > column, both, jnp.where(row < column, turned, diagonal))
    return parts


def partners(size, step):
    return [(i, i ^ step) for i in range(size)]


def blend_kernel(buffers, has_sum, *refs):
    refs = list(refs)
    place = refs.pop(0)
    gradient, momentum = refs.pop(0), refs.pop(0)
    del refs[:buffers]
    before = refs.pop(0) if has_sum else None
    renewed, rows, total, held = refs
    step = pl.program_id(0)

    @pl.when(step == 0)
    def _():
        held[...] = before[...] if has_sum else jnp.zeros_like(held)

    g = gradient[...].astype(f32)
    m = momentum_decay * momentum[...] + g
    renewed[...] = m
    x = (g + momentum_decay * m).astype(bf16)
    rows[...] = x
    add_gram(held, x)

    @pl.when(step == pl.num_programs(0) - 1)
    def _():
        total[...] = held[...]


def add_gram(held, x):
    half, dims = RANK // 2, (((0,), (0,)), ((), ()))
    upper = lax.dot_general(x[:, :half], x, dims, preferred_element_type=f32)
    lower = lax.dot_general(x[:, half:], x[:, half:], dims, preferred_element_type=f32)

    def block(i, j):
        part, i0, j0 = (upper, i, j) if i < SIDES // 2 else (lower, i - SIDES // 2, j - SIDES // 2)
        return part[i0 * TILE : (i0 + 1) * TILE, j0 * TILE : (j0 + 1) * TILE]

    blocks, diagonals = pack(block)
    for n, part in enumerate(blocks):
        held[n * TILE : (n + 1) * TILE, :] += part
    for n, part in enumerate(diagonals):
        held[DIAGONALS + n : DIAGONALS + n + 1, :] += part


def fetch_kernel(slot, d, count, place, momentum, target, sem):
    rows = target.shape[0]
    start = pl.multiple_of(jnp.bitwise_xor(place[count], d) * rows, 8)
    copy = pltpu.make_async_copy(momentum.at[slot, pl.ds(start, rows)], target, sem)
    copy.start()
    copy.wait()


def fetch(line, momentum, slot, d, count, piece_rows):
    return line.run(
        functools.partial(fetch_kernel, slot, d, count),
        [in_hbm(momentum)],
        [IN_HBM],
        [jax.ShapeDtypeStruct((piece_rows, RANK), f32)],
        [IN_VMEM],
        name="fetch",
        scratch=[pltpu.SemaphoreType.DMA],
        work=(0, 8 * piece_rows * RANK),
    )[0]


def blend_last_kernel(slot, d, count, place, gradient, momentum, _buffer, _pair, before, renewed, pair, total, held, new, sems):
    rows = gradient.shape[0]
    tile = min(256, rows)
    first = jnp.bitwise_xor(place[count], d) * rows
    copies = []
    for n in range(rows // tile):
        part = pl.ds(n * tile, tile)
        g = gradient[part].astype(f32)
        m = momentum_decay * momentum[part] + g
        new[part] = m
        target = renewed.at[slot, pl.ds(pl.multiple_of(first + n * tile, 8), tile)]
        copies.append(pltpu.make_async_copy(new.at[part], target, sems.at[n]))
        copies[-1].start()
        pair[1, part] = (g + momentum_decay * m).astype(bf16)
    held[...] = before[...]
    add_gram(held, pair[1])
    near, far, size, _ = total.shape
    for e1 in range(near):
        for e2 in range(far):
            who = jnp.bitwise_xor(group_index(place), e2 * near + e1)
            total[e1, e2] = held[pl.ds(pl.multiple_of(who * size, 8), size), :]
    for copy in copies:
        copy.wait()


def blend_last(line, gradient, momentum, slot, d, count, buffer, pair, before, shares):
    piece_rows = gradient.shape[0]
    total = (*shares, before.shape[0] // (shares[0] * shares[1]), TILE)
    return line.run(
        functools.partial(blend_last_kernel, slot, d, count),
        [gradient, momentum, in_hbm(buffer), pair, before],
        [IN_VMEM, IN_VMEM, IN_HBM, IN_VMEM, IN_VMEM],
        [
            pltpu.HBM(buffer.shape, f32),
            jax.ShapeDtypeStruct(pair.shape, bf16),
            jax.ShapeDtypeStruct(total, f32),
        ],
        [IN_HBM, IN_VMEM, IN_VMEM],
        name="blend_last",
        token=2,
        scratch=[
            pltpu.VMEM(before.shape, f32),
            pltpu.VMEM((piece_rows, RANK), f32),
            pltpu.SemaphoreType.DMA((piece_rows // min(256, piece_rows),)),
        ],
        aliases={2: 0, 3: 1},
        vmem=12,
        work=(2 * piece_rows * RANK * RANK, piece_rows * RANK * 12),
    )


class Line:
    def __init__(self, place):
        self.place, self.last, self.due, self.waiting, self.passed = place, None, [], {}, {}

    def run(
        self,
        kernel,
        operands,
        specs,
        out_shape,
        out_specs,
        *,
        name,
        work,
        token=0,
        grid=(1,),
        scratch=(),
        aliases=None,
        vmem=8,
    ):
        before = [] if self.last is None or (token is None and out_shape) else [self.last]
        before += self.due
        keys = list(self.waiting)
        before += [self.waiting[key] for key in keys]
        skip, given, results = len(before), len(before) + len(operands), len(out_shape)
        aliases = {1 + skip + i: o for i, o in (aliases or {}).items()}
        for k in range(len(keys)):
            aliases[1 + skip - len(keys) + k] = results + k

        def body(place, *refs):
            kernel(place, *refs[skip : given + results], *refs[given + results + len(keys) :])

        any_spec = pl.BlockSpec(memory_space=pl.ANY)
        flops, moved = work
        outs = pl.pallas_call(
            body,
            grid_spec=pltpu.PrefetchScalarGridSpec(
                num_scalar_prefetch=1,
                grid=grid,
                in_specs=[any_spec] * skip + specs,
                out_specs=out_specs + [any_spec] * len(keys),
                scratch_shapes=list(scratch),
            ),
            out_shape=out_shape
            + [jax.ShapeDtypeStruct(self.waiting[key].shape, self.waiting[key].dtype) for key in keys],
            input_output_aliases=aliases,
            compiler_params=pltpu.CompilerParams(vmem_limit_bytes=vmem * 2**20),
            cost_estimate=pl.CostEstimate(flops=20 * flops, bytes_accessed=20 * moved, transcendentals=0),
            name=name,
        )(self.place, *before, *operands)
        if token is not None:
            self.last = outs[token]
        elif not out_shape:
            self.last = outs[0]
        self.due, self.waiting = [], {}
        self.passed.update(zip(keys, outs[results:]))
        return outs[:results]


IN_VMEM = pl.BlockSpec(memory_space=pltpu.VMEM)
IN_HBM = pl.BlockSpec(memory_space=pltpu.HBM)


def pick_kernel(slots, count, wanted, place, gradients, *refs):
    targets, sems = refs[:-1], refs[-1]
    copies = []
    for n, (slot, d) in enumerate(wanted):
        source = gradients.at[matrix_of(place, count, slots, slot, d)]
        copies.append(pltpu.make_async_copy(source, targets[n], sems.at[n]))
        copies[-1].start()
    for copy in copies:
        copy.wait()


def pick(line, gradients, slots, wanted):
    count, rows, _ = gradients.shape
    return line.run(
        functools.partial(pick_kernel, slots, count, wanted),
        [in_hbm(gradients)],
        [IN_HBM],
        [jax.ShapeDtypeStruct((rows, RANK), bf16) for _ in wanted],
        [IN_VMEM for _ in wanted],
        name="pick",
        scratch=[pltpu.SemaphoreType.DMA((len(wanted),))],
        work=(0, 4 * len(wanted) * rows * RANK),
    )


def blend(line, gradient, momentum, slot, d, count, buffer, pair, before, summed):
    slots = momentum.shape[0]
    piece_rows = gradient.shape[-2]
    tile = min(256, piece_rows)
    steps = piece_rows // tile
    if d == 0:
        gradient_spec = pl.BlockSpec(
            (None, tile, RANK), lambda i, p: (matrix_of(p, count, slots, slot, 0), i, 0)
        )
        gradient = in_hbm(gradient)
    else:
        gradient_spec = pl.BlockSpec((tile, RANK), lambda i, p: (i, 0))
    momentum_spec = pl.BlockSpec(
        (None, tile, RANK), lambda i, p: (slot, jnp.bitwise_xor(p[count], d) * steps + i, 0)
    )
    in_specs, operands = [gradient_spec, momentum_spec], [gradient, in_hbm(momentum)]
    aliases = {}
    for result, array in enumerate((buffer, pair)):
        if array is not None:
            aliases[len(operands)] = result
            in_specs.append(IN_HBM if result == 0 else pl.BlockSpec(memory_space=pl.ANY))
            operands.append(in_hbm(array) if result == 0 else array)
    if d < 2:
        rows_shape, rows_spec = (piece_rows, RANK), pl.BlockSpec((tile, RANK), lambda i, p: (i, 0))
    else:
        rows_shape = (2, piece_rows, RANK)
        rows_spec = pl.BlockSpec((None, tile, RANK), lambda i, p: (d % 2, i, 0))
    total = (summed, TILE)
    if before is not None:
        in_specs.append(pl.BlockSpec(total, lambda i, p: (0, 0)))
        operands.append(before)
    return line.run(
        functools.partial(blend_kernel, len(aliases), before is not None),
        operands,
        in_specs,
        [
            pltpu.HBM(momentum.shape, f32),
            jax.ShapeDtypeStruct(rows_shape, bf16),
            jax.ShapeDtypeStruct(total, f32),
        ],
        [
            momentum_spec,
            rows_spec,
            pl.BlockSpec(total, lambda i, p: (0, 0)),
        ],
        name="blend",
        token=2,
        grid=(steps,),
        scratch=[pltpu.VMEM(total, f32)],
        aliases=aliases,
        vmem=12,
        work=(2 * piece_rows * RANK * RANK, piece_rows * RANK * 12),
    )


def add_near_kernel(place, share, *refs):
    far = share.shape[1]
    received, targets = refs[: len(refs) - far], refs[len(refs) - far :]
    for e2, target in enumerate(targets):
        total = share[0, e2]
        for other in received:
            total = total + other[e2]
        target[...] = total


def add_near(line, share, received):
    _, far, count, _ = share.shape
    return line.run(
        add_near_kernel,
        [share, *received],
        [IN_VMEM] * (1 + len(received)),
        [jax.ShapeDtypeStruct((count, TILE), f32)] * far,
        [IN_VMEM] * far,
        name="add_near",
        work=(0, 12 * far * count * TILE),
    )


def add_far_kernel(place, *refs):
    total = refs[0][...]
    for other in refs[1:-1]:
        total = total + other[...]
    refs[-1][...] = total


def add_far(line, parts):
    return line.run(
        add_far_kernel,
        list(parts),
        [IN_VMEM] * len(parts),
        [jax.ShapeDtypeStruct(parts[0].shape, f32)],
        [IN_VMEM],
        name="add_far",
        work=(0, 4 * (len(parts) + 1) * parts[0].size),
    )[0]


def step(line, array):
    line.waiting["step"] = array
    line.run(lambda place: None, [], [], [], [], name="step", token=None, work=(0, 0))
    return line.passed["step"]


def stack_kernel(place, *refs):
    for e, part in enumerate(refs[:-1]):
        refs[-1][e] = part[...]


def stack(line, parts):
    return line.run(
        stack_kernel,
        list(parts),
        [IN_VMEM] * len(parts),
        [jax.ShapeDtypeStruct((len(parts), *parts[0].shape), f32)],
        [IN_VMEM],
        name="stack",
        work=(0, 8 * len(parts) * parts[0].size),
    )[0]


SHIFTS = (0.0, 0.0, 0.1, 0.6, 0.85)
FINE_TURN, FINE_POLY = 2, 3
HALF = RANK // 2


def dot(a, b):
    return jnp.dot(a, b, preferred_element_type=f32)


def whole(x):
    top, corner = x
    return jnp.concatenate([top, jnp.concatenate([top[:, HALF:].T, corner], axis=1)], axis=0)


def operand(x, passes):
    high = tuple(part.astype(bf16) for part in x)
    if passes == 1:
        return (whole(high),)
    low = tuple((part - rounded.astype(f32)).astype(bf16) for part, rounded in zip(x, high))
    return (whole(high), whole(low))


def product(a, b):
    top, corner = dot(a[0][:HALF], b[0]), dot(a[0][HALF:], b[0][:, HALF:])
    if len(a) > 1:
        top += dot(a[0][:HALF], b[1]) + dot(a[1][:HALF], b[0])
        corner += dot(a[0][HALF:], b[1][:, HALF:]) + dot(a[1][HALF:], b[0][:, HALF:])
    return (top, corner)


def combine(*terms):
    return tuple(
        functools.reduce(lambda x, y: x + y, [w * x[part] for w, x in terms]) for part in range(2)
    )


def add_identity(x, value):
    top, corner = x
    row = lax.broadcasted_iota(jnp.int32, (HALF, HALF), 0)
    column = lax.broadcasted_iota(jnp.int32, (HALF, HALF), 1)
    eye = jnp.where(row == column, value, 0.0)
    return (jnp.concatenate([top[:, :HALF] + eye, top[:, HALF:]], axis=1), corner + eye)


def polynomial_kernel(near, far, count, place, *refs):
    *shared, result, packed = refs
    for e1, other in enumerate(shared):
        for e2 in range(far):
            who = jnp.bitwise_xor(group_index(place), e2 * near + e1)
            packed[pl.ds(pl.multiple_of(who * count, 8), count), :] = other[e2]
    blocks = [packed[n * TILE : (n + 1) * TILE, :] for n in range(len(ABOVE) + len(TWOS))]
    diagonals = [packed[DIAGONALS + n : DIAGONALS + n + 1, :] for n in range(len(TWOS))]
    parts = unpack(blocks, diagonals)
    trace = jnp.sum(sum(diagonals) + sum(diagonal_of(both) for both in blocks[len(ABOVE) :]))
    for i, j in ((0, 1), (2, 3)):
        parts[j, i] = parts[i, j].T

    def rows_of(count, first):
        return jnp.concatenate(
            [
                jnp.concatenate([parts[i, j] for j in range(first, SIDES)], axis=1)
                for i in range(first, first + count)
            ],
            axis=0,
        )

    half = HALF // TILE
    scale = 1.0 / (jnp.sqrt(jnp.full((1, 1), trace, f32)) + epsilon)
    rest = tuple((x * scale) * scale for x in (rows_of(half, 0), rows_of(half, half)))
    a, b, c = quintic
    poly = None
    for k in range(ITERS):
        shift = SHIFTS[k]
        gain = a + b * shift + c * shift * shift
        d = operand(rest, 3 if k == FINE_TURN else 1)
        step = combine((b + 2 * c * shift, rest), (c, product(d[:1], d[:1])))
        s = operand(step, 3 if k in (FINE_TURN, FINE_POLY) else 1)
        if poly is None:
            poly = add_identity(step, gain)
        else:
            p = operand(poly, 3 if k == FINE_POLY else 1)
            poly = combine((gain, poly), (1.0, product(p, s)))
        if k < ITERS - 1:
            middle = combine((gain, rest), (shift, step), (1.0, product(d, s)))
            turned = product(operand(middle, 1), s)
            rest = combine((gain, middle), (gain * shift, step), (1.0, turned))
            rest = add_identity(rest, gain * gain * shift - SHIFTS[k + 1])
    top, corner = tuple(x * (scale * math.sqrt(max(LONG, RANK))) for x in poly)

    def block(i, j):
        part, i0, j0 = (top, i, j) if i < half else (corner, i - half, j - half)
        return part[i0 * TILE : (i0 + 1) * TILE, j0 * TILE : (j0 + 1) * TILE]

    blocks, seconds = pack(block)
    for n, part in enumerate(blocks):
        result[n * TILE : (n + 1) * TILE, :] = part.astype(bf16)
    lows = []
    for i in range(SIDES):
        diagonal = diagonal_of(block(i, i))
        lows.append(diagonal - diagonal.astype(bf16).astype(f32))
    rows = lows + seconds
    rows.append(jnp.zeros((POLY_ROWS - DIAGONALS - len(rows), TILE), f32))
    result[DIAGONALS:, :] = jnp.concatenate(rows, axis=0).astype(bf16)


def polynomial(line, shared):
    near, (far, count, _) = len(shared), shared[0].shape
    return line.run(
        functools.partial(polynomial_kernel, near, far, count),
        list(shared),
        [IN_VMEM] * near,
        [jax.ShapeDtypeStruct((POLY_ROWS, TILE), bf16)],
        [IN_VMEM],
        name="polynomial",
        scratch=[pltpu.VMEM((near * far * count, TILE), f32)],
        vmem=20,
        work=(RANK**3, 2**16),
    )[0]


def finish_kernel(slots, slot, steps, matrices, picks, place, *refs):
    refs = list(refs)
    count = len(steps)
    pieces, polys = refs[:count], refs[count : 2 * count]
    updates, _, held, sems = refs[-4:]
    copies = []
    for n, d in enumerate(steps):
        tail = polys[n][DIAGONALS:, :].astype(f32)
        blocks = [polys[n][k * TILE : (k + 1) * TILE, :] for k in range(len(ABOVE) + len(TWOS))]
        twos = [part.astype(f32) for part in blocks[len(ABOVE) :]]
        seconds = [tail[SIDES + k : SIDES + k + 1] for k in range(len(TWOS))]
        parts = unpack(blocks[: len(ABOVE)] + twos, seconds)
        for i in range(SIDES):
            parts[i, i] = parts[i, i].astype(bf16)
        for i, j in ABOVE:
            parts[j, i] = parts[i, j].T
        sides = range(SIDES)
        poly = jnp.concatenate(
            [jnp.concatenate([parts[i, j] for j in sides], axis=1) for i in sides], axis=0
        )
        low = jnp.concatenate([tail[i : i + 1] for i in sides], axis=1)
        rows = held.shape[1]
        tile = min(256, rows)
        target = updates.at[matrix_of(place, matrices, slots, slot, d)]
        for k in range(rows // tile):
            part = pl.ds(k * tile, tile)
            x = pieces[n][part] if picks[n] is None else pieces[n][picks[n], part]
            held[n, part] = (dot(x, poly) + x.astype(f32) * low).astype(bf16)
            copies.append(pltpu.make_async_copy(held.at[n, part], target.at[part], sems.at[len(copies)]))
            copies[-1].start()
    for copy in copies:
        copy.wait()


def finish(line, slots, slot, steps, pieces, polys, shape, buffer):
    operands = [piece for piece, _ in pieces] + list(polys)
    specs = [IN_VMEM] * len(operands)
    aliases = {}
    if buffer is not None:
        aliases = {len(operands): 0}
        operands.append(in_hbm(buffer))
        specs.append(IN_HBM)
    return line.run(
        functools.partial(finish_kernel, slots, slot, steps, shape[0], [index for _, index in pieces]),
        operands,
        specs,
        [pltpu.HBM(shape, bf16), jax.ShapeDtypeStruct((8, TILE), f32)],
        [IN_HBM, IN_VMEM],
        name="finish",
        token=1,
        scratch=[pltpu.VMEM((len(steps), shape[1], RANK), bf16), pltpu.SemaphoreType.DMA((len(steps) * max(1, shape[1] // 256),))],
        aliases=aliases,
        vmem=12,
        work=(2 * len(steps) * shape[1] * RANK * RANK, 4 * len(steps) * shape[1] * RANK),
    )[0]


def on_device(gradients, momentum, slot_table, *, owners, group):
    matrix_count = gradients.shape[0]
    held_slots = momentum.shape[0]
    near = 1 << ((group.bit_length() - 1) // 2)
    shares = (near, group // near)
    place = jnp.concatenate(
        [
            slot_table.astype(jnp.int32),
            jnp.stack([lax.axis_index("owner"), lax.axis_index("fsdp")]).astype(jnp.int32),
        ]
    )

    line = Line(place)
    all_slots = range(held_slots)
    far_steps, near_steps = list(range(2, owners)), list(range(1, min(2, owners)))
    arrived = {}
    wanted = [(0, d) for d in far_steps] + [(slot, d) for slot in all_slots for d in near_steps]
    wanted += [(slot, d) for slot in range(1, held_slots) for d in far_steps]
    picked = {}
    for few in (wanted[:1], wanted[1:]):
        picked.update(zip(few, pick(line, gradients, held_slots, few)))

    def send(pieces):
        for slot, d in pieces:
            arrived[slot, d] = lax.ppermute(picked[slot, d], "owner", partners(owners, d))

    fetched = {}
    renewed, rows, returned, sums, lines, mine, whole_lines, gathered, polys = None, {}, {}, {}, {}, {}, {}, {}, {}

    summed = packed_rows(group)

    def blend_piece(slot, d, then=()):
        nonlocal renewed
        line.waiting.update({piece: picked[piece] for piece in then})
        gradient = arrived[slot, d] if d else gradients
        if d == owners - 1:
            renewed, rows[slot, d], sums[slot] = blend_last(
                line, gradient, fetched[slot], slot, d, matrix_count, renewed, rows[slot, d - 1], sums[slot], shares
            )
        else:
            renewed, rows[slot, d], sums[slot] = blend(
                line,
                gradient,
                momentum,
                slot,
                d,
                matrix_count,
                renewed,
                rows[slot, d - 1] if d > 1 and d % 2 else None,
                sums.get(slot),
                summed,
            )
        picked.update({piece: line.passed[piece] for piece in then})
        send(then)

    def send_back(slot, d):
        if d == 0:
            returned[slot, 0] = rows[slot, 0], None
        elif d == 1:
            returned[slot, 1] = lax.ppermute(rows[slot, 1], "owner", partners(owners, 1)), None
        else:
            pair = lax.ppermute(rows[slot, d + 1], "owner", partners(owners, d))
            returned[slot, d] = pair, 0
            returned[slot, d + 1] = lax.ppermute(pair, "owner", partners(owners, 1)), 1

    def across_near(x, e1):
        return lax.ppermute(x, "fsdp", partners(group, e1))

    def across_far(x, e2):
        return lax.ppermute(x, "fsdp", partners(group, e2 * near))

    def first_sum(slot):
        received = [across_near(sums[slot][e1], e1) for e1 in range(1, near)]
        lines[slot] = add_near(line, sums[slot], received)

    def second_sum(slot):
        parts = lines[slot]
        received = [across_far(parts[e2], e2) for e2 in range(1, shares[1])]
        mine[slot] = add_far(line, [parts[0], *received])

    def collect(slot):
        part = mine[slot]
        whole_lines[slot] = stack(line, [part] + [across_far(part, e2) for e2 in range(1, shares[1])])

    def send_line(slot):
        whole_line = whole_lines[slot]
        gathered[slot] = [whole_line] + [across_near(whole_line, e1) for e1 in range(1, near)]

    def make_polynomial(slot):
        polys[slot, 0] = polynomial(line, gathered[slot])
        for d in far_steps[::2]:
            polys[slot, d] = lax.ppermute(polys[slot, 0], "owner", partners(owners, d))
        for d in near_steps:
            polys[slot, d] = lax.ppermute(polys[slot, 0], "owner", partners(owners, d))

    def pass_polynomials(slot):
        for d in far_steps[::2]:
            polys[slot, d] = step(line, polys[slot, d])
            polys[slot, d + 1] = lax.ppermute(polys[slot, d], "owner", partners(owners, 1))

    updates = None

    def finish_steps(slot, steps):
        nonlocal updates
        updates = finish(
            line,
            held_slots,
            slot,
            steps,
            [returned[slot, d] for d in steps],
            [polys[slot, d] for d in steps],
            gradients.shape,
            updates,
        )

    def expect(*wanted):
        line.due += [returned[slot, d][0] for slot, d in wanted if d < owners]

    far_pieces = [(slot, d) for slot in all_slots for d in far_steps]
    near_pieces = [(slot, d) for slot in all_slots for d in near_steps]
    send(far_pieces[:2] + near_pieces[:1])
    blend_piece(0, 0, far_pieces[2:] + near_pieces[1:])
    blend_piece(1, 0)
    for slot in all_slots:
        send_back(slot, 0)
    for d in near_steps:
        for slot in all_slots:
            blend_piece(slot, d)
            send_back(slot, d)
    for d in far_steps[:-1]:
        blend_piece(0, d)
    fetched[0] = fetch(line, momentum, 0, owners - 1, matrix_count, gradients.shape[1])
    expect((0, 1))
    for d in far_steps[-1:]:
        blend_piece(0, d)
    fetched[1] = fetch(line, momentum, 1, owners - 1, matrix_count, gradients.shape[1])
    expect((1, 1))
    first_sum(0)
    for d in far_steps[1::2]:
        line.waiting[d] = rows[0, d]
    for d in far_steps[:-1]:
        blend_piece(1, d)
    for d in far_steps[1::2]:
        rows[0, d] = line.passed[d]
        send_back(0, d - 1)
    for d in far_steps[-1:]:
        blend_piece(1, d)
    line.waiting["sum"] = sums[1]
    second_sum(0)
    sums[1] = line.passed["sum"]
    first_sum(1)
    for d in far_steps[1::2]:
        line.waiting[d] = rows[1, d]
    collect(0)
    for d in far_steps[1::2]:
        rows[1, d] = line.passed[d]
        send_back(1, d - 1)
    expect(*[(0, d) for d in far_steps[::2]])
    line.waiting["line"] = whole_lines[0]
    second_sum(1)
    whole_lines[0] = line.passed["line"]
    send_line(0)
    collect(1)
    send_line(1)
    make_polynomial(0)
    expect(*[(1, d) for d in far_steps[::2]])
    make_polynomial(1)
    finish_steps(0, [0] + near_steps)
    pass_polynomials(0)
    finish_steps(1, [0] + near_steps)
    pass_polynomials(1)
    finish_steps(0, far_steps)
    for k in range(0, len(far_steps), 2):
        finish_steps(1, far_steps[k : k + 2])
    return (updates, renewed)


def solution(mesh):
    return jax.shard_map(
        functools.partial(on_device, owners=mesh.shape["owner"], group=mesh.shape["fsdp"]),
        mesh=mesh,
        in_specs=(P(None, ("fsdp", "owner"), None), P("owner", "fsdp", None), P()),
        out_specs=(P(None, ("fsdp", "owner"), None), P("owner", "fsdp", None)),
        check_vma=False,
    )
```

```python
import functools
import math

import jax
import jax.numpy as jnp
from jax import lax
from jax.experimental import pallas as pl
from jax.experimental.pallas import tpu as pltpu
from jax.sharding import PartitionSpec as P

LONG = 16384
RANK = 512
ITERS = 5
TILE = 128

quintic = (3.4445, -4.775, 2.0315)
momentum_decay = 0.95
epsilon = 1e-07

SIDES = RANK // TILE
ABOVE = [(i, j) for i in range(SIDES) for j in range(i + 1, SIDES)]
TWOS = [(i, i + 1) for i in range(0, SIDES, 2)]
DIAGONALS = (len(ABOVE) + len(TWOS)) * TILE
POLY_ROWS = DIAGONALS + 16

f32, bf16 = jnp.float32, jnp.bfloat16


def in_hbm(x):
    return pltpu.with_memory_space_constraint(x, pltpu.HBM)


def matrix_of(place, count, slots, slot, d):
    wanted = slots * jnp.bitwise_xor(place[count], d) + slot
    found = jnp.int32(0)
    for m in range(1, count):
        found = found + jnp.where(place[m] == wanted, m, 0)
    return found


def group_index(place):
    return place[place.shape[0] - 1]


def packed_rows(group):
    return -(-(DIAGONALS + 8) // (8 * group)) * (8 * group)


def block_ids():
    return (
        lax.broadcasted_iota(jnp.int32, (TILE, TILE), 0),
        lax.broadcasted_iota(jnp.int32, (TILE, TILE), 1),
    )


def diagonal_of(block):
    row, column = block_ids()
    return jnp.sum(jnp.where(row == column, block, 0.0), axis=0, keepdims=True)


def pack(block):
    row, column = block_ids()
    blocks = [block(i, j) for i, j in ABOVE]
    blocks += [jnp.where(row <= column, block(i, i), block(j, j)) for i, j in TWOS]
    return blocks, [diagonal_of(block(j, j)) for _, j in TWOS]


def unpack(blocks, diagonals):
    row, column = block_ids()
    parts = dict(zip(ABOVE, blocks))
    for (i, j), both, diagonal in zip(TWOS, blocks[len(ABOVE) :], diagonals):
        turned = both.T
        parts[i, i] = jnp.where(row <= column, both, turned)
        parts[j, j] = jnp.where(row > column, both, jnp.where(row < column, turned, diagonal))
    return parts


def partners(size, step):
    return [(i, i ^ step) for i in range(size)]


def blend_kernel(buffers, has_sum, *refs):
    refs = list(refs)
    place = refs.pop(0)
    gradient, momentum = refs.pop(0), refs.pop(0)
    del refs[:buffers]
    before = refs.pop(0) if has_sum else None
    renewed, rows, total, held = refs
    step = pl.program_id(0)

    @pl.when(step == 0)
    def _():
        held[...] = before[...] if has_sum else jnp.zeros_like(held)

    g = gradient[...].astype(f32)
    m = momentum_decay * momentum[...] + g
    renewed[...] = m
    x = (g + momentum_decay * m).astype(bf16)
    rows[...] = x
    add_gram(held, x)

    @pl.when(step == pl.num_programs(0) - 1)
    def _():
        total[...] = held[...]


def add_gram(held, x):
    half, dims = RANK // 2, (((0,), (0,)), ((), ()))
    upper = lax.dot_general(x[:, :half], x, dims, preferred_element_type=f32)
    lower = lax.dot_general(x[:, half:], x[:, half:], dims, preferred_element_type=f32)

    def block(i, j):
        part, i0, j0 = (upper, i, j) if i < SIDES // 2 else (lower, i - SIDES // 2, j - SIDES // 2)
        return part[i0 * TILE : (i0 + 1) * TILE, j0 * TILE : (j0 + 1) * TILE]

    blocks, diagonals = pack(block)
    for n, part in enumerate(blocks):
        held[n * TILE : (n + 1) * TILE, :] += part
    for n, part in enumerate(diagonals):
        held[DIAGONALS + n : DIAGONALS + n + 1, :] += part


def fetch_kernel(slot, d, count, place, momentum, target, sem):
    rows = target.shape[0]
    start = pl.multiple_of(jnp.bitwise_xor(place[count], d) * rows, 8)
    copy = pltpu.make_async_copy(momentum.at[slot, pl.ds(start, rows)], target, sem)
    copy.start()
    copy.wait()


def fetch(line, momentum, slot, d, count, piece_rows):
    return line.run(
        functools.partial(fetch_kernel, slot, d, count),
        [in_hbm(momentum)],
        [IN_HBM],
        [jax.ShapeDtypeStruct((piece_rows, RANK), f32)],
        [IN_VMEM],
        name="fetch",
        scratch=[pltpu.SemaphoreType.DMA],
        work=(0, 8 * piece_rows * RANK),
    )[0]


def blend_last_kernel(slot, d, count, place, gradient, momentum, _buffer, _pair, before, renewed, pair, total, held, new, sems):
    rows = gradient.shape[0]
    tile = min(256, rows)
    first = jnp.bitwise_xor(place[count], d) * rows
    copies = []
    for n in range(rows // tile):
        part = pl.ds(n * tile, tile)
        g = gradient[part].astype(f32)
        m = momentum_decay * momentum[part] + g
        new[part] = m
        target = renewed.at[slot, pl.ds(pl.multiple_of(first + n * tile, 8), tile)]
        copies.append(pltpu.make_async_copy(new.at[part], target, sems.at[n]))
        copies[-1].start()
        pair[1, part] = (g + momentum_decay * m).astype(bf16)
    held[...] = before[...]
    add_gram(held, pair[1])
    near, far, size, _ = total.shape
    for e1 in range(near):
        for e2 in range(far):
            who = jnp.bitwise_xor(group_index(place), e2 * near + e1)
            total[e1, e2] = held[pl.ds(pl.multiple_of(who * size, 8), size), :]
    for copy in copies:
        copy.wait()


def blend_last(line, gradient, momentum, slot, d, count, buffer, pair, before, shares):
    piece_rows = gradient.shape[0]
    total = (*shares, before.shape[0] // (shares[0] * shares[1]), TILE)
    return line.run(
        functools.partial(blend_last_kernel, slot, d, count),
        [gradient, momentum, in_hbm(buffer), pair, before],
        [IN_VMEM, IN_VMEM, IN_HBM, IN_VMEM, IN_VMEM],
        [
            pltpu.HBM(buffer.shape, f32),
            jax.ShapeDtypeStruct(pair.shape, bf16),
            jax.ShapeDtypeStruct(total, f32),
        ],
        [IN_HBM, IN_VMEM, IN_VMEM],
        name="blend_last",
        token=2,
        scratch=[
            pltpu.VMEM(before.shape, f32),
            pltpu.VMEM((piece_rows, RANK), f32),
            pltpu.SemaphoreType.DMA((piece_rows // min(256, piece_rows),)),
        ],
        aliases={2: 0, 3: 1},
        vmem=12,
        work=(2 * piece_rows * RANK * RANK, piece_rows * RANK * 12),
    )


class Line:
    def __init__(self, place):
        self.place, self.last, self.due, self.waiting, self.passed = place, None, [], {}, {}

    def run(
        self,
        kernel,
        operands,
        specs,
        out_shape,
        out_specs,
        *,
        name,
        work,
        token=0,
        grid=(1,),
        scratch=(),
        aliases=None,
        vmem=8,
        scalars=True,
    ):
        before = [] if self.last is None or (token is None and out_shape) else [self.last]
        before += self.due
        keys = list(self.waiting)
        before += [self.waiting[key] for key in keys]
        skip, given, results = len(before), len(before) + len(operands), len(out_shape)
        lead = 1 if scalars else 0
        aliases = {lead + skip + i: o for i, o in (aliases or {}).items()}
        for k in range(len(keys)):
            aliases[lead + skip - len(keys) + k] = results + k

        def body(*refs):
            refs, place = refs[lead:], refs[:lead]
            kernel(*place, *refs[skip : given + results], *refs[given + results + len(keys) :])

        any_spec = pl.BlockSpec(memory_space=pl.ANY)
        flops, moved = work
        in_specs = [any_spec] * skip + specs
        out_specs = out_specs + [any_spec] * len(keys)
        if scalars:
            layout = {
                "grid_spec": pltpu.PrefetchScalarGridSpec(
                    num_scalar_prefetch=1,
                    grid=grid,
                    in_specs=in_specs,
                    out_specs=out_specs,
                    scratch_shapes=list(scratch),
                )
            }
        else:
            layout = {"in_specs": in_specs, "out_specs": out_specs, "scratch_shapes": list(scratch)}
        outs = pl.pallas_call(
            body,
            **layout,
            out_shape=out_shape
            + [jax.ShapeDtypeStruct(self.waiting[key].shape, self.waiting[key].dtype) for key in keys],
            input_output_aliases=aliases,
            compiler_params=pltpu.CompilerParams(vmem_limit_bytes=vmem * 2**20),
            cost_estimate=pl.CostEstimate(flops=20 * flops, bytes_accessed=20 * moved, transcendentals=0),
            name=name,
        )(*([self.place] if scalars else []), *before, *operands)
        if token is not None:
            self.last = outs[token]
        elif not out_shape:
            self.last = outs[0]
        self.due, self.waiting = [], {}
        self.passed.update(zip(keys, outs[results:]))
        return outs[:results]


IN_VMEM = pl.BlockSpec(memory_space=pltpu.VMEM)
IN_HBM = pl.BlockSpec(memory_space=pltpu.HBM)


def pick_kernel(slots, count, wanted, place, gradients, *refs):
    targets, sems = refs[:-1], refs[-1]
    copies = []
    for n, (slot, d) in enumerate(wanted):
        source = gradients.at[matrix_of(place, count, slots, slot, d)]
        copies.append(pltpu.make_async_copy(source, targets[n], sems.at[n]))
        copies[-1].start()
    for copy in copies:
        copy.wait()


def pick(line, gradients, slots, wanted):
    count, rows, _ = gradients.shape
    return line.run(
        functools.partial(pick_kernel, slots, count, wanted),
        [in_hbm(gradients)],
        [IN_HBM],
        [jax.ShapeDtypeStruct((rows, RANK), bf16) for _ in wanted],
        [IN_VMEM for _ in wanted],
        name="pick",
        scratch=[pltpu.SemaphoreType.DMA((len(wanted),))],
        work=(0, 4 * len(wanted) * rows * RANK),
    )


def blend(line, gradient, momentum, slot, d, count, buffer, pair, before, summed):
    slots = momentum.shape[0]
    piece_rows = gradient.shape[-2]
    tile = min(256, piece_rows)
    steps = piece_rows // tile
    if d == 0:
        gradient_spec = pl.BlockSpec(
            (None, tile, RANK), lambda i, p: (matrix_of(p, count, slots, slot, 0), i, 0)
        )
        gradient = in_hbm(gradient)
    else:
        gradient_spec = pl.BlockSpec((tile, RANK), lambda i, p: (i, 0))
    momentum_spec = pl.BlockSpec(
        (None, tile, RANK), lambda i, p: (slot, jnp.bitwise_xor(p[count], d) * steps + i, 0)
    )
    in_specs, operands = [gradient_spec, momentum_spec], [gradient, in_hbm(momentum)]
    aliases = {}
    for result, array in enumerate((buffer, pair)):
        if array is not None:
            aliases[len(operands)] = result
            in_specs.append(IN_HBM if result == 0 else pl.BlockSpec(memory_space=pl.ANY))
            operands.append(in_hbm(array) if result == 0 else array)
    if d < 2:
        rows_shape, rows_spec = (piece_rows, RANK), pl.BlockSpec((tile, RANK), lambda i, p: (i, 0))
    else:
        rows_shape = (2, piece_rows, RANK)
        rows_spec = pl.BlockSpec((None, tile, RANK), lambda i, p: (d % 2, i, 0))
    total = (summed, TILE)
    if before is not None:
        in_specs.append(pl.BlockSpec(total, lambda i, p: (0, 0)))
        operands.append(before)
    return line.run(
        functools.partial(blend_kernel, len(aliases), before is not None),
        operands,
        in_specs,
        [
            pltpu.HBM(momentum.shape, f32),
            jax.ShapeDtypeStruct(rows_shape, bf16),
            jax.ShapeDtypeStruct(total, f32),
        ],
        [
            momentum_spec,
            rows_spec,
            pl.BlockSpec(total, lambda i, p: (0, 0)),
        ],
        name="blend",
        token=2,
        grid=(steps,),
        scratch=[pltpu.VMEM(total, f32)],
        aliases=aliases,
        vmem=12,
        work=(2 * piece_rows * RANK * RANK, piece_rows * RANK * 12),
    )


def add_near_kernel(share, *refs):
    far = share.shape[1]
    received, targets = refs[: len(refs) - far], refs[len(refs) - far :]
    for e2, target in enumerate(targets):
        total = share[0, e2]
        for other in received:
            total = total + other[e2]
        target[...] = total


def add_near(line, share, received):
    _, far, count, _ = share.shape
    return line.run(
        add_near_kernel,
        [share, *received],
        [IN_VMEM] * (1 + len(received)),
        [jax.ShapeDtypeStruct((count, TILE), f32)] * far,
        [IN_VMEM] * far,
        name="add_near",
        scalars=False,
        work=(0, 12 * far * count * TILE),
    )


def add_far_kernel(*refs):
    total = refs[0][...]
    for other in refs[1:-1]:
        total = total + other[...]
    refs[-1][...] = total


def add_far(line, parts):
    return line.run(
        add_far_kernel,
        list(parts),
        [IN_VMEM] * len(parts),
        [jax.ShapeDtypeStruct(parts[0].shape, f32)],
        [IN_VMEM],
        name="add_far",
        scalars=False,
        work=(0, 4 * (len(parts) + 1) * parts[0].size),
    )[0]


def step(line, array=None):
    if array is not None:
        line.waiting["step"] = array
    line.run(lambda: None, [], [], [], [], name="step", token=None, scalars=False, work=(0, 0))
    return line.passed.get("step")


def stack_kernel(*refs):
    for e, part in enumerate(refs[:-1]):
        refs[-1][e] = part[...]


def stack(line, parts):
    return line.run(
        stack_kernel,
        list(parts),
        [IN_VMEM] * len(parts),
        [jax.ShapeDtypeStruct((len(parts), *parts[0].shape), f32)],
        [IN_VMEM],
        name="stack",
        scalars=False,
        work=(0, 8 * len(parts) * parts[0].size),
    )[0]


SHIFTS = (0.0, 0.0, 0.1, 0.6, 0.85)
FINE_TURN, FINE_POLY = 2, 3
HALF = RANK // 2


def dot(a, b):
    return jnp.dot(a, b, preferred_element_type=f32)


def whole(x):
    top, corner = x
    return jnp.concatenate([top, jnp.concatenate([top[:, HALF:].T, corner], axis=1)], axis=0)


def operand(x, passes):
    high = tuple(part.astype(bf16) for part in x)
    if passes == 1:
        return (whole(high),)
    low = tuple((part - rounded.astype(f32)).astype(bf16) for part, rounded in zip(x, high))
    return (whole(high), whole(low))


def product(a, b):
    top, corner = dot(a[0][:HALF], b[0]), dot(a[0][HALF:], b[0][:, HALF:])
    if len(a) > 1:
        top += dot(a[0][:HALF], b[1]) + dot(a[1][:HALF], b[0])
        corner += dot(a[0][HALF:], b[1][:, HALF:]) + dot(a[1][HALF:], b[0][:, HALF:])
    return (top, corner)


def combine(*terms):
    return tuple(
        functools.reduce(lambda x, y: x + y, [w * x[part] for w, x in terms]) for part in range(2)
    )


def add_identity(x, value):
    top, corner = x
    row = lax.broadcasted_iota(jnp.int32, (HALF, HALF), 0)
    column = lax.broadcasted_iota(jnp.int32, (HALF, HALF), 1)
    eye = jnp.where(row == column, value, 0.0)
    return (jnp.concatenate([top[:, :HALF] + eye, top[:, HALF:]], axis=1), corner + eye)


def polynomial_kernel(near, far, count, place, *refs):
    *shared, result, packed = refs
    for e1, other in enumerate(shared):
        for e2 in range(far):
            who = jnp.bitwise_xor(group_index(place), e2 * near + e1)
            packed[pl.ds(pl.multiple_of(who * count, 8), count), :] = other[e2]
    blocks = [packed[n * TILE : (n + 1) * TILE, :] for n in range(len(ABOVE) + len(TWOS))]
    diagonals = [packed[DIAGONALS + n : DIAGONALS + n + 1, :] for n in range(len(TWOS))]
    parts = unpack(blocks, diagonals)
    trace = jnp.sum(sum(diagonals) + sum(diagonal_of(both) for both in blocks[len(ABOVE) :]))
    for i, j in ((0, 1), (2, 3)):
        parts[j, i] = parts[i, j].T

    def rows_of(count, first):
        return jnp.concatenate(
            [
                jnp.concatenate([parts[i, j] for j in range(first, SIDES)], axis=1)
                for i in range(first, first + count)
            ],
            axis=0,
        )

    half = HALF // TILE
    scale = 1.0 / (jnp.sqrt(jnp.full((1, 1), trace, f32)) + epsilon)
    rest = tuple((x * scale) * scale for x in (rows_of(half, 0), rows_of(half, half)))
    a, b, c = quintic
    poly = None
    for k in range(ITERS):
        shift = SHIFTS[k]
        gain = a + b * shift + c * shift * shift
        d = operand(rest, 3 if k == FINE_TURN else 1)
        step = combine((b + 2 * c * shift, rest), (c, product(d[:1], d[:1])))
        s = operand(step, 3 if k in (FINE_TURN, FINE_POLY) else 1)
        if poly is None:
            poly = add_identity(step, gain)
        else:
            p = operand(poly, 3 if k == FINE_POLY else 1)
            poly = combine((gain, poly), (1.0, product(p, s)))
        if k < ITERS - 1:
            middle = combine((gain, rest), (shift, step), (1.0, product(d, s)))
            turned = product(operand(middle, 1), s)
            rest = combine((gain, middle), (gain * shift, step), (1.0, turned))
            rest = add_identity(rest, gain * gain * shift - SHIFTS[k + 1])
    top, corner = tuple(x * (scale * math.sqrt(max(LONG, RANK))) for x in poly)

    def block(i, j):
        part, i0, j0 = (top, i, j) if i < half else (corner, i - half, j - half)
        return part[i0 * TILE : (i0 + 1) * TILE, j0 * TILE : (j0 + 1) * TILE]

    blocks, seconds = pack(block)
    for n, part in enumerate(blocks):
        result[n * TILE : (n + 1) * TILE, :] = part.astype(bf16)
    lows = []
    for i in range(SIDES):
        diagonal = diagonal_of(block(i, i))
        lows.append(diagonal - diagonal.astype(bf16).astype(f32))
    rows = lows + seconds
    rows.append(jnp.zeros((POLY_ROWS - DIAGONALS - len(rows), TILE), f32))
    result[DIAGONALS:, :] = jnp.concatenate(rows, axis=0).astype(bf16)


def polynomial(line, shared):
    near, (far, count, _) = len(shared), shared[0].shape
    return line.run(
        functools.partial(polynomial_kernel, near, far, count),
        list(shared),
        [IN_VMEM] * near,
        [jax.ShapeDtypeStruct((POLY_ROWS, TILE), bf16)],
        [IN_VMEM],
        name="polynomial",
        scratch=[pltpu.VMEM((near * far * count, TILE), f32)],
        vmem=20,
        work=(RANK**3, 2**16),
    )[0]


def finish_kernel(slots, slot, steps, matrices, picks, place, *refs):
    refs = list(refs)
    count = len(steps)
    pieces, polys = refs[:count], refs[count : 2 * count]
    updates, _, held, sems = refs[-4:]
    copies = []
    for n, d in enumerate(steps):
        tail = polys[n][DIAGONALS:, :].astype(f32)
        blocks = [polys[n][k * TILE : (k + 1) * TILE, :] for k in range(len(ABOVE) + len(TWOS))]
        twos = [part.astype(f32) for part in blocks[len(ABOVE) :]]
        seconds = [tail[SIDES + k : SIDES + k + 1] for k in range(len(TWOS))]
        parts = unpack(blocks[: len(ABOVE)] + twos, seconds)
        for i in range(SIDES):
            parts[i, i] = parts[i, i].astype(bf16)
        for i, j in ABOVE:
            parts[j, i] = parts[i, j].T
        sides = range(SIDES)
        poly = jnp.concatenate(
            [jnp.concatenate([parts[i, j] for j in sides], axis=1) for i in sides], axis=0
        )
        low = jnp.concatenate([tail[i : i + 1] for i in sides], axis=1)
        rows = held.shape[1]
        tile = min(256, rows)
        target = updates.at[matrix_of(place, matrices, slots, slot, d)]
        for k in range(rows // tile):
            part = pl.ds(k * tile, tile)
            x = pieces[n][part] if picks[n] is None else pieces[n][picks[n], part]
            held[n, part] = (dot(x, poly) + x.astype(f32) * low).astype(bf16)
            copies.append(pltpu.make_async_copy(held.at[n, part], target.at[part], sems.at[len(copies)]))
            copies[-1].start()
    for copy in copies:
        copy.wait()


def finish(line, slots, slot, steps, pieces, polys, shape, buffer):
    operands = [piece for piece, _ in pieces] + list(polys)
    specs = [IN_VMEM] * len(operands)
    aliases = {}
    if buffer is not None:
        aliases = {len(operands): 0}
        operands.append(in_hbm(buffer))
        specs.append(IN_HBM)
    return line.run(
        functools.partial(finish_kernel, slots, slot, steps, shape[0], [index for _, index in pieces]),
        operands,
        specs,
        [pltpu.HBM(shape, bf16), jax.ShapeDtypeStruct((8, TILE), f32)],
        [IN_HBM, IN_VMEM],
        name="finish",
        token=1,
        scratch=[pltpu.VMEM((len(steps), shape[1], RANK), bf16), pltpu.SemaphoreType.DMA((len(steps) * max(1, shape[1] // 256),))],
        aliases=aliases,
        vmem=12,
        work=(2 * len(steps) * shape[1] * RANK * RANK, 4 * len(steps) * shape[1] * RANK),
    )[0]


def on_device(gradients, momentum, slot_table, *, owners, group):
    matrix_count = gradients.shape[0]
    held_slots = momentum.shape[0]
    near = 1 << ((group.bit_length() - 1) // 2)
    shares = (near, group // near)
    place = jnp.concatenate(
        [
            slot_table.astype(jnp.int32),
            jnp.stack([lax.axis_index("owner"), lax.axis_index("fsdp")]).astype(jnp.int32),
        ]
    )

    line = Line(place)
    all_slots = range(held_slots)
    far_steps, near_steps = list(range(2, owners)), list(range(1, min(2, owners)))
    arrived = {}
    wanted = [(0, d) for d in far_steps] + [(slot, d) for slot in all_slots for d in near_steps]
    wanted += [(slot, d) for slot in range(1, held_slots) for d in far_steps]
    picked = {}
    for few in (wanted[:1], wanted[1:]):
        picked.update(zip(few, pick(line, gradients, held_slots, few)))

    def send(pieces):
        for slot, d in pieces:
            arrived[slot, d] = lax.ppermute(picked[slot, d], "owner", partners(owners, d))

    fetched = {}
    renewed, rows, returned, sums, lines, mine, whole_lines, gathered, polys = None, {}, {}, {}, {}, {}, {}, {}, {}

    summed = packed_rows(group)

    def blend_piece(slot, d, then=()):
        nonlocal renewed
        line.waiting.update({piece: picked[piece] for piece in then})
        gradient = arrived[slot, d] if d else gradients
        if d == owners - 1:
            renewed, rows[slot, d], sums[slot] = blend_last(
                line, gradient, fetched[slot], slot, d, matrix_count, renewed, rows[slot, d - 1], sums[slot], shares
            )
        else:
            renewed, rows[slot, d], sums[slot] = blend(
                line,
                gradient,
                momentum,
                slot,
                d,
                matrix_count,
                renewed,
                rows[slot, d - 1] if d > 1 and d % 2 else None,
                sums.get(slot),
                summed,
            )
        picked.update({piece: line.passed[piece] for piece in then})
        send(then)

    def send_back(slot, d):
        if d == 0:
            returned[slot, 0] = rows[slot, 0], None
        elif d == 1:
            returned[slot, 1] = lax.ppermute(rows[slot, 1], "owner", partners(owners, 1)), None
        else:
            pair = lax.ppermute(rows[slot, d + 1], "owner", partners(owners, d))
            returned[slot, d] = pair, 0

    def across_near(x, e1):
        return lax.ppermute(x, "fsdp", partners(group, e1))

    def across_far(x, e2):
        return lax.ppermute(x, "fsdp", partners(group, e2 * near))

    def first_sum(slot):
        received = [across_near(sums[slot][e1], e1) for e1 in range(1, near)]
        lines[slot] = add_near(line, sums[slot], received)

    def second_sum(slot):
        parts = lines[slot]
        received = [across_far(parts[e2], e2) for e2 in range(1, shares[1])]
        mine[slot] = add_far(line, [parts[0], *received])

    def collect(slot):
        part = mine[slot]
        whole_lines[slot] = stack(line, [part] + [across_far(part, e2) for e2 in range(1, shares[1])])

    def send_line(slot):
        whole_line = whole_lines[slot]
        gathered[slot] = [whole_line] + [across_near(whole_line, e1) for e1 in range(1, near)]

    def make_polynomial(slot):
        polys[slot, 0] = polynomial(line, gathered[slot])
        for d in far_steps[::2]:
            polys[slot, d] = lax.ppermute(polys[slot, 0], "owner", partners(owners, d))
        for d in near_steps:
            polys[slot, d] = lax.ppermute(polys[slot, 0], "owner", partners(owners, d))

    def pass_polynomials(slot):
        for d in far_steps[::2]:
            polys[slot, d] = step(line, polys[slot, d])
            polys[slot, d + 1] = lax.ppermute(polys[slot, d], "owner", partners(owners, 1))

    updates = None

    def finish_steps(slot, steps):
        nonlocal updates
        updates = finish(
            line,
            held_slots,
            slot,
            steps,
            [returned[slot, d] for d in steps],
            [polys[slot, d] for d in steps],
            gradients.shape,
            updates,
        )

    def expect(*wanted):
        line.due += [returned[slot, d][0] for slot, d in wanted if d < owners]

    far_pieces = [(slot, d) for slot in all_slots for d in far_steps]
    near_pieces = [(slot, d) for slot in all_slots for d in near_steps]
    send(far_pieces[:2] + near_pieces[:1])
    blend_piece(0, 0, far_pieces[2:] + near_pieces[1:])
    blend_piece(1, 0)
    for slot in all_slots:
        send_back(slot, 0)
    for d in near_steps:
        for slot in all_slots:
            blend_piece(slot, d)
            send_back(slot, d)
    for d in far_steps[:-1]:
        blend_piece(0, d)
    fetched[0] = fetch(line, momentum, 0, owners - 1, matrix_count, gradients.shape[1])
    expect((0, 1))
    for d in far_steps[-1:]:
        blend_piece(0, d)
    fetched[1] = fetch(line, momentum, 1, owners - 1, matrix_count, gradients.shape[1])
    expect((1, 1))
    first_sum(0)
    for d in far_steps[1::2]:
        line.waiting[d] = rows[0, d]
    for d in far_steps[:-1]:
        blend_piece(1, d)
    for d in far_steps[1::2]:
        rows[0, d] = line.passed[d]
        send_back(0, d - 1)
    for d in far_steps[-1:]:
        blend_piece(1, d)
    line.waiting["sum"] = sums[1]
    second_sum(0)
    sums[1] = line.passed["sum"]
    first_sum(1)
    for d in far_steps[1::2]:
        line.waiting[d] = rows[1, d]
    collect(0)
    for d in far_steps[1::2]:
        rows[1, d] = line.passed[d]
        send_back(1, d - 1)
    expect(*[(0, d) for d in far_steps[::2]])
    line.waiting["line"] = whole_lines[0]
    second_sum(1)
    whole_lines[0] = line.passed["line"]
    send_line(0)
    collect(1)
    send_line(1)
    make_polynomial(0)
    make_polynomial(1)
    for slot in all_slots:
        for d in far_steps[::2]:
            line.waiting[slot, d] = returned[slot, d][0]
    step(line)
    for slot in all_slots:
        for d in far_steps[::2]:
            pair = line.passed[slot, d]
            returned[slot, d] = pair, 0
            returned[slot, d + 1] = lax.ppermute(pair, "owner", partners(owners, 1)), 1
    finish_steps(0, [0] + near_steps)
    pass_polynomials(0)
    finish_steps(1, [0] + near_steps)
    pass_polynomials(1)
    finish_steps(0, far_steps)
    for k in range(0, len(far_steps), 2):
        finish_steps(1, far_steps[k : k + 2])
    return (updates, renewed)


def solution(mesh):
    return jax.shard_map(
        functools.partial(on_device, owners=mesh.shape["owner"], group=mesh.shape["fsdp"]),
        mesh=mesh,
        in_specs=(P(None, ("fsdp", "owner"), None), P("owner", "fsdp", None), P()),
        out_specs=(P(None, ("fsdp", "owner"), None), P("owner", "fsdp", None)),
        check_vma=False,
    )
```

```python
import functools
import math

import jax
import jax.numpy as jnp
from jax import lax
from jax.experimental import pallas as pl
from jax.experimental.pallas import tpu as pltpu
from jax.sharding import PartitionSpec as P

LONG = 16384
RANK = 512
ITERS = 5
TILE = 128

quintic = (3.4445, -4.775, 2.0315)
momentum_decay = 0.95
epsilon = 1e-07

SIDES = RANK // TILE
ABOVE = [(i, j) for i in range(SIDES) for j in range(i + 1, SIDES)]
TWOS = [(i, i + 1) for i in range(0, SIDES, 2)]
DIAGONALS = (len(ABOVE) + len(TWOS)) * TILE
POLY_ROWS = DIAGONALS + 16

f32, bf16 = jnp.float32, jnp.bfloat16


def in_hbm(x):
    return pltpu.with_memory_space_constraint(x, pltpu.HBM)


def matrix_of(place, count, slots, slot, d):
    wanted = slots * jnp.bitwise_xor(place[count], d) + slot
    found = jnp.int32(0)
    for m in range(1, count):
        found = found + jnp.where(place[m] == wanted, m, 0)
    return found


def group_index(place):
    return place[place.shape[0] - 1]


def packed_rows(group):
    return -(-(DIAGONALS + 8) // (8 * group)) * (8 * group)


def block_ids():
    return (
        lax.broadcasted_iota(jnp.int32, (TILE, TILE), 0),
        lax.broadcasted_iota(jnp.int32, (TILE, TILE), 1),
    )


def diagonal_of(block):
    row, column = block_ids()
    return jnp.sum(jnp.where(row == column, block, 0.0), axis=0, keepdims=True)


def pack(block):
    row, column = block_ids()
    blocks = [block(i, j) for i, j in ABOVE]
    blocks += [jnp.where(row <= column, block(i, i), block(j, j)) for i, j in TWOS]
    return blocks, [diagonal_of(block(j, j)) for _, j in TWOS]


def unpack(blocks, diagonals):
    row, column = block_ids()
    parts = dict(zip(ABOVE, blocks))
    for (i, j), both, diagonal in zip(TWOS, blocks[len(ABOVE) :], diagonals):
        turned = both.T
        parts[i, i] = jnp.where(row <= column, both, turned)
        parts[j, j] = jnp.where(row > column, both, jnp.where(row < column, turned, diagonal))
    return parts


def partners(size, step):
    return [(i, i ^ step) for i in range(size)]


def blend_kernel(buffers, has_sum, *refs):
    refs = list(refs)
    place = refs.pop(0)
    gradient, momentum = refs.pop(0), refs.pop(0)
    del refs[:buffers]
    before = refs.pop(0) if has_sum else None
    renewed, rows, total, held = refs
    step = pl.program_id(0)

    @pl.when(step == 0)
    def _():
        held[...] = before[...] if has_sum else jnp.zeros_like(held)

    g = gradient[...].astype(f32)
    m = momentum_decay * momentum[...] + g
    renewed[...] = m
    x = (g + momentum_decay * m).astype(bf16)
    rows[...] = x
    add_gram(held, x)

    @pl.when(step == pl.num_programs(0) - 1)
    def _():
        total[...] = held[...]


def add_gram(held, x):
    half, dims = RANK // 2, (((0,), (0,)), ((), ()))
    upper = lax.dot_general(x[:, :half], x, dims, preferred_element_type=f32)
    lower = lax.dot_general(x[:, half:], x[:, half:], dims, preferred_element_type=f32)

    def block(i, j):
        part, i0, j0 = (upper, i, j) if i < SIDES // 2 else (lower, i - SIDES // 2, j - SIDES // 2)
        return part[i0 * TILE : (i0 + 1) * TILE, j0 * TILE : (j0 + 1) * TILE]

    blocks, diagonals = pack(block)
    for n, part in enumerate(blocks):
        held[n * TILE : (n + 1) * TILE, :] += part
    for n, part in enumerate(diagonals):
        held[DIAGONALS + n : DIAGONALS + n + 1, :] += part


def fetch_kernel(slot, d, count, place, momentum, target, sem):
    rows = target.shape[0]
    start = pl.multiple_of(jnp.bitwise_xor(place[count], d) * rows, 8)
    copy = pltpu.make_async_copy(momentum.at[slot, pl.ds(start, rows)], target, sem)
    copy.start()
    copy.wait()


def fetch(line, momentum, slot, d, count, piece_rows):
    return line.run(
        functools.partial(fetch_kernel, slot, d, count),
        [in_hbm(momentum)],
        [IN_HBM],
        [jax.ShapeDtypeStruct((piece_rows, RANK), f32)],
        [IN_VMEM],
        name="fetch",
        scratch=[pltpu.SemaphoreType.DMA],
        work=(0, 8 * piece_rows * RANK),
    )[0]


def blend_last_kernel(slot, d, count, place, gradient, momentum, _buffer, _pair, before, renewed, pair, total, held, new, sems):
    rows = gradient.shape[0]
    tile = min(256, rows)
    first = jnp.bitwise_xor(place.owner(), d) * rows
    copies = []
    for n in range(rows // tile):
        part = pl.ds(n * tile, tile)
        g = gradient[part].astype(f32)
        m = momentum_decay * momentum[part] + g
        new[part] = m
        target = renewed.at[slot, pl.ds(pl.multiple_of(first + n * tile, 8), tile)]
        copies.append(pltpu.make_async_copy(new.at[part], target, sems.at[n]))
        copies[-1].start()
        pair[1, part] = (g + momentum_decay * m).astype(bf16)
    held[...] = before[...]
    add_gram(held, pair[1])
    near, far, size, _ = total.shape
    for e1 in range(near):
        for e2 in range(far):
            who = jnp.bitwise_xor(place.group(), e2 * near + e1)
            total[e1, e2] = held[pl.ds(pl.multiple_of(who * size, 8), size), :]
    for copy in copies:
        copy.wait()


def blend_last(line, gradient, momentum, slot, d, count, buffer, pair, before, shares):
    piece_rows = gradient.shape[0]
    total = (*shares, before.shape[0] // (shares[0] * shares[1]), TILE)
    return line.run(
        functools.partial(blend_last_kernel, slot, d, count),
        [gradient, momentum, in_hbm(buffer), pair, before],
        [IN_VMEM, IN_VMEM, IN_HBM, IN_VMEM, IN_VMEM],
        [
            pltpu.HBM(buffer.shape, f32),
            jax.ShapeDtypeStruct(pair.shape, bf16),
            jax.ShapeDtypeStruct(total, f32),
        ],
        [IN_HBM, IN_VMEM, IN_VMEM],
        name="blend_last",
        scalars=SPOTS,
        token=2,
        scratch=[
            pltpu.VMEM(before.shape, f32),
            pltpu.VMEM((piece_rows, RANK), f32),
            pltpu.SemaphoreType.DMA((piece_rows // min(256, piece_rows),)),
        ],
        aliases={2: 0, 3: 1},
        vmem=8,
        work=(2 * piece_rows * RANK * RANK, piece_rows * RANK * 12),
    )


SPOTS = "spots"


class Spots:
    def __init__(self, ref, owners):
        self.ref, self.owners = ref, owners

    def matrix(self, slot, d):
        return self.ref[slot * self.owners + d, 0]

    def owner(self):
        return self.ref[self.ref.shape[0] - 2, 0]

    def group(self):
        return self.ref[self.ref.shape[0] - 1, 0]


def make_spots(place, count, slots, owners):
    targets = slots * jnp.bitwise_xor(place[count], jnp.arange(owners))[None, :] + jnp.arange(slots)[:, None]
    found = place[None, :count] == targets.reshape(-1, 1)
    matrices = jnp.sum(jnp.where(found, jnp.arange(count)[None, :], 0), axis=1).astype(jnp.int32)
    free = -(matrices.shape[0] + 2) % 8
    column = jnp.concatenate([matrices, jnp.zeros((free,), jnp.int32), place[count:]])
    return jnp.broadcast_to(column[:, None], (column.shape[0], TILE))


class Line:
    def __init__(self, place):
        self.place, self.last, self.due, self.waiting, self.passed = place, None, [], {}, {}
        self.spots, self.owners = None, 0

    def run(
        self,
        kernel,
        operands,
        specs,
        out_shape,
        out_specs,
        *,
        name,
        work,
        token=0,
        grid=(1,),
        scratch=(),
        aliases=None,
        vmem=8,
        scalars=True,
    ):
        before = [] if self.last is None or (token is None and out_shape) else [self.last]
        before += self.due
        keys = list(self.waiting)
        before += [self.waiting[key] for key in keys]
        skip, given, results = len(before), len(before) + len(operands), len(out_shape)
        lead = 1 if scalars else 0
        prefetched = scalars is True
        spots = None if scalars is not SPOTS else self.spots
        aliases = {lead + skip + i: o for i, o in (aliases or {}).items()}
        for k in range(len(keys)):
            aliases[lead + skip - len(keys) + k] = results + k

        def body(*refs):
            refs, place = refs[lead:], refs[:lead]
            if spots is not None:
                place = (Spots(place[0], self.owners),)
            kernel(*place, *refs[skip : given + results], *refs[given + results + len(keys) :])

        any_spec = pl.BlockSpec(memory_space=pl.ANY)
        flops, moved = work
        in_specs = [any_spec] * skip + specs
        out_specs = out_specs + [any_spec] * len(keys)
        if prefetched:
            layout = {
                "grid_spec": pltpu.PrefetchScalarGridSpec(
                    num_scalar_prefetch=1,
                    grid=grid,
                    in_specs=in_specs,
                    out_specs=out_specs,
                    scratch_shapes=list(scratch),
                )
            }
        else:
            in_specs = [IN_VMEM] * lead + in_specs
            layout = {"in_specs": in_specs, "out_specs": out_specs, "scratch_shapes": list(scratch)}
        outs = pl.pallas_call(
            body,
            **layout,
            out_shape=out_shape
            + [jax.ShapeDtypeStruct(self.waiting[key].shape, self.waiting[key].dtype) for key in keys],
            input_output_aliases=aliases,
            compiler_params=pltpu.CompilerParams(vmem_limit_bytes=vmem * 2**20),
            cost_estimate=pl.CostEstimate(flops=20 * flops, bytes_accessed=20 * moved, transcendentals=0),
            name=name,
        )(*([self.place] if prefetched else [spots] * lead), *before, *operands)
        if token is not None:
            self.last = outs[token]
        elif not out_shape:
            self.last = outs[0]
        self.due, self.waiting = [], {}
        self.passed.update(zip(keys, outs[results:]))
        return outs[:results]


IN_VMEM = pl.BlockSpec(memory_space=pltpu.VMEM)
IN_HBM = pl.BlockSpec(memory_space=pltpu.HBM)


def pick_kernel(slots, count, wanted, place, gradients, *refs):
    targets, sems = refs[:-1], refs[-1]
    copies = []
    for n, (slot, d) in enumerate(wanted):
        source = gradients.at[matrix_of(place, count, slots, slot, d)]
        copies.append(pltpu.make_async_copy(source, targets[n], sems.at[n]))
        copies[-1].start()
    for copy in copies:
        copy.wait()


def pick(line, gradients, slots, wanted):
    count, rows, _ = gradients.shape
    return line.run(
        functools.partial(pick_kernel, slots, count, wanted),
        [in_hbm(gradients)],
        [IN_HBM],
        [jax.ShapeDtypeStruct((rows, RANK), bf16) for _ in wanted],
        [IN_VMEM for _ in wanted],
        name="pick",
        scratch=[pltpu.SemaphoreType.DMA((len(wanted),))],
        work=(0, 4 * len(wanted) * rows * RANK),
    )


def blend(line, gradient, momentum, slot, d, count, buffer, pair, before, summed):
    slots = momentum.shape[0]
    piece_rows = gradient.shape[-2]
    tile = min(256, piece_rows)
    steps = piece_rows // tile
    if d == 0:
        gradient_spec = pl.BlockSpec(
            (None, tile, RANK), lambda i, p: (matrix_of(p, count, slots, slot, 0), i, 0)
        )
        gradient = in_hbm(gradient)
    else:
        gradient_spec = pl.BlockSpec((tile, RANK), lambda i, p: (i, 0))
    momentum_spec = pl.BlockSpec(
        (None, tile, RANK), lambda i, p: (slot, jnp.bitwise_xor(p[count], d) * steps + i, 0)
    )
    in_specs, operands = [gradient_spec, momentum_spec], [gradient, in_hbm(momentum)]
    aliases = {}
    for result, array in enumerate((buffer, pair)):
        if array is not None:
            aliases[len(operands)] = result
            in_specs.append(IN_HBM if result == 0 else pl.BlockSpec(memory_space=pl.ANY))
            operands.append(in_hbm(array) if result == 0 else array)
    if d < 2:
        rows_shape, rows_spec = (piece_rows, RANK), pl.BlockSpec((tile, RANK), lambda i, p: (i, 0))
    else:
        rows_shape = (2, piece_rows, RANK)
        rows_spec = pl.BlockSpec((None, tile, RANK), lambda i, p: (d % 2, i, 0))
    total = (summed, TILE)
    if before is not None:
        in_specs.append(pl.BlockSpec(total, lambda i, p: (0, 0)))
        operands.append(before)
    return line.run(
        functools.partial(blend_kernel, len(aliases), before is not None),
        operands,
        in_specs,
        [
            pltpu.HBM(momentum.shape, f32),
            jax.ShapeDtypeStruct(rows_shape, bf16),
            jax.ShapeDtypeStruct(total, f32),
        ],
        [
            momentum_spec,
            rows_spec,
            pl.BlockSpec(total, lambda i, p: (0, 0)),
        ],
        name="blend",
        token=2,
        grid=(steps,),
        scratch=[pltpu.VMEM(total, f32)],
        aliases=aliases,
        vmem=8,
        work=(2 * piece_rows * RANK * RANK, piece_rows * RANK * 12),
    )


def add_near_kernel(share, *refs):
    far = share.shape[1]
    received, targets = refs[: len(refs) - far], refs[len(refs) - far :]
    for e2, target in enumerate(targets):
        total = share[0, e2]
        for other in received:
            total = total + other[e2]
        target[...] = total


def add_near(line, share, received):
    _, far, count, _ = share.shape
    return line.run(
        add_near_kernel,
        [share, *received],
        [IN_VMEM] * (1 + len(received)),
        [jax.ShapeDtypeStruct((count, TILE), f32)] * far,
        [IN_VMEM] * far,
        name="add_near",
        scalars=False,
        work=(0, 12 * far * count * TILE),
    )


def add_far_kernel(*refs):
    total = refs[0][...]
    for other in refs[1:-1]:
        total = total + other[...]
    refs[-1][...] = total


def add_far(line, parts):
    return line.run(
        add_far_kernel,
        list(parts),
        [IN_VMEM] * len(parts),
        [jax.ShapeDtypeStruct(parts[0].shape, f32)],
        [IN_VMEM],
        name="add_far",
        scalars=False,
        work=(0, 4 * (len(parts) + 1) * parts[0].size),
    )[0]


def step(line, array=None):
    if array is not None:
        line.waiting["step"] = array
    line.run(lambda: None, [], [], [], [], name="step", token=None, scalars=False, work=(0, 0))
    return line.passed.get("step")


def stack_kernel(*refs):
    for e, part in enumerate(refs[:-1]):
        refs[-1][e] = part[...]


def stack(line, parts):
    return line.run(
        stack_kernel,
        list(parts),
        [IN_VMEM] * len(parts),
        [jax.ShapeDtypeStruct((len(parts), *parts[0].shape), f32)],
        [IN_VMEM],
        name="stack",
        scalars=False,
        work=(0, 8 * len(parts) * parts[0].size),
    )[0]


SHIFTS = (0.0, 0.0, 0.1, 0.6, 0.85)
FINE_TURN, FINE_POLY = 2, 3
HALF = RANK // 2


def dot(a, b):
    return jnp.dot(a, b, preferred_element_type=f32)


def whole(x):
    top, corner = x
    return jnp.concatenate([top, jnp.concatenate([top[:, HALF:].T, corner], axis=1)], axis=0)


def operand(x, passes):
    high = tuple(part.astype(bf16) for part in x)
    if passes == 1:
        return (whole(high),)
    low = tuple((part - rounded.astype(f32)).astype(bf16) for part, rounded in zip(x, high))
    return (whole(high), whole(low))


def product(a, b):
    top, corner = dot(a[0][:HALF], b[0]), dot(a[0][HALF:], b[0][:, HALF:])
    if len(a) > 1:
        top += dot(a[0][:HALF], b[1]) + dot(a[1][:HALF], b[0])
        corner += dot(a[0][HALF:], b[1][:, HALF:]) + dot(a[1][HALF:], b[0][:, HALF:])
    return (top, corner)


def combine(*terms):
    return tuple(
        functools.reduce(lambda x, y: x + y, [w * x[part] for w, x in terms]) for part in range(2)
    )


def add_identity(x, value):
    top, corner = x
    row = lax.broadcasted_iota(jnp.int32, (HALF, HALF), 0)
    column = lax.broadcasted_iota(jnp.int32, (HALF, HALF), 1)
    eye = jnp.where(row == column, value, 0.0)
    return (jnp.concatenate([top[:, :HALF] + eye, top[:, HALF:]], axis=1), corner + eye)


def polynomial_kernel(near, far, count, place, *refs):
    *shared, result, packed = refs
    for e1, other in enumerate(shared):
        for e2 in range(far):
            who = jnp.bitwise_xor(place.group(), e2 * near + e1)
            packed[pl.ds(pl.multiple_of(who * count, 8), count), :] = other[e2]
    blocks = [packed[n * TILE : (n + 1) * TILE, :] for n in range(len(ABOVE) + len(TWOS))]
    diagonals = [packed[DIAGONALS + n : DIAGONALS + n + 1, :] for n in range(len(TWOS))]
    parts = unpack(blocks, diagonals)
    trace = jnp.sum(sum(diagonals) + sum(diagonal_of(both) for both in blocks[len(ABOVE) :]))
    for i, j in ((0, 1), (2, 3)):
        parts[j, i] = parts[i, j].T

    def rows_of(count, first):
        return jnp.concatenate(
            [
                jnp.concatenate([parts[i, j] for j in range(first, SIDES)], axis=1)
                for i in range(first, first + count)
            ],
            axis=0,
        )

    half = HALF // TILE
    scale = 1.0 / (jnp.sqrt(jnp.full((1, 1), trace, f32)) + epsilon)
    rest = tuple((x * scale) * scale for x in (rows_of(half, 0), rows_of(half, half)))
    a, b, c = quintic
    poly = None
    for k in range(ITERS):
        shift = SHIFTS[k]
        gain = a + b * shift + c * shift * shift
        d = operand(rest, 3 if k == FINE_TURN else 1)
        step = combine((b + 2 * c * shift, rest), (c, product(d[:1], d[:1])))
        s = operand(step, 3 if k in (FINE_TURN, FINE_POLY) else 1)
        if poly is None:
            poly = add_identity(step, gain)
        else:
            p = operand(poly, 3 if k == FINE_POLY else 1)
            poly = combine((gain, poly), (1.0, product(p, s)))
        if k < ITERS - 1:
            middle = combine((gain, rest), (shift, step), (1.0, product(d, s)))
            turned = product(operand(middle, 1), s)
            rest = combine((gain, middle), (gain * shift, step), (1.0, turned))
            rest = add_identity(rest, gain * gain * shift - SHIFTS[k + 1])
    top, corner = tuple(x * (scale * math.sqrt(max(LONG, RANK))) for x in poly)

    def block(i, j):
        part, i0, j0 = (top, i, j) if i < half else (corner, i - half, j - half)
        return part[i0 * TILE : (i0 + 1) * TILE, j0 * TILE : (j0 + 1) * TILE]

    blocks, seconds = pack(block)
    for n, part in enumerate(blocks):
        result[n * TILE : (n + 1) * TILE, :] = part.astype(bf16)
    lows = []
    for i in range(SIDES):
        diagonal = diagonal_of(block(i, i))
        lows.append(diagonal - diagonal.astype(bf16).astype(f32))
    rows = lows + seconds
    rows.append(jnp.zeros((POLY_ROWS - DIAGONALS - len(rows), TILE), f32))
    result[DIAGONALS:, :] = jnp.concatenate(rows, axis=0).astype(bf16)


def polynomial(line, shared):
    near, (far, count, _) = len(shared), shared[0].shape
    return line.run(
        functools.partial(polynomial_kernel, near, far, count),
        list(shared),
        [IN_VMEM] * near,
        [jax.ShapeDtypeStruct((POLY_ROWS, TILE), bf16)],
        [IN_VMEM],
        name="polynomial",
        scalars=SPOTS,
        scratch=[pltpu.VMEM((near * far * count, TILE), f32)],
        vmem=12,
        work=(RANK**3, 2**16),
    )[0]


def finish_kernel(slots, slot, steps, matrices, picks, place, *refs):
    refs = list(refs)
    count = len(steps)
    pieces, polys = refs[:count], refs[count : 2 * count]
    updates, _, held, sems = refs[-4:]
    copies = []
    for n, d in enumerate(steps):
        tail = polys[n][DIAGONALS:, :].astype(f32)
        blocks = [polys[n][k * TILE : (k + 1) * TILE, :] for k in range(len(ABOVE) + len(TWOS))]
        twos = [part.astype(f32) for part in blocks[len(ABOVE) :]]
        seconds = [tail[SIDES + k : SIDES + k + 1] for k in range(len(TWOS))]
        parts = unpack(blocks[: len(ABOVE)] + twos, seconds)
        for i in range(SIDES):
            parts[i, i] = parts[i, i].astype(bf16)
        for i, j in ABOVE:
            parts[j, i] = parts[i, j].T
        sides = range(SIDES)
        poly = jnp.concatenate(
            [jnp.concatenate([parts[i, j] for j in sides], axis=1) for i in sides], axis=0
        )
        low = jnp.concatenate([tail[i : i + 1] for i in sides], axis=1)
        rows = held.shape[1]
        tile = min(256, rows)
        target = updates.at[place.matrix(slot, d)]
        for k in range(rows // tile):
            part = pl.ds(k * tile, tile)
            x = pieces[n][part] if picks[n] is None else pieces[n][picks[n], part]
            held[n, part] = (dot(x, poly) + x.astype(f32) * low).astype(bf16)
            copies.append(pltpu.make_async_copy(held.at[n, part], target.at[part], sems.at[len(copies)]))
            copies[-1].start()
    for copy in copies:
        copy.wait()


def finish(line, slots, slot, steps, pieces, polys, shape, buffer):
    operands = [piece for piece, _ in pieces] + list(polys)
    specs = [IN_VMEM] * len(operands)
    aliases = {}
    if buffer is not None:
        aliases = {len(operands): 0}
        operands.append(in_hbm(buffer))
        specs.append(IN_HBM)
    return line.run(
        functools.partial(finish_kernel, slots, slot, steps, shape[0], [index for _, index in pieces]),
        operands,
        specs,
        [pltpu.HBM(shape, bf16), jax.ShapeDtypeStruct((8, TILE), f32)],
        [IN_HBM, IN_VMEM],
        name="finish",
        scalars=SPOTS,
        token=1,
        scratch=[pltpu.VMEM((len(steps), shape[1], RANK), bf16), pltpu.SemaphoreType.DMA((len(steps) * max(1, shape[1] // 256),))],
        aliases=aliases,
        vmem=8,
        work=(2 * len(steps) * shape[1] * RANK * RANK, 4 * len(steps) * shape[1] * RANK),
    )[0]


def on_device(gradients, momentum, slot_table, *, owners, group):
    matrix_count = gradients.shape[0]
    held_slots = momentum.shape[0]
    near = 1 << ((group.bit_length() - 1) // 2)
    shares = (near, group // near)
    place = jnp.concatenate(
        [
            slot_table.astype(jnp.int32),
            jnp.stack([lax.axis_index("owner"), lax.axis_index("fsdp")]).astype(jnp.int32),
        ]
    )

    line = Line(place)
    line.owners = owners
    line.spots = make_spots(place, matrix_count, held_slots, owners)
    all_slots = range(held_slots)
    far_steps, near_steps = list(range(2, owners)), list(range(1, min(2, owners)))
    arrived = {}
    wanted = [(0, d) for d in far_steps] + [(slot, d) for slot in all_slots for d in near_steps]
    wanted += [(slot, d) for slot in range(1, held_slots) for d in far_steps]
    picked = {}
    for few in (wanted[:1], wanted[1:]):
        picked.update(zip(few, pick(line, gradients, held_slots, few)))

    def send(pieces):
        for slot, d in pieces:
            arrived[slot, d] = lax.ppermute(picked[slot, d], "owner", partners(owners, d))

    fetched = {}
    renewed, rows, returned, sums, lines, mine, whole_lines, gathered, polys = None, {}, {}, {}, {}, {}, {}, {}, {}

    summed = packed_rows(group)

    def blend_piece(slot, d, then=()):
        nonlocal renewed
        line.waiting.update({piece: picked[piece] for piece in then})
        gradient = arrived[slot, d] if d else gradients
        if d == owners - 1:
            renewed, rows[slot, d], sums[slot] = blend_last(
                line, gradient, fetched[slot], slot, d, matrix_count, renewed, rows[slot, d - 1], sums[slot], shares
            )
        else:
            renewed, rows[slot, d], sums[slot] = blend(
                line,
                gradient,
                momentum,
                slot,
                d,
                matrix_count,
                renewed,
                rows[slot, d - 1] if d > 1 and d % 2 else None,
                sums.get(slot),
                summed,
            )
        picked.update({piece: line.passed[piece] for piece in then})
        send(then)

    def send_back(slot, d):
        if d == 0:
            returned[slot, 0] = rows[slot, 0], None
        elif d == 1:
            returned[slot, 1] = lax.ppermute(rows[slot, 1], "owner", partners(owners, 1)), None
        else:
            pair = lax.ppermute(rows[slot, d + 1], "owner", partners(owners, d))
            returned[slot, d] = pair, 0

    def across_near(x, e1):
        return lax.ppermute(x, "fsdp", partners(group, e1))

    def across_far(x, e2):
        return lax.ppermute(x, "fsdp", partners(group, e2 * near))

    def first_sum(slot):
        received = [across_near(sums[slot][e1], e1) for e1 in range(1, near)]
        lines[slot] = add_near(line, sums[slot], received)

    def second_sum(slot):
        parts = lines[slot]
        received = [across_far(parts[e2], e2) for e2 in range(1, shares[1])]
        mine[slot] = add_far(line, [parts[0], *received])

    def collect(slot):
        part = mine[slot]
        whole_lines[slot] = stack(line, [part] + [across_far(part, e2) for e2 in range(1, shares[1])])

    def send_line(slot):
        whole_line = whole_lines[slot]
        gathered[slot] = [whole_line] + [across_near(whole_line, e1) for e1 in range(1, near)]

    def make_polynomial(slot):
        polys[slot, 0] = polynomial(line, gathered[slot])
        for d in far_steps[::2]:
            polys[slot, d] = lax.ppermute(polys[slot, 0], "owner", partners(owners, d))
        for d in near_steps:
            polys[slot, d] = lax.ppermute(polys[slot, 0], "owner", partners(owners, d))

    def pass_polynomials(slot):
        for d in far_steps[::2]:
            polys[slot, d] = step(line, polys[slot, d])
            polys[slot, d + 1] = lax.ppermute(polys[slot, d], "owner", partners(owners, 1))

    updates = None

    def finish_steps(slot, steps):
        nonlocal updates
        updates = finish(
            line,
            held_slots,
            slot,
            steps,
            [returned[slot, d] for d in steps],
            [polys[slot, d] for d in steps],
            gradients.shape,
            updates,
        )

    def expect(*wanted):
        line.due += [returned[slot, d][0] for slot, d in wanted if d < owners]

    far_pieces = [(slot, d) for slot in all_slots for d in far_steps]
    near_pieces = [(slot, d) for slot in all_slots for d in near_steps]
    send(far_pieces[:2] + near_pieces[:1])
    blend_piece(0, 0, far_pieces[2:] + near_pieces[1:])
    blend_piece(1, 0)
    for slot in all_slots:
        send_back(slot, 0)
    for d in near_steps:
        for slot in all_slots:
            blend_piece(slot, d)
            send_back(slot, d)
    for d in far_steps[:-1]:
        blend_piece(0, d)
    fetched[0] = fetch(line, momentum, 0, owners - 1, matrix_count, gradients.shape[1])
    expect((0, 1))
    for d in far_steps[-1:]:
        blend_piece(0, d)
    fetched[1] = fetch(line, momentum, 1, owners - 1, matrix_count, gradients.shape[1])
    expect((1, 1))
    first_sum(0)
    for d in far_steps[1::2]:
        line.waiting[d] = rows[0, d]
    for d in far_steps[:-1]:
        blend_piece(1, d)
    for d in far_steps[1::2]:
        rows[0, d] = line.passed[d]
        send_back(0, d - 1)
    for d in far_steps[-1:]:
        blend_piece(1, d)
    line.waiting["sum"] = sums[1]
    second_sum(0)
    sums[1] = line.passed["sum"]
    first_sum(1)
    for d in far_steps[1::2]:
        line.waiting[d] = rows[1, d]
    collect(0)
    for d in far_steps[1::2]:
        rows[1, d] = line.passed[d]
        send_back(1, d - 1)
    expect(*[(0, d) for d in far_steps[::2]])
    line.waiting["line"] = whole_lines[0]
    second_sum(1)
    whole_lines[0] = line.passed["line"]
    send_line(0)
    collect(1)
    send_line(1)
    make_polynomial(0)
    make_polynomial(1)
    for slot in all_slots:
        for d in far_steps[::2]:
            line.waiting[slot, d] = returned[slot, d][0]
    step(line)
    for slot in all_slots:
        for d in far_steps[::2]:
            pair = line.passed[slot, d]
            returned[slot, d] = pair, 0
            returned[slot, d + 1] = lax.ppermute(pair, "owner", partners(owners, 1)), 1
    finish_steps(0, [0] + near_steps)
    pass_polynomials(0)
    finish_steps(1, [0] + near_steps)
    finish_steps(0, far_steps)
    pass_polynomials(1)
    for d in far_steps:
        finish_steps(1, [d])
    return (updates, renewed)


def solution(mesh):
    return jax.shard_map(
        functools.partial(on_device, owners=mesh.shape["owner"], group=mesh.shape["fsdp"]),
        mesh=mesh,
        in_specs=(P(None, ("fsdp", "owner"), None), P("owner", "fsdp", None), P()),
        out_specs=(P(None, ("fsdp", "owner"), None), P("owner", "fsdp", None)),
        check_vma=False,
    )
```

```python
import functools
import math

import jax
import jax.numpy as jnp
from jax import lax
from jax.experimental import pallas as pl
from jax.experimental.pallas import tpu as pltpu
from jax.sharding import PartitionSpec as P

LONG = 16384
RANK = 512
ITERS = 5
TILE = 128

quintic = (3.4445, -4.775, 2.0315)
momentum_decay = 0.95
epsilon = 1e-07

SIDES = RANK // TILE
ABOVE = [(i, j) for i in range(SIDES) for j in range(i + 1, SIDES)]
TWOS = [(i, i + 1) for i in range(0, SIDES, 2)]
DIAGONALS = (len(ABOVE) + len(TWOS)) * TILE
POLY_ROWS = DIAGONALS + 16

f32, bf16 = jnp.float32, jnp.bfloat16


def in_hbm(x):
    return pltpu.with_memory_space_constraint(x, pltpu.HBM)


def matrix_of(place, count, slots, slot, d):
    wanted = slots * jnp.bitwise_xor(place[count], d) + slot
    found = jnp.int32(0)
    for m in range(1, count):
        found = found + jnp.where(place[m] == wanted, m, 0)
    return found


def group_index(place):
    return place[place.shape[0] - 1]


def packed_rows(group):
    return -(-(DIAGONALS + 8) // (8 * group)) * (8 * group)


def block_ids():
    return (
        lax.broadcasted_iota(jnp.int32, (TILE, TILE), 0),
        lax.broadcasted_iota(jnp.int32, (TILE, TILE), 1),
    )


def diagonal_of(block):
    row, column = block_ids()
    return jnp.sum(jnp.where(row == column, block, 0.0), axis=0, keepdims=True)


def pack(block):
    row, column = block_ids()
    blocks = [block(i, j) for i, j in ABOVE]
    blocks += [jnp.where(row <= column, block(i, i), block(j, j)) for i, j in TWOS]
    return blocks, [diagonal_of(block(j, j)) for _, j in TWOS]


def unpack(blocks, diagonals):
    row, column = block_ids()
    parts = dict(zip(ABOVE, blocks))
    for (i, j), both, diagonal in zip(TWOS, blocks[len(ABOVE) :], diagonals):
        turned = both.T
        parts[i, i] = jnp.where(row <= column, both, turned)
        parts[j, j] = jnp.where(row > column, both, jnp.where(row < column, turned, diagonal))
    return parts


def partners(size, step):
    return [(i, i ^ step) for i in range(size)]


def blend_kernel(buffers, has_sum, *refs):
    refs = list(refs)
    place = refs.pop(0)
    gradient, momentum = refs.pop(0), refs.pop(0)
    del refs[:buffers]
    before = refs.pop(0) if has_sum else None
    renewed, rows, total, held = refs
    step = pl.program_id(0)

    @pl.when(step == 0)
    def _():
        held[...] = before[...] if has_sum else jnp.zeros_like(held)

    g = gradient[...].astype(f32)
    m = momentum_decay * momentum[...] + g
    renewed[...] = m
    x = (g + momentum_decay * m).astype(bf16)
    rows[...] = x
    add_gram(held, x)

    @pl.when(step == pl.num_programs(0) - 1)
    def _():
        total[...] = held[...]


def add_gram(held, x):
    half, dims = RANK // 2, (((0,), (0,)), ((), ()))
    upper = lax.dot_general(x[:, :half], x, dims, preferred_element_type=f32)
    lower = lax.dot_general(x[:, half:], x[:, half:], dims, preferred_element_type=f32)

    def block(i, j):
        part, i0, j0 = (upper, i, j) if i < SIDES // 2 else (lower, i - SIDES // 2, j - SIDES // 2)
        return part[i0 * TILE : (i0 + 1) * TILE, j0 * TILE : (j0 + 1) * TILE]

    blocks, diagonals = pack(block)
    for n, part in enumerate(blocks):
        held[n * TILE : (n + 1) * TILE, :] += part
    for n, part in enumerate(diagonals):
        held[DIAGONALS + n : DIAGONALS + n + 1, :] += part


def blend_whole_kernel(slot, d, has_pair, place, gradient, momentum, _buffer, before, *refs):
    renewed, rows, total, loaded, new, sems = refs[1:] if has_pair else refs
    size = gradient.shape[0]
    tile = min(256, size)
    count = size // tile
    first = jnp.bitwise_xor(place.owner(), d) * size
    parts = [pl.ds(n * tile, tile) for n in range(count)]
    spans = [pl.ds(pl.multiple_of(first + n * tile, 8), tile) for n in range(count)]
    loads = [
        pltpu.make_async_copy(momentum.at[slot, spans[n]], loaded.at[parts[n]], sems.at[n])
        for n in range(count)
    ]
    stores = [
        pltpu.make_async_copy(new.at[parts[n]], renewed.at[slot, spans[n]], sems.at[count + n])
        for n in range(count)
    ]
    for load in loads:
        load.start()
    total[...] = before[...]
    for n, part in enumerate(parts):
        loads[n].wait()
        g = gradient[part].astype(f32)
        m = momentum_decay * loaded[part] + g
        new[part] = m
        stores[n].start()
        x = (g + momentum_decay * m).astype(bf16)
        if d < 2:
            rows[part] = x
        else:
            rows[d % 2, part] = x
    add_gram(total, rows[...] if d < 2 else rows[d % 2])
    for store in stores:
        store.wait()


def blend_whole(line, gradient, momentum, slot, d, buffer, pair, before):
    size = gradient.shape[0]
    count = size // min(256, size)
    aliases = {2: 0}
    operands, specs = [gradient, in_hbm(momentum), in_hbm(buffer), before], [IN_VMEM, IN_HBM, IN_HBM, IN_VMEM]
    if pair is not None:
        aliases[4] = 1
        operands.append(pair)
        specs.append(IN_VMEM)
    return line.run(
        functools.partial(blend_whole_kernel, slot, d, pair is not None),
        operands,
        specs,
        [
            pltpu.HBM(buffer.shape, f32),
            jax.ShapeDtypeStruct((size, RANK) if d < 2 else (2, size, RANK), bf16),
            jax.ShapeDtypeStruct(before.shape, f32),
        ],
        [IN_HBM, IN_VMEM, IN_VMEM],
        name="blend_whole",
        scalars=SPOTS,
        token=2,
        scratch=[
            pltpu.VMEM((size, RANK), f32),
            pltpu.VMEM((size, RANK), f32),
            pltpu.SemaphoreType.DMA((2 * count,)),
        ],
        aliases=aliases,
        vmem=8,
        work=(2 * size * RANK * RANK, size * RANK * 12),
    )


def fetch_kernel(slot, d, count, place, momentum, target, sem):
    rows = target.shape[0]
    start = pl.multiple_of(jnp.bitwise_xor(place[count], d) * rows, 8)
    copy = pltpu.make_async_copy(momentum.at[slot, pl.ds(start, rows)], target, sem)
    copy.start()
    copy.wait()


def fetch(line, momentum, slot, d, count, piece_rows):
    return line.run(
        functools.partial(fetch_kernel, slot, d, count),
        [in_hbm(momentum)],
        [IN_HBM],
        [jax.ShapeDtypeStruct((piece_rows, RANK), f32)],
        [IN_VMEM],
        name="fetch",
        scratch=[pltpu.SemaphoreType.DMA],
        work=(0, 8 * piece_rows * RANK),
    )[0]


def blend_last_kernel(slot, d, count, place, gradient, momentum, _buffer, _pair, before, renewed, pair, total, held, new, sems):
    rows = gradient.shape[0]
    tile = min(256, rows)
    first = jnp.bitwise_xor(place.owner(), d) * rows
    copies = []
    for n in range(rows // tile):
        part = pl.ds(n * tile, tile)
        g = gradient[part].astype(f32)
        m = momentum_decay * momentum[part] + g
        new[part] = m
        target = renewed.at[slot, pl.ds(pl.multiple_of(first + n * tile, 8), tile)]
        copies.append(pltpu.make_async_copy(new.at[part], target, sems.at[n]))
        copies[-1].start()
        pair[1, part] = (g + momentum_decay * m).astype(bf16)
    held[...] = before[...]
    add_gram(held, pair[1])
    near, far, size, _ = total.shape
    for e1 in range(near):
        for e2 in range(far):
            who = jnp.bitwise_xor(place.group(), e2 * near + e1)
            total[e1, e2] = held[pl.ds(pl.multiple_of(who * size, 8), size), :]
    for copy in copies:
        copy.wait()


def blend_last(line, gradient, momentum, slot, d, count, buffer, pair, before, shares):
    piece_rows = gradient.shape[0]
    total = (*shares, before.shape[0] // (shares[0] * shares[1]), TILE)
    return line.run(
        functools.partial(blend_last_kernel, slot, d, count),
        [gradient, momentum, in_hbm(buffer), pair, before],
        [IN_VMEM, IN_VMEM, IN_HBM, IN_VMEM, IN_VMEM],
        [
            pltpu.HBM(buffer.shape, f32),
            jax.ShapeDtypeStruct(pair.shape, bf16),
            jax.ShapeDtypeStruct(total, f32),
        ],
        [IN_HBM, IN_VMEM, IN_VMEM],
        name="blend_last",
        scalars=SPOTS,
        token=2,
        scratch=[
            pltpu.VMEM(before.shape, f32),
            pltpu.VMEM((piece_rows, RANK), f32),
            pltpu.SemaphoreType.DMA((piece_rows // min(256, piece_rows),)),
        ],
        aliases={2: 0, 3: 1},
        vmem=8,
        work=(2 * piece_rows * RANK * RANK, piece_rows * RANK * 12),
    )


SPOTS, RAW = "spots", "raw"


class Column:
    def __init__(self, ref):
        self.ref = ref

    def __getitem__(self, k):
        return self.ref[k, 0]


class Spots:
    def __init__(self, ref, owners):
        self.ref, self.owners = ref, owners

    def matrix(self, slot, d):
        return self.ref[slot * self.owners + d, 0]

    def owner(self):
        return self.ref[self.ref.shape[0] - 2, 0]

    def group(self):
        return self.ref[self.ref.shape[0] - 1, 0]


def make_spots(place, count, slots, owners):
    targets = slots * jnp.bitwise_xor(place[count], jnp.arange(owners))[None, :] + jnp.arange(slots)[:, None]
    found = place[None, :count] == targets.reshape(-1, 1)
    matrices = jnp.sum(jnp.where(found, jnp.arange(count)[None, :], 0), axis=1).astype(jnp.int32)
    free = -(matrices.shape[0] + 2) % 8
    column = jnp.concatenate([matrices, jnp.zeros((free,), jnp.int32), place[count:]])
    return jnp.broadcast_to(column[:, None], (column.shape[0], TILE))


class Line:
    def __init__(self, place):
        self.place, self.last, self.due, self.waiting, self.passed = place, None, [], {}, {}
        self.spots, self.raw, self.owners = None, None, 0

    def run(
        self,
        kernel,
        operands,
        specs,
        out_shape,
        out_specs,
        *,
        name,
        work,
        token=0,
        grid=(1,),
        scratch=(),
        aliases=None,
        vmem=8,
        scalars=True,
    ):
        before = [] if self.last is None or (token is None and out_shape) else [self.last]
        before += self.due
        keys = list(self.waiting)
        before += [self.waiting[key] for key in keys]
        skip, given, results = len(before), len(before) + len(operands), len(out_shape)
        lead = 1 if scalars else 0
        prefetched = scalars is True
        spots = {SPOTS: self.spots, RAW: self.raw}.get(scalars) if lead else None
        aliases = {lead + skip + i: o for i, o in (aliases or {}).items()}
        for k in range(len(keys)):
            aliases[lead + skip - len(keys) + k] = results + k

        def body(*refs):
            refs, place = refs[lead:], refs[:lead]
            if spots is not None:
                place = (Spots(place[0], self.owners) if scalars is SPOTS else Column(place[0]),)
            kernel(*place, *refs[skip : given + results], *refs[given + results + len(keys) :])

        any_spec = pl.BlockSpec(memory_space=pl.ANY)
        flops, moved = work
        in_specs = [any_spec] * skip + specs
        out_specs = out_specs + [any_spec] * len(keys)
        if prefetched:
            layout = {
                "grid_spec": pltpu.PrefetchScalarGridSpec(
                    num_scalar_prefetch=1,
                    grid=grid,
                    in_specs=in_specs,
                    out_specs=out_specs,
                    scratch_shapes=list(scratch),
                )
            }
        else:
            in_specs = [IN_VMEM] * lead + in_specs
            layout = {"in_specs": in_specs, "out_specs": out_specs, "scratch_shapes": list(scratch)}
        outs = pl.pallas_call(
            body,
            **layout,
            out_shape=out_shape
            + [jax.ShapeDtypeStruct(self.waiting[key].shape, self.waiting[key].dtype) for key in keys],
            input_output_aliases=aliases,
            compiler_params=pltpu.CompilerParams(vmem_limit_bytes=vmem * 2**20),
            cost_estimate=pl.CostEstimate(flops=20 * flops, bytes_accessed=20 * moved, transcendentals=0),
            name=name,
        )(*([self.place] if prefetched else [spots] * lead), *before, *operands)
        if token is not None:
            self.last = outs[token]
        elif not out_shape:
            self.last = outs[0]
        self.due, self.waiting = [], {}
        self.passed.update(zip(keys, outs[results:]))
        return outs[:results]


IN_VMEM = pl.BlockSpec(memory_space=pltpu.VMEM)
IN_HBM = pl.BlockSpec(memory_space=pltpu.HBM)


def pick_kernel(slots, count, wanted, place, gradients, *refs):
    targets, sems = refs[:-1], refs[-1]
    copies = []
    for n, (slot, d) in enumerate(wanted):
        source = gradients.at[matrix_of(place, count, slots, slot, d)]
        copies.append(pltpu.make_async_copy(source, targets[n], sems.at[n]))
        copies[-1].start()
    for copy in copies:
        copy.wait()


def pick(line, gradients, slots, wanted):
    count, rows, _ = gradients.shape
    return line.run(
        functools.partial(pick_kernel, slots, count, wanted),
        [in_hbm(gradients)],
        [IN_HBM],
        [jax.ShapeDtypeStruct((rows, RANK), bf16) for _ in wanted],
        [IN_VMEM for _ in wanted],
        name="pick",
        scalars=RAW,
        scratch=[pltpu.SemaphoreType.DMA((len(wanted),))],
        work=(0, 4 * len(wanted) * rows * RANK),
    )


def blend(line, gradient, momentum, slot, d, count, buffer, pair, before, summed):
    slots = momentum.shape[0]
    piece_rows = gradient.shape[-2]
    tile = min(256, piece_rows)
    steps = piece_rows // tile
    if d == 0:
        gradient_spec = pl.BlockSpec(
            (None, tile, RANK), lambda i, p: (matrix_of(p, count, slots, slot, 0), i, 0)
        )
        gradient = in_hbm(gradient)
    else:
        gradient_spec = pl.BlockSpec((tile, RANK), lambda i, p: (i, 0))
    momentum_spec = pl.BlockSpec(
        (None, tile, RANK), lambda i, p: (slot, jnp.bitwise_xor(p[count], d) * steps + i, 0)
    )
    in_specs, operands = [gradient_spec, momentum_spec], [gradient, in_hbm(momentum)]
    aliases = {}
    for result, array in enumerate((buffer, pair)):
        if array is not None:
            aliases[len(operands)] = result
            in_specs.append(IN_HBM if result == 0 else pl.BlockSpec(memory_space=pl.ANY))
            operands.append(in_hbm(array) if result == 0 else array)
    if d < 2:
        rows_shape, rows_spec = (piece_rows, RANK), pl.BlockSpec((tile, RANK), lambda i, p: (i, 0))
    else:
        rows_shape = (2, piece_rows, RANK)
        rows_spec = pl.BlockSpec((None, tile, RANK), lambda i, p: (d % 2, i, 0))
    total = (summed, TILE)
    if before is not None:
        in_specs.append(pl.BlockSpec(total, lambda i, p: (0, 0)))
        operands.append(before)
    return line.run(
        functools.partial(blend_kernel, len(aliases), before is not None),
        operands,
        in_specs,
        [
            pltpu.HBM(momentum.shape, f32),
            jax.ShapeDtypeStruct(rows_shape, bf16),
            jax.ShapeDtypeStruct(total, f32),
        ],
        [
            momentum_spec,
            rows_spec,
            pl.BlockSpec(total, lambda i, p: (0, 0)),
        ],
        name="blend",
        token=2,
        grid=(steps,),
        scratch=[pltpu.VMEM(total, f32)],
        aliases=aliases,
        vmem=8,
        work=(2 * piece_rows * RANK * RANK, piece_rows * RANK * 12),
    )


def add_near_kernel(share, *refs):
    far = share.shape[1]
    received, targets = refs[: len(refs) - far], refs[len(refs) - far :]
    for e2, target in enumerate(targets):
        total = share[0, e2]
        for other in received:
            total = total + other[e2]
        target[...] = total


def add_near(line, share, received):
    _, far, count, _ = share.shape
    return line.run(
        add_near_kernel,
        [share, *received],
        [IN_VMEM] * (1 + len(received)),
        [jax.ShapeDtypeStruct((count, TILE), f32)] * far,
        [IN_VMEM] * far,
        name="add_near",
        scalars=False,
        work=(0, 12 * far * count * TILE),
    )


def add_far_kernel(*refs):
    total = refs[0][...]
    for other in refs[1:-1]:
        total = total + other[...]
    refs[-1][...] = total


def add_far(line, parts):
    return line.run(
        add_far_kernel,
        list(parts),
        [IN_VMEM] * len(parts),
        [jax.ShapeDtypeStruct(parts[0].shape, f32)],
        [IN_VMEM],
        name="add_far",
        scalars=False,
        work=(0, 4 * (len(parts) + 1) * parts[0].size),
    )[0]


def step(line, array=None):
    if array is not None:
        line.waiting["step"] = array
    line.run(lambda: None, [], [], [], [], name="step", token=None, scalars=False, work=(0, 0))
    return line.passed.get("step")


def stack_kernel(*refs):
    for e, part in enumerate(refs[:-1]):
        refs[-1][e] = part[...]


def stack(line, parts):
    return line.run(
        stack_kernel,
        list(parts),
        [IN_VMEM] * len(parts),
        [jax.ShapeDtypeStruct((len(parts), *parts[0].shape), f32)],
        [IN_VMEM],
        name="stack",
        scalars=False,
        work=(0, 8 * len(parts) * parts[0].size),
    )[0]


SHIFTS = (0.0, 0.0, 0.1, 0.6, 0.85)
FINE_TURN, FINE_POLY = 2, 3
HALF = RANK // 2


def dot(a, b):
    return jnp.dot(a, b, preferred_element_type=f32)


def whole(x):
    top, corner = x
    return jnp.concatenate([top, jnp.concatenate([top[:, HALF:].T, corner], axis=1)], axis=0)


def operand(x, passes):
    high = tuple(part.astype(bf16) for part in x)
    if passes == 1:
        return (whole(high),)
    low = tuple((part - rounded.astype(f32)).astype(bf16) for part, rounded in zip(x, high))
    return (whole(high), whole(low))


def product(a, b):
    top, corner = dot(a[0][:HALF], b[0]), dot(a[0][HALF:], b[0][:, HALF:])
    if len(a) > 1:
        top += dot(a[0][:HALF], b[1]) + dot(a[1][:HALF], b[0])
        corner += dot(a[0][HALF:], b[1][:, HALF:]) + dot(a[1][HALF:], b[0][:, HALF:])
    return (top, corner)


def combine(*terms):
    return tuple(
        functools.reduce(lambda x, y: x + y, [w * x[part] for w, x in terms]) for part in range(2)
    )


def add_identity(x, value):
    top, corner = x
    row = lax.broadcasted_iota(jnp.int32, (HALF, HALF), 0)
    column = lax.broadcasted_iota(jnp.int32, (HALF, HALF), 1)
    eye = jnp.where(row == column, value, 0.0)
    return (jnp.concatenate([top[:, :HALF] + eye, top[:, HALF:]], axis=1), corner + eye)


def polynomial_kernel(near, far, count, place, *refs):
    *shared, result, packed = refs
    for e1, other in enumerate(shared):
        for e2 in range(far):
            who = jnp.bitwise_xor(place.group(), e2 * near + e1)
            packed[pl.ds(pl.multiple_of(who * count, 8), count), :] = other[e2]
    blocks = [packed[n * TILE : (n + 1) * TILE, :] for n in range(len(ABOVE) + len(TWOS))]
    diagonals = [packed[DIAGONALS + n : DIAGONALS + n + 1, :] for n in range(len(TWOS))]
    parts = unpack(blocks, diagonals)
    trace = jnp.sum(sum(diagonals) + sum(diagonal_of(both) for both in blocks[len(ABOVE) :]))
    for i, j in ((0, 1), (2, 3)):
        parts[j, i] = parts[i, j].T

    def rows_of(count, first):
        return jnp.concatenate(
            [
                jnp.concatenate([parts[i, j] for j in range(first, SIDES)], axis=1)
                for i in range(first, first + count)
            ],
            axis=0,
        )

    half = HALF // TILE
    scale = 1.0 / (jnp.sqrt(jnp.full((1, 1), trace, f32)) + epsilon)
    rest = tuple((x * scale) * scale for x in (rows_of(half, 0), rows_of(half, half)))
    a, b, c = quintic
    poly = None
    for k in range(ITERS):
        shift = SHIFTS[k]
        gain = a + b * shift + c * shift * shift
        d = operand(rest, 3 if k == FINE_TURN else 1)
        step = combine((b + 2 * c * shift, rest), (c, product(d[:1], d[:1])))
        s = operand(step, 3 if k in (FINE_TURN, FINE_POLY) else 1)
        if poly is None:
            poly = add_identity(step, gain)
        else:
            p = operand(poly, 3 if k == FINE_POLY else 1)
            poly = combine((gain, poly), (1.0, product(p, s)))
        if k < ITERS - 1:
            middle = combine((gain, rest), (shift, step), (1.0, product(d, s)))
            turned = product(operand(middle, 1), s)
            rest = combine((gain, middle), (gain * shift, step), (1.0, turned))
            rest = add_identity(rest, gain * gain * shift - SHIFTS[k + 1])
    top, corner = tuple(x * (scale * math.sqrt(max(LONG, RANK))) for x in poly)

    def block(i, j):
        part, i0, j0 = (top, i, j) if i < half else (corner, i - half, j - half)
        return part[i0 * TILE : (i0 + 1) * TILE, j0 * TILE : (j0 + 1) * TILE]

    blocks, seconds = pack(block)
    for n, part in enumerate(blocks):
        result[n * TILE : (n + 1) * TILE, :] = part.astype(bf16)
    lows = []
    for i in range(SIDES):
        diagonal = diagonal_of(block(i, i))
        lows.append(diagonal - diagonal.astype(bf16).astype(f32))
    rows = lows + seconds
    rows.append(jnp.zeros((POLY_ROWS - DIAGONALS - len(rows), TILE), f32))
    result[DIAGONALS:, :] = jnp.concatenate(rows, axis=0).astype(bf16)


def polynomial(line, shared):
    near, (far, count, _) = len(shared), shared[0].shape
    return line.run(
        functools.partial(polynomial_kernel, near, far, count),
        list(shared),
        [IN_VMEM] * near,
        [jax.ShapeDtypeStruct((POLY_ROWS, TILE), bf16)],
        [IN_VMEM],
        name="polynomial",
        scalars=SPOTS,
        scratch=[pltpu.VMEM((near * far * count, TILE), f32)],
        vmem=12,
        work=(RANK**3, 2**16),
    )[0]


def finish_kernel(slots, slot, steps, matrices, picks, place, *refs):
    refs = list(refs)
    count = len(steps)
    pieces, polys = refs[:count], refs[count : 2 * count]
    updates, _, held, sems = refs[-4:]
    copies = []
    for n, d in enumerate(steps):
        tail = polys[n][DIAGONALS:, :].astype(f32)
        blocks = [polys[n][k * TILE : (k + 1) * TILE, :] for k in range(len(ABOVE) + len(TWOS))]
        twos = [part.astype(f32) for part in blocks[len(ABOVE) :]]
        seconds = [tail[SIDES + k : SIDES + k + 1] for k in range(len(TWOS))]
        parts = unpack(blocks[: len(ABOVE)] + twos, seconds)
        for i in range(SIDES):
            parts[i, i] = parts[i, i].astype(bf16)
        for i, j in ABOVE:
            parts[j, i] = parts[i, j].T
        sides = range(SIDES)
        poly = jnp.concatenate(
            [jnp.concatenate([parts[i, j] for j in sides], axis=1) for i in sides], axis=0
        )
        low = jnp.concatenate([tail[i : i + 1] for i in sides], axis=1)
        rows = held.shape[1]
        tile = min(256, rows)
        target = updates.at[place.matrix(slot, d)]
        for k in range(rows // tile):
            part = pl.ds(k * tile, tile)
            x = pieces[n][part] if picks[n] is None else pieces[n][picks[n], part]
            held[n, part] = (dot(x, poly) + x.astype(f32) * low).astype(bf16)
            copies.append(pltpu.make_async_copy(held.at[n, part], target.at[part], sems.at[len(copies)]))
            copies[-1].start()
    for copy in copies:
        copy.wait()


def finish(line, slots, slot, steps, pieces, polys, shape, buffer):
    operands = [piece for piece, _ in pieces] + list(polys)
    specs = [IN_VMEM] * len(operands)
    aliases = {}
    if buffer is not None:
        aliases = {len(operands): 0}
        operands.append(in_hbm(buffer))
        specs.append(IN_HBM)
    return line.run(
        functools.partial(finish_kernel, slots, slot, steps, shape[0], [index for _, index in pieces]),
        operands,
        specs,
        [pltpu.HBM(shape, bf16), jax.ShapeDtypeStruct((8, TILE), f32)],
        [IN_HBM, IN_VMEM],
        name="finish",
        scalars=SPOTS,
        token=1,
        scratch=[pltpu.VMEM((len(steps), shape[1], RANK), bf16), pltpu.SemaphoreType.DMA((len(steps) * max(1, shape[1] // 256),))],
        aliases=aliases,
        vmem=8,
        work=(2 * len(steps) * shape[1] * RANK * RANK, 4 * len(steps) * shape[1] * RANK),
    )[0]


def on_device(gradients, momentum, slot_table, *, owners, group):
    matrix_count = gradients.shape[0]
    held_slots = momentum.shape[0]
    near = 1 << ((group.bit_length() - 1) // 2)
    shares = (near, group // near)
    place = jnp.concatenate(
        [
            slot_table.astype(jnp.int32),
            jnp.stack([lax.axis_index("owner"), lax.axis_index("fsdp")]).astype(jnp.int32),
        ]
    )

    line = Line(place)
    line.owners = owners
    line.raw = jnp.broadcast_to(jnp.pad(place, (0, -place.shape[0] % 8))[:, None], (-(-place.shape[0] // 8) * 8, TILE))
    line.spots = make_spots(place, matrix_count, held_slots, owners)
    all_slots = range(held_slots)
    far_steps, near_steps = list(range(2, owners)), list(range(1, min(2, owners)))
    arrived = {}
    wanted = [(0, d) for d in far_steps] + [(slot, d) for slot in all_slots for d in near_steps]
    wanted += [(slot, d) for slot in range(1, held_slots) for d in far_steps]
    picked = {}
    for few in (wanted[:1], wanted[1:]):
        picked.update(zip(few, pick(line, gradients, held_slots, few)))

    def send(pieces):
        for slot, d in pieces:
            arrived[slot, d] = lax.ppermute(picked[slot, d], "owner", partners(owners, d))

    fetched = {}
    renewed, rows, returned, sums, lines, mine, whole_lines, gathered, polys = None, {}, {}, {}, {}, {}, {}, {}, {}

    summed = packed_rows(group)

    def blend_piece(slot, d, then=()):
        nonlocal renewed
        line.waiting.update({piece: picked[piece] for piece in then})
        gradient = arrived[slot, d] if d else gradients
        if d == owners - 1:
            renewed, rows[slot, d], sums[slot] = blend_last(
                line, gradient, fetched[slot], slot, d, matrix_count, renewed, rows[slot, d - 1], sums[slot], shares
            )
        elif d:
            renewed, rows[slot, d], sums[slot] = blend_whole(
                line,
                gradient,
                momentum,
                slot,
                d,
                renewed,
                rows[slot, d - 1] if d > 1 and d % 2 else None,
                sums[slot],
            )
        else:
            renewed, rows[slot, d], sums[slot] = blend(
                line,
                gradient,
                momentum,
                slot,
                d,
                matrix_count,
                renewed,
                rows[slot, d - 1] if d > 1 and d % 2 else None,
                sums.get(slot),
                summed,
            )
        picked.update({piece: line.passed[piece] for piece in then})
        send(then)

    def send_back(slot, d):
        if d == 0:
            returned[slot, 0] = rows[slot, 0], None
        elif d == 1:
            returned[slot, 1] = lax.ppermute(rows[slot, 1], "owner", partners(owners, 1)), None
        else:
            pair = lax.ppermute(rows[slot, d + 1], "owner", partners(owners, d))
            returned[slot, d] = pair, 0

    def across_near(x, e1):
        return lax.ppermute(x, "fsdp", partners(group, e1))

    def across_far(x, e2):
        return lax.ppermute(x, "fsdp", partners(group, e2 * near))

    def first_sum(slot):
        received = [across_near(sums[slot][e1], e1) for e1 in range(1, near)]
        lines[slot] = add_near(line, sums[slot], received)

    def second_sum(slot):
        parts = lines[slot]
        received = [across_far(parts[e2], e2) for e2 in range(1, shares[1])]
        mine[slot] = add_far(line, [parts[0], *received])

    def collect(slot):
        part = mine[slot]
        whole_lines[slot] = stack(line, [part] + [across_far(part, e2) for e2 in range(1, shares[1])])

    def send_line(slot):
        whole_line = whole_lines[slot]
        gathered[slot] = [whole_line] + [across_near(whole_line, e1) for e1 in range(1, near)]

    def make_polynomial(slot):
        polys[slot, 0] = polynomial(line, gathered[slot])
        for d in far_steps[::2]:
            polys[slot, d] = lax.ppermute(polys[slot, 0], "owner", partners(owners, d))
        for d in near_steps:
            polys[slot, d] = lax.ppermute(polys[slot, 0], "owner", partners(owners, d))

    def pass_polynomials(slot):
        for d in far_steps[::2]:
            polys[slot, d] = step(line, polys[slot, d])
            polys[slot, d + 1] = lax.ppermute(polys[slot, d], "owner", partners(owners, 1))

    updates = None

    def finish_steps(slot, steps):
        nonlocal updates
        updates = finish(
            line,
            held_slots,
            slot,
            steps,
            [returned[slot, d] for d in steps],
            [polys[slot, d] for d in steps],
            gradients.shape,
            updates,
        )

    def expect(*wanted):
        line.due += [returned[slot, d][0] for slot, d in wanted if d < owners]

    far_pieces = [(slot, d) for slot in all_slots for d in far_steps]
    near_pieces = [(slot, d) for slot in all_slots for d in near_steps]
    send(far_pieces[:2] + near_pieces[:1])
    blend_piece(0, 0, far_pieces[2:] + near_pieces[1:])
    blend_piece(1, 0)
    for slot in all_slots:
        send_back(slot, 0)
    for d in near_steps:
        for slot in all_slots:
            blend_piece(slot, d)
            send_back(slot, d)
    for d in far_steps[:-1]:
        blend_piece(0, d)
    fetched[0] = fetch(line, momentum, 0, owners - 1, matrix_count, gradients.shape[1])
    expect((0, 1))
    for d in far_steps[-1:]:
        blend_piece(0, d)
    fetched[1] = fetch(line, momentum, 1, owners - 1, matrix_count, gradients.shape[1])
    expect((1, 1))
    for d in far_steps[1::2]:
        line.waiting[d] = rows[0, d]
    first_sum(0)
    for d in far_steps[1::2]:
        rows[0, d] = line.passed[d]
        send_back(0, d - 1)
    for d in far_steps:
        blend_piece(1, d)
    line.waiting["sum"] = sums[1]
    second_sum(0)
    sums[1] = line.passed["sum"]
    first_sum(1)
    for d in far_steps[1::2]:
        line.waiting[d] = rows[1, d]
    collect(0)
    for d in far_steps[1::2]:
        rows[1, d] = line.passed[d]
        send_back(1, d - 1)
    expect(*[(0, d) for d in far_steps[::2]])
    line.waiting["line"] = whole_lines[0]
    second_sum(1)
    whole_lines[0] = line.passed["line"]
    send_line(0)
    collect(1)
    send_line(1)
    make_polynomial(0)
    make_polynomial(1)
    for slot in all_slots:
        for d in far_steps[::2]:
            line.waiting[slot, d] = returned[slot, d][0]
    step(line)
    for slot in all_slots:
        for d in far_steps[::2]:
            pair = line.passed[slot, d]
            returned[slot, d] = pair, 0
            returned[slot, d + 1] = lax.ppermute(pair, "owner", partners(owners, 1)), 1
    finish_steps(0, [0] + near_steps)
    pass_polynomials(0)
    finish_steps(1, [0] + near_steps)
    finish_steps(0, far_steps)
    pass_polynomials(1)
    for d in far_steps:
        finish_steps(1, [d])
    return (updates, renewed)


def solution(mesh):
    return jax.shard_map(
        functools.partial(on_device, owners=mesh.shape["owner"], group=mesh.shape["fsdp"]),
        mesh=mesh,
        in_specs=(P(None, ("fsdp", "owner"), None), P("owner", "fsdp", None), P()),
        out_specs=(P(None, ("fsdp", "owner"), None), P("owner", "fsdp", None)),
        check_vma=False,
    )
```

```python
import functools
import math

import jax
import jax.numpy as jnp
from jax import lax
from jax.experimental import pallas as pl
from jax.experimental.pallas import tpu as pltpu
from jax.sharding import PartitionSpec as P

LONG = 16384
RANK = 512
ITERS = 5
TILE = 128

quintic = (3.4445, -4.775, 2.0315)
momentum_decay = 0.95
epsilon = 1e-07

SIDES = RANK // TILE
ABOVE = [(i, j) for i in range(SIDES) for j in range(i + 1, SIDES)]
TWOS = [(i, i + 1) for i in range(0, SIDES, 2)]
DIAGONALS = (len(ABOVE) + len(TWOS)) * TILE
POLY_ROWS = DIAGONALS + 16

f32, bf16 = jnp.float32, jnp.bfloat16


def in_hbm(x):
    return pltpu.with_memory_space_constraint(x, pltpu.HBM)


def matrix_of(place, count, slots, slot, d):
    wanted = slots * jnp.bitwise_xor(place[count], d) + slot
    found = jnp.int32(0)
    for m in range(1, count):
        found = found + jnp.where(place[m] == wanted, m, 0)
    return found


def group_index(place):
    return place[place.shape[0] - 1]


def packed_rows(group):
    return -(-(DIAGONALS + 8) // (8 * group)) * (8 * group)


def block_ids():
    return (
        lax.broadcasted_iota(jnp.int32, (TILE, TILE), 0),
        lax.broadcasted_iota(jnp.int32, (TILE, TILE), 1),
    )


def diagonal_of(block):
    row, column = block_ids()
    return jnp.sum(jnp.where(row == column, block, 0.0), axis=0, keepdims=True)


def pack(block):
    row, column = block_ids()
    blocks = [block(i, j) for i, j in ABOVE]
    blocks += [jnp.where(row <= column, block(i, i), block(j, j)) for i, j in TWOS]
    return blocks, [diagonal_of(block(j, j)) for _, j in TWOS]


def unpack(blocks, diagonals):
    row, column = block_ids()
    parts = dict(zip(ABOVE, blocks))
    for (i, j), both, diagonal in zip(TWOS, blocks[len(ABOVE) :], diagonals):
        turned = both.T
        parts[i, i] = jnp.where(row <= column, both, turned)
        parts[j, j] = jnp.where(row > column, both, jnp.where(row < column, turned, diagonal))
    return parts


def partners(size, step):
    return [(i, i ^ step) for i in range(size)]


def blend_kernel(buffers, has_sum, *refs):
    refs = list(refs)
    place = refs.pop(0)
    gradient, momentum = refs.pop(0), refs.pop(0)
    del refs[:buffers]
    before = refs.pop(0) if has_sum else None
    renewed, rows, total, held = refs
    step = pl.program_id(0)

    @pl.when(step == 0)
    def _():
        held[...] = before[...] if has_sum else jnp.zeros_like(held)

    g = gradient[...].astype(f32)
    m = momentum_decay * momentum[...] + g
    renewed[...] = m
    x = (g + momentum_decay * m).astype(bf16)
    rows[...] = x
    add_gram(held, x)

    @pl.when(step == pl.num_programs(0) - 1)
    def _():
        total[...] = held[...]


def add_gram(held, x):
    half, dims = RANK // 2, (((0,), (0,)), ((), ()))
    upper = lax.dot_general(x[:, :half], x, dims, preferred_element_type=f32)
    lower = lax.dot_general(x[:, half:], x[:, half:], dims, preferred_element_type=f32)

    def block(i, j):
        part, i0, j0 = (upper, i, j) if i < SIDES // 2 else (lower, i - SIDES // 2, j - SIDES // 2)
        return part[i0 * TILE : (i0 + 1) * TILE, j0 * TILE : (j0 + 1) * TILE]

    blocks, diagonals = pack(block)
    for n, part in enumerate(blocks):
        held[n * TILE : (n + 1) * TILE, :] += part
    for n, part in enumerate(diagonals):
        held[DIAGONALS + n : DIAGONALS + n + 1, :] += part


def blend_whole_kernel(slot, d, has_pair, place, gradient, momentum, _buffer, before, *refs):
    renewed, rows, total, loaded, new, sems = refs[1:] if has_pair else refs
    size = gradient.shape[0]
    tile = min(256, size)
    count = size // tile
    first = jnp.bitwise_xor(place.owner(), d) * size
    parts = [pl.ds(n * tile, tile) for n in range(count)]
    spans = [pl.ds(pl.multiple_of(first + n * tile, 8), tile) for n in range(count)]
    loads = [
        pltpu.make_async_copy(momentum.at[slot, spans[n]], loaded.at[parts[n]], sems.at[n])
        for n in range(count)
    ]
    stores = [
        pltpu.make_async_copy(new.at[parts[n]], renewed.at[slot, spans[n]], sems.at[count + n])
        for n in range(count)
    ]
    for load in loads:
        load.start()
    total[...] = before[...]
    for n, part in enumerate(parts):
        loads[n].wait()
        g = gradient[part].astype(f32)
        m = momentum_decay * loaded[part] + g
        new[part] = m
        stores[n].start()
        x = (g + momentum_decay * m).astype(bf16)
        if d < 2:
            rows[part] = x
        else:
            rows[d % 2, part] = x
    add_gram(total, rows[...] if d < 2 else rows[d % 2])
    for store in stores:
        store.wait()


def blend_whole(line, gradient, momentum, slot, d, buffer, pair, before):
    size = gradient.shape[0]
    count = size // min(256, size)
    aliases = {2: 0}
    operands, specs = [gradient, in_hbm(momentum), in_hbm(buffer), before], [IN_VMEM, IN_HBM, IN_HBM, IN_VMEM]
    if pair is not None:
        aliases[4] = 1
        operands.append(pair)
        specs.append(IN_VMEM)
    return line.run(
        functools.partial(blend_whole_kernel, slot, d, pair is not None),
        operands,
        specs,
        [
            pltpu.HBM(buffer.shape, f32),
            jax.ShapeDtypeStruct((size, RANK) if d < 2 else (2, size, RANK), bf16),
            jax.ShapeDtypeStruct(before.shape, f32),
        ],
        [IN_HBM, IN_VMEM, IN_VMEM],
        name="blend_whole",
        scalars=SPOTS,
        token=2,
        scratch=[
            pltpu.VMEM((size, RANK), f32),
            pltpu.VMEM((size, RANK), f32),
            pltpu.SemaphoreType.DMA((2 * count,)),
        ],
        aliases=aliases,
        vmem=8,
        work=(2 * size * RANK * RANK, size * RANK * 12),
    )


def fetch_kernel(slot, d, count, place, momentum, target, sem):
    rows = target.shape[0]
    start = pl.multiple_of(jnp.bitwise_xor(place[count], d) * rows, 8)
    copy = pltpu.make_async_copy(momentum.at[slot, pl.ds(start, rows)], target, sem)
    copy.start()
    copy.wait()


def fetch(line, momentum, slot, d, count, piece_rows):
    return line.run(
        functools.partial(fetch_kernel, slot, d, count),
        [in_hbm(momentum)],
        [IN_HBM],
        [jax.ShapeDtypeStruct((piece_rows, RANK), f32)],
        [IN_VMEM],
        name="fetch",
        scratch=[pltpu.SemaphoreType.DMA],
        work=(0, 8 * piece_rows * RANK),
    )[0]


def blend_last_kernel(slot, d, count, place, gradient, momentum, _buffer, _pair, before, renewed, pair, total, held, new, sems):
    rows = gradient.shape[0]
    tile = min(256, rows)
    first = jnp.bitwise_xor(place.owner(), d) * rows
    copies = []
    for n in range(rows // tile):
        part = pl.ds(n * tile, tile)
        g = gradient[part].astype(f32)
        m = momentum_decay * momentum[part] + g
        new[part] = m
        target = renewed.at[slot, pl.ds(pl.multiple_of(first + n * tile, 8), tile)]
        copies.append(pltpu.make_async_copy(new.at[part], target, sems.at[n]))
        copies[-1].start()
        pair[1, part] = (g + momentum_decay * m).astype(bf16)
    held[...] = before[...]
    add_gram(held, pair[1])
    near, far, size, _ = total.shape
    for e1 in range(near):
        for e2 in range(far):
            who = jnp.bitwise_xor(place.group(), e2 * near + e1)
            total[e1, e2] = held[pl.ds(pl.multiple_of(who * size, 8), size), :]
    for copy in copies:
        copy.wait()


def blend_last(line, gradient, momentum, slot, d, count, buffer, pair, before, shares):
    piece_rows = gradient.shape[0]
    total = (*shares, before.shape[0] // (shares[0] * shares[1]), TILE)
    return line.run(
        functools.partial(blend_last_kernel, slot, d, count),
        [gradient, momentum, in_hbm(buffer), pair, before],
        [IN_VMEM, IN_VMEM, IN_HBM, IN_VMEM, IN_VMEM],
        [
            pltpu.HBM(buffer.shape, f32),
            jax.ShapeDtypeStruct(pair.shape, bf16),
            jax.ShapeDtypeStruct(total, f32),
        ],
        [IN_HBM, IN_VMEM, IN_VMEM],
        name="blend_last",
        scalars=SPOTS,
        token=2,
        scratch=[
            pltpu.VMEM(before.shape, f32),
            pltpu.VMEM((piece_rows, RANK), f32),
            pltpu.SemaphoreType.DMA((piece_rows // min(256, piece_rows),)),
        ],
        aliases={2: 0, 3: 1},
        vmem=8,
        work=(2 * piece_rows * RANK * RANK, piece_rows * RANK * 12),
    )


SPOTS, RAW = "spots", "raw"


class Column:
    def __init__(self, ref):
        self.ref = ref

    def __getitem__(self, k):
        return self.ref[k, 0]


class Spots:
    def __init__(self, ref, owners):
        self.ref, self.owners = ref, owners

    def matrix(self, slot, d):
        return self.ref[slot * self.owners + d, 0]

    def owner(self):
        return self.ref[self.ref.shape[0] - 2, 0]

    def group(self):
        return self.ref[self.ref.shape[0] - 1, 0]


def make_spots(place, count, slots, owners):
    targets = slots * jnp.bitwise_xor(place[count], jnp.arange(owners))[None, :] + jnp.arange(slots)[:, None]
    found = place[None, :count] == targets.reshape(-1, 1)
    matrices = jnp.sum(jnp.where(found, jnp.arange(count)[None, :], 0), axis=1).astype(jnp.int32)
    free = -(matrices.shape[0] + 2) % 8
    column = jnp.concatenate([matrices, jnp.zeros((free,), jnp.int32), place[count:]])
    return jnp.broadcast_to(column[:, None], (column.shape[0], TILE))


class Line:
    def __init__(self, place):
        self.place, self.last, self.due, self.waiting, self.passed = place, None, [], {}, {}
        self.spots, self.raw, self.owners = None, None, 0

    def run(
        self,
        kernel,
        operands,
        specs,
        out_shape,
        out_specs,
        *,
        name,
        work,
        token=0,
        grid=(1,),
        scratch=(),
        aliases=None,
        vmem=8,
        scalars=True,
    ):
        before = [] if self.last is None or (token is None and out_shape) else [self.last]
        before += self.due
        keys = list(self.waiting)
        before += [self.waiting[key] for key in keys]
        skip, given, results = len(before), len(before) + len(operands), len(out_shape)
        lead = 1 if scalars else 0
        prefetched = scalars is True
        spots = {SPOTS: self.spots, RAW: self.raw}.get(scalars) if lead else None
        aliases = {lead + skip + i: o for i, o in (aliases or {}).items()}
        for k in range(len(keys)):
            aliases[lead + skip - len(keys) + k] = results + k

        def body(*refs):
            refs, place = refs[lead:], refs[:lead]
            if spots is not None:
                place = (Spots(place[0], self.owners) if scalars is SPOTS else Column(place[0]),)
            kernel(*place, *refs[skip : given + results], *refs[given + results + len(keys) :])

        any_spec = pl.BlockSpec(memory_space=pl.ANY)
        flops, moved = work
        in_specs = [any_spec] * skip + specs
        out_specs = out_specs + [any_spec] * len(keys)
        if prefetched:
            layout = {
                "grid_spec": pltpu.PrefetchScalarGridSpec(
                    num_scalar_prefetch=1,
                    grid=grid,
                    in_specs=in_specs,
                    out_specs=out_specs,
                    scratch_shapes=list(scratch),
                )
            }
        else:
            in_specs = [IN_VMEM] * lead + in_specs
            layout = {"in_specs": in_specs, "out_specs": out_specs, "scratch_shapes": list(scratch)}
        outs = pl.pallas_call(
            body,
            **layout,
            out_shape=out_shape
            + [jax.ShapeDtypeStruct(self.waiting[key].shape, self.waiting[key].dtype) for key in keys],
            input_output_aliases=aliases,
            compiler_params=pltpu.CompilerParams(vmem_limit_bytes=vmem * 2**20),
            cost_estimate=pl.CostEstimate(flops=20 * flops, bytes_accessed=20 * moved, transcendentals=0),
            name=name,
        )(*([self.place] if prefetched else [spots] * lead), *before, *operands)
        if token is not None:
            self.last = outs[token]
        elif not out_shape:
            self.last = outs[0]
        self.due, self.waiting = [], {}
        self.passed.update(zip(keys, outs[results:]))
        return outs[:results]


IN_VMEM = pl.BlockSpec(memory_space=pltpu.VMEM)
IN_HBM = pl.BlockSpec(memory_space=pltpu.HBM)


def pick_kernel(slots, count, wanted, place, gradients, *refs):
    targets, sems = refs[:-1], refs[-1]
    copies = []
    for n, (slot, d) in enumerate(wanted):
        source = gradients.at[matrix_of(place, count, slots, slot, d)]
        copies.append(pltpu.make_async_copy(source, targets[n], sems.at[n]))
        copies[-1].start()
    for copy in copies:
        copy.wait()


def pick(line, gradients, slots, wanted):
    count, rows, _ = gradients.shape
    return line.run(
        functools.partial(pick_kernel, slots, count, wanted),
        [in_hbm(gradients)],
        [IN_HBM],
        [jax.ShapeDtypeStruct((rows, RANK), bf16) for _ in wanted],
        [IN_VMEM for _ in wanted],
        name="pick",
        scalars=RAW,
        scratch=[pltpu.SemaphoreType.DMA((len(wanted),))],
        work=(0, 4 * len(wanted) * rows * RANK),
    )


def blend(line, gradient, momentum, slot, d, count, buffer, pair, before, summed):
    slots = momentum.shape[0]
    piece_rows = gradient.shape[-2]
    tile = min(256, piece_rows)
    steps = piece_rows // tile
    if d == 0:
        gradient_spec = pl.BlockSpec(
            (None, tile, RANK), lambda i, p: (matrix_of(p, count, slots, slot, 0), i, 0)
        )
        gradient = in_hbm(gradient)
    else:
        gradient_spec = pl.BlockSpec((tile, RANK), lambda i, p: (i, 0))
    momentum_spec = pl.BlockSpec(
        (None, tile, RANK), lambda i, p: (slot, jnp.bitwise_xor(p[count], d) * steps + i, 0)
    )
    in_specs, operands = [gradient_spec, momentum_spec], [gradient, in_hbm(momentum)]
    aliases = {}
    for result, array in enumerate((buffer, pair)):
        if array is not None:
            aliases[len(operands)] = result
            in_specs.append(IN_HBM if result == 0 else pl.BlockSpec(memory_space=pl.ANY))
            operands.append(in_hbm(array) if result == 0 else array)
    if d < 2:
        rows_shape, rows_spec = (piece_rows, RANK), pl.BlockSpec((tile, RANK), lambda i, p: (i, 0))
    else:
        rows_shape = (2, piece_rows, RANK)
        rows_spec = pl.BlockSpec((None, tile, RANK), lambda i, p: (d % 2, i, 0))
    total = (summed, TILE)
    if before is not None:
        in_specs.append(pl.BlockSpec(total, lambda i, p: (0, 0)))
        operands.append(before)
    return line.run(
        functools.partial(blend_kernel, len(aliases), before is not None),
        operands,
        in_specs,
        [
            pltpu.HBM(momentum.shape, f32),
            jax.ShapeDtypeStruct(rows_shape, bf16),
            jax.ShapeDtypeStruct(total, f32),
        ],
        [
            momentum_spec,
            rows_spec,
            pl.BlockSpec(total, lambda i, p: (0, 0)),
        ],
        name="blend",
        token=2,
        grid=(steps,),
        scratch=[pltpu.VMEM(total, f32)],
        aliases=aliases,
        vmem=8,
        work=(2 * piece_rows * RANK * RANK, piece_rows * RANK * 12),
    )


def add_near_kernel(share, *refs):
    far = share.shape[1]
    received, targets = refs[: len(refs) - far], refs[len(refs) - far :]
    for e2, target in enumerate(targets):
        total = share[0, e2]
        for other in received:
            total = total + other[e2]
        target[...] = total


def add_near(line, share, received):
    _, far, count, _ = share.shape
    return line.run(
        add_near_kernel,
        [share, *received],
        [IN_VMEM] * (1 + len(received)),
        [jax.ShapeDtypeStruct((count, TILE), f32)] * far,
        [IN_VMEM] * far,
        name="add_near",
        scalars=False,
        work=(0, 12 * far * count * TILE),
    )


def add_far_kernel(*refs):
    total = refs[0][...]
    for other in refs[1:-1]:
        total = total + other[...]
    refs[-1][...] = total


def add_far(line, parts):
    return line.run(
        add_far_kernel,
        list(parts),
        [IN_VMEM] * len(parts),
        [jax.ShapeDtypeStruct(parts[0].shape, f32)],
        [IN_VMEM],
        name="add_far",
        scalars=False,
        work=(0, 4 * (len(parts) + 1) * parts[0].size),
    )[0]


def step(line, array=None):
    if array is not None:
        line.waiting["step"] = array
    line.run(lambda: None, [], [], [], [], name="step", token=None, scalars=False, work=(0, 0))
    return line.passed.get("step")


def stack_kernel(*refs):
    for e, part in enumerate(refs[:-1]):
        refs[-1][e] = part[...]


def stack(line, parts):
    return line.run(
        stack_kernel,
        list(parts),
        [IN_VMEM] * len(parts),
        [jax.ShapeDtypeStruct((len(parts), *parts[0].shape), f32)],
        [IN_VMEM],
        name="stack",
        scalars=False,
        work=(0, 8 * len(parts) * parts[0].size),
    )[0]


SHIFTS = (0.0, 0.0, 0.1, 0.6, 0.85)
FINE_TURN, FINE_POLY = 2, 3
HALF = RANK // 2


def dot(a, b):
    return jnp.dot(a, b, preferred_element_type=f32)


def whole(x):
    top, corner = x
    return jnp.concatenate([top, jnp.concatenate([top[:, HALF:].T, corner], axis=1)], axis=0)


def operand(x, passes):
    high = tuple(part.astype(bf16) for part in x)
    if passes == 1:
        return (whole(high),)
    low = tuple((part - rounded.astype(f32)).astype(bf16) for part, rounded in zip(x, high))
    return (whole(high), whole(low))


def product(a, b):
    top, corner = dot(a[0][:HALF], b[0]), dot(a[0][HALF:], b[0][:, HALF:])
    if len(a) > 1:
        top += dot(a[0][:HALF], b[1]) + dot(a[1][:HALF], b[0])
        corner += dot(a[0][HALF:], b[1][:, HALF:]) + dot(a[1][HALF:], b[0][:, HALF:])
    return (top, corner)


def combine(*terms):
    return tuple(
        functools.reduce(lambda x, y: x + y, [w * x[part] for w, x in terms]) for part in range(2)
    )


def add_identity(x, value):
    top, corner = x
    row = lax.broadcasted_iota(jnp.int32, (HALF, HALF), 0)
    column = lax.broadcasted_iota(jnp.int32, (HALF, HALF), 1)
    eye = jnp.where(row == column, value, 0.0)
    return (jnp.concatenate([top[:, :HALF] + eye, top[:, HALF:]], axis=1), corner + eye)


def polynomial_kernel(near, far, count, place, *refs):
    *shared, result, packed = refs
    for e1, other in enumerate(shared):
        for e2 in range(far):
            who = jnp.bitwise_xor(place.group(), e2 * near + e1)
            packed[pl.ds(pl.multiple_of(who * count, 8), count), :] = other[e2]
    blocks = [packed[n * TILE : (n + 1) * TILE, :] for n in range(len(ABOVE) + len(TWOS))]
    diagonals = [packed[DIAGONALS + n : DIAGONALS + n + 1, :] for n in range(len(TWOS))]
    parts = unpack(blocks, diagonals)
    trace = jnp.sum(sum(diagonals) + sum(diagonal_of(both) for both in blocks[len(ABOVE) :]))
    for i, j in ((0, 1), (2, 3)):
        parts[j, i] = parts[i, j].T

    def rows_of(count, first):
        return jnp.concatenate(
            [
                jnp.concatenate([parts[i, j] for j in range(first, SIDES)], axis=1)
                for i in range(first, first + count)
            ],
            axis=0,
        )

    half = HALF // TILE
    scale = 1.0 / (jnp.sqrt(jnp.full((1, 1), trace, f32)) + epsilon)
    rest = tuple((x * scale) * scale for x in (rows_of(half, 0), rows_of(half, half)))
    a, b, c = quintic
    poly = None
    for k in range(ITERS):
        shift = SHIFTS[k]
        gain = a + b * shift + c * shift * shift
        d = operand(rest, 3 if k == FINE_TURN else 1)
        step = combine((b + 2 * c * shift, rest), (c, product(d[:1], d[:1])))
        s = operand(step, 3 if k in (FINE_TURN, FINE_POLY) else 1)
        if poly is None:
            poly = add_identity(step, gain)
        else:
            p = operand(poly, 3 if k == FINE_POLY else 1)
            poly = combine((gain, poly), (1.0, product(p, s)))
        if k < ITERS - 1:
            middle = combine((gain, rest), (shift, step), (1.0, product(d, s)))
            turned = product(operand(middle, 1), s)
            rest = combine((gain, middle), (gain * shift, step), (1.0, turned))
            rest = add_identity(rest, gain * gain * shift - SHIFTS[k + 1])
    top, corner = tuple(x * (scale * math.sqrt(max(LONG, RANK))) for x in poly)

    def block(i, j):
        part, i0, j0 = (top, i, j) if i < half else (corner, i - half, j - half)
        return part[i0 * TILE : (i0 + 1) * TILE, j0 * TILE : (j0 + 1) * TILE]

    blocks, seconds = pack(block)
    for n, part in enumerate(blocks):
        result[n * TILE : (n + 1) * TILE, :] = part.astype(bf16)
    lows = []
    for i in range(SIDES):
        diagonal = diagonal_of(block(i, i))
        lows.append(diagonal - diagonal.astype(bf16).astype(f32))
    rows = lows + seconds
    rows.append(jnp.zeros((POLY_ROWS - DIAGONALS - len(rows), TILE), f32))
    result[DIAGONALS:, :] = jnp.concatenate(rows, axis=0).astype(bf16)


def polynomial(line, shared):
    near, (far, count, _) = len(shared), shared[0].shape
    return line.run(
        functools.partial(polynomial_kernel, near, far, count),
        list(shared),
        [IN_VMEM] * near,
        [jax.ShapeDtypeStruct((POLY_ROWS, TILE), bf16)],
        [IN_VMEM],
        name="polynomial",
        scalars=SPOTS,
        scratch=[pltpu.VMEM((near * far * count, TILE), f32)],
        vmem=12,
        work=(RANK**3, 2**16),
    )[0]


def finish_kernel(slots, slot, steps, matrices, picks, last, place, *refs):
    refs = list(refs)
    count = len(steps)
    pieces, polys = refs[:count], refs[count : 2 * count]
    updates, held, sems = refs[len(refs) - (3 if last else 4)], *refs[-2:]
    copies = []
    for n, d in enumerate(steps):
        tail = polys[n][DIAGONALS:, :].astype(f32)
        blocks = [polys[n][k * TILE : (k + 1) * TILE, :] for k in range(len(ABOVE) + len(TWOS))]
        twos = [part.astype(f32) for part in blocks[len(ABOVE) :]]
        seconds = [tail[SIDES + k : SIDES + k + 1] for k in range(len(TWOS))]
        parts = unpack(blocks[: len(ABOVE)] + twos, seconds)
        for i in range(SIDES):
            parts[i, i] = parts[i, i].astype(bf16)
        for i, j in ABOVE:
            parts[j, i] = parts[i, j].T
        sides = range(SIDES)
        poly = jnp.concatenate(
            [jnp.concatenate([parts[i, j] for j in sides], axis=1) for i in sides], axis=0
        )
        low = jnp.concatenate([tail[i : i + 1] for i in sides], axis=1)
        rows = held.shape[1]
        tile = min(256, rows)
        target = updates.at[place.matrix(slot, d)]
        for k in range(rows // tile):
            part = pl.ds(k * tile, tile)
            x = pieces[n][part] if picks[n] is None else pieces[n][picks[n], part]
            held[n, part] = (dot(x, poly) + x.astype(f32) * low).astype(bf16)
            copies.append(pltpu.make_async_copy(held.at[n, part], target.at[part], sems.at[len(copies)]))
            copies[-1].start()
    for copy in copies:
        copy.wait()


def finish(line, slots, slot, steps, pieces, polys, shape, buffer, last):
    operands = [piece for piece, _ in pieces] + list(polys)
    specs = [IN_VMEM] * len(operands)
    aliases = {}
    if buffer is not None:
        aliases = {len(operands): 0}
        operands.append(in_hbm(buffer))
        specs.append(IN_HBM)
    return line.run(
        functools.partial(finish_kernel, slots, slot, steps, shape[0], [index for _, index in pieces], last),
        operands,
        specs,
        [pltpu.HBM(shape, bf16)] + [jax.ShapeDtypeStruct((8, TILE), f32)] * (not last),
        [IN_HBM] + [IN_VMEM] * (not last),
        name="finish",
        scalars=SPOTS,
        token=0 if last else 1,
        scratch=[pltpu.VMEM((len(steps), shape[1], RANK), bf16), pltpu.SemaphoreType.DMA((len(steps) * max(1, shape[1] // 256),))],
        aliases=aliases,
        vmem=8,
        work=(2 * len(steps) * shape[1] * RANK * RANK, 4 * len(steps) * shape[1] * RANK),
    )[0]


def on_device(gradients, momentum, slot_table, *, owners, group):
    matrix_count = gradients.shape[0]
    held_slots = momentum.shape[0]
    near = 1 << ((group.bit_length() - 1) // 2)
    shares = (near, group // near)
    place = jnp.concatenate(
        [
            slot_table.astype(jnp.int32),
            jnp.stack([lax.axis_index("owner"), lax.axis_index("fsdp")]).astype(jnp.int32),
        ]
    )

    line = Line(place)
    line.owners = owners
    line.raw = jnp.broadcast_to(jnp.pad(place, (0, -place.shape[0] % 8))[:, None], (-(-place.shape[0] // 8) * 8, TILE))
    line.spots = make_spots(place, matrix_count, held_slots, owners)
    all_slots = range(held_slots)
    far_steps, near_steps = list(range(2, owners)), list(range(1, min(2, owners)))
    arrived = {}
    wanted = [(0, d) for d in far_steps] + [(slot, d) for slot in all_slots for d in near_steps]
    wanted += [(slot, d) for slot in range(1, held_slots) for d in far_steps]
    picked = {}
    for few in (wanted[:1], wanted[1:]):
        picked.update(zip(few, pick(line, gradients, held_slots, few)))

    def send(pieces):
        for slot, d in pieces:
            arrived[slot, d] = lax.ppermute(picked[slot, d], "owner", partners(owners, d))

    fetched = {}
    renewed, rows, returned, sums, lines, mine, whole_lines, gathered, polys = None, {}, {}, {}, {}, {}, {}, {}, {}

    summed = packed_rows(group)

    def blend_piece(slot, d, then=()):
        nonlocal renewed
        line.waiting.update({piece: picked[piece] for piece in then})
        gradient = arrived[slot, d] if d else gradients
        if d == owners - 1:
            renewed, rows[slot, d], sums[slot] = blend_last(
                line, gradient, fetched[slot], slot, d, matrix_count, renewed, rows[slot, d - 1], sums[slot], shares
            )
        elif d:
            renewed, rows[slot, d], sums[slot] = blend_whole(
                line,
                gradient,
                momentum,
                slot,
                d,
                renewed,
                rows[slot, d - 1] if d > 1 and d % 2 else None,
                sums[slot],
            )
        else:
            renewed, rows[slot, d], sums[slot] = blend(
                line,
                gradient,
                momentum,
                slot,
                d,
                matrix_count,
                renewed,
                rows[slot, d - 1] if d > 1 and d % 2 else None,
                sums.get(slot),
                summed,
            )
        picked.update({piece: line.passed[piece] for piece in then})
        send(then)

    def send_back(slot, d):
        if d == 0:
            returned[slot, 0] = rows[slot, 0], None
        elif d == 1:
            returned[slot, 1] = lax.ppermute(rows[slot, 1], "owner", partners(owners, 1)), None
        else:
            pair = lax.ppermute(rows[slot, d + 1], "owner", partners(owners, d))
            returned[slot, d] = pair, 0

    def across_near(x, e1):
        return lax.ppermute(x, "fsdp", partners(group, e1))

    def across_far(x, e2):
        return lax.ppermute(x, "fsdp", partners(group, e2 * near))

    def first_sum(slot):
        received = [across_near(sums[slot][e1], e1) for e1 in range(1, near)]
        lines[slot] = add_near(line, sums[slot], received)

    def second_sum(slot):
        parts = lines[slot]
        received = [across_far(parts[e2], e2) for e2 in range(1, shares[1])]
        mine[slot] = add_far(line, [parts[0], *received])

    def collect(slot):
        part = mine[slot]
        whole_lines[slot] = stack(line, [part] + [across_far(part, e2) for e2 in range(1, shares[1])])

    def send_line(slot):
        whole_line = whole_lines[slot]
        gathered[slot] = [whole_line] + [across_near(whole_line, e1) for e1 in range(1, near)]

    def make_polynomial(slot):
        polys[slot, 0] = polynomial(line, gathered[slot])
        for d in far_steps[::2]:
            polys[slot, d] = lax.ppermute(polys[slot, 0], "owner", partners(owners, d))
        for d in near_steps:
            polys[slot, d] = lax.ppermute(polys[slot, 0], "owner", partners(owners, d))

    def pass_polynomials(slot):
        for d in far_steps[::2]:
            polys[slot, d] = step(line, polys[slot, d])
            polys[slot, d + 1] = lax.ppermute(polys[slot, d], "owner", partners(owners, 1))

    updates = None

    def finish_steps(slot, steps):
        nonlocal updates
        updates = finish(
            line,
            held_slots,
            slot,
            steps,
            [returned[slot, d] for d in steps],
            [polys[slot, d] for d in steps],
            gradients.shape,
            updates,
            slot == held_slots - 1 and steps[-1] == owners - 1,
        )

    def expect(*wanted):
        line.due += [returned[slot, d][0] for slot, d in wanted if d < owners]

    far_pieces = [(slot, d) for slot in all_slots for d in far_steps]
    near_pieces = [(slot, d) for slot in all_slots for d in near_steps]
    send(far_pieces[:2] + near_pieces[:1])
    blend_piece(0, 0, far_pieces[2:] + near_pieces[1:])
    blend_piece(1, 0)
    for slot in all_slots:
        send_back(slot, 0)
    for d in near_steps:
        for slot in all_slots:
            blend_piece(slot, d)
            send_back(slot, d)
    for d in far_steps[:-1]:
        blend_piece(0, d)
    fetched[0] = fetch(line, momentum, 0, owners - 1, matrix_count, gradients.shape[1])
    expect((0, 1))
    for d in far_steps[-1:]:
        blend_piece(0, d)
    fetched[1] = fetch(line, momentum, 1, owners - 1, matrix_count, gradients.shape[1])
    expect((1, 1))
    for d in far_steps[1::2]:
        line.waiting[d] = rows[0, d]
    first_sum(0)
    for d in far_steps[1::2]:
        rows[0, d] = line.passed[d]
        send_back(0, d - 1)
    for d in far_steps:
        blend_piece(1, d)
    line.waiting["sum"] = sums[1]
    second_sum(0)
    sums[1] = line.passed["sum"]
    first_sum(1)
    for d in far_steps[1::2]:
        line.waiting[d] = rows[1, d]
    collect(0)
    for d in far_steps[1::2]:
        rows[1, d] = line.passed[d]
        send_back(1, d - 1)
    expect(*[(0, d) for d in far_steps[::2]])
    line.waiting["line"] = whole_lines[0]
    second_sum(1)
    whole_lines[0] = line.passed["line"]
    send_line(0)
    collect(1)
    send_line(1)
    make_polynomial(0)
    make_polynomial(1)
    for slot in all_slots:
        for d in far_steps[::2]:
            line.waiting[slot, d] = returned[slot, d][0]
    step(line)
    for slot in all_slots:
        for d in far_steps[::2]:
            pair = line.passed[slot, d]
            returned[slot, d] = pair, 0
            returned[slot, d + 1] = lax.ppermute(pair, "owner", partners(owners, 1)), 1
    finish_steps(0, [0] + near_steps)
    pass_polynomials(0)
    finish_steps(1, [0] + near_steps)
    finish_steps(0, far_steps)
    pass_polynomials(1)
    for d in far_steps:
        finish_steps(1, [d])
    return (updates, renewed)


def solution(mesh):
    return jax.shard_map(
        functools.partial(on_device, owners=mesh.shape["owner"], group=mesh.shape["fsdp"]),
        mesh=mesh,
        in_specs=(P(None, ("fsdp", "owner"), None), P("owner", "fsdp", None), P()),
        out_specs=(P(None, ("fsdp", "owner"), None), P("owner", "fsdp", None)),
        check_vma=False,
    )
```
